128 devices in a mesh: grp: 4 (over z), dev: 32 (over x, y, core).
Axes of the slice: x: 4, y: 4, z: 4, core: 2. Of those that a mesh axis runs over, the one named last changes fastest.
Arguments:
- tokens: bfloat16 [512, 7168], P(('grp', 'dev')), may hold values from -6 to 6
- expert_ids: int32 [512, 8], P(('grp', 'dev')), may hold values from 0 to 31, all different within a row; in each aligned block of 4 rows (0 to 3, 4 to 7, ...) at most 2 rows name the same one
- route_weights: float32 [512, 8], P(('grp', 'dev')), may hold values from 0.1 to 0.6
- gate_weight: bfloat16 [32, 7168, 2048], P('dev', None, 'grp'), may hold values from -0.0625 to 0.0625
- up_weight: bfloat16 [32, 7168, 2048], P('dev', None, 'grp'), may hold values from -0.0625 to 0.0625
- down_weight: bfloat16 [32, 2048, 7168], P('dev', 'grp'), may hold values from -0.125 to 0.125
Outputs:
- mixed: bfloat16 [512, 7168], P(('grp', 'dev'))
The draws below stay inside these ranges and needn't reach their ends.
Inputs may be any that keep to these rules, and one draw needn't show every extreme that they name: `expert_ids`: each row names 8 different experts. Among the 4 tokens of one device no expert is named more than 2 times, a bound that some block reaches.
All inputs are finite; a program needn't handle non-finite values.
Results may differ from the reference program's by a relative error of at most 0.012.
Values may be sent and summed in bfloat16 or wider, within the bound.
No kernel may reach another device: no remote copies, remote signals or barrier semaphores. Data moves between devices by JAX's collectives and lax.ppermute only.
A program may use at most 128 MiB of HBM per device.

```python
import math
import jax
import jax.numpy as jnp
import numpy as np
from jax import lax

D = 7168
FF = 2048
TOK_DEV = 4
EXPERTS = 32
TOP = 8
CAP = 2
TOKENS = 512
N_GRP = 4
N_DEV = 32


def steps_of(key, extent, split, smallest, largest):
    def one(dim, parts):
        draws = jax.random.uniform(jax.random.fold_in(jax.random.fold_in(key, 6), dim), (parts,), jnp.float32, smallest / len(split), largest / len(split))
        return jnp.repeat(jnp.exp(draws), extent[dim] // parts).reshape((-1,) + (1,) * (len(extent) - dim - 1))

    factor_of = one(*split[0])
    for cut in split[1:]:
        factor_of = factor_of * one(*cut)
    return factor_of


def assign_block(rng, own, number, rows, number_of, top, most, lean):
    sequence = jax.random.permutation(rng, number_of)
    crowded, common = shares(number_of, rows * top, most, lean, True), shares(number_of, rows * top, most, lean, False)
    places = jnp.arange(number_of)

    def named(sizes, turn):
        used = int((sizes > 0).sum())
        fixed = max(1, used // 4)
        moved = fixed + (places - fixed + turn * (used - fixed)) % max(1, number_of - fixed)
        return jnp.zeros((number_of,), jnp.int32).at[sequence[jnp.where(places < fixed, places, moved)]].set(jnp.asarray(sizes, jnp.int32))

    sizes = jnp.where(number % 4 == 0, named(crowded, number // 4), named(common, number - number // 4 - 1))
    mixed = jax.random.permutation(jax.random.fold_in(own, 3), number_of)
    source_of, taker = mixed[0:number_of // 2 * 2:2], mixed[1:number_of // 2 * 2:2]
    slack = jnp.minimum(sizes[source_of] - 1, most - sizes[taker]) // 2
    slack = jnp.where((source_of == sequence[0]) | (taker == sequence[0]) | (sizes[taker] == 0), 0, jnp.maximum(slack, 0))
    moved = jax.random.randint(jax.random.fold_in(own, 4), (number_of // 2,), 0, 1 << 20) % (slack + 1)
    sizes = sizes.at[source_of].add(-moved).at[taker].add(moved)
    labels = jnp.searchsorted(jnp.cumsum(sizes), jnp.arange(rows * top), side="right").astype(jnp.int32)
    grid = labels.reshape(top, rows).T
    grid = grid[jax.random.permutation(jax.random.fold_in(own, 1), rows)]
    turn = jax.random.randint(jax.random.fold_in(own, 2), (rows, 1), 0, top)
    return jnp.take_along_axis(grid, (jnp.arange(top)[None, :] + turn) % top, axis=1)


def shares(number_of, total, bound, skew, full):
    weights = [(1 << 20) // math.isqrt(grade ** skew) + 1 for grade in range(1, number_of + 1)]
    largest = bound if full else min(bound, max(-(-total // number_of), total * weights[0] // sum(weights)))
    least = 1 if total - largest >= number_of - 1 else 0
    counts, surplus = [largest] + [least] * (number_of - 1), total - largest - least * (number_of - 1)
    while surplus > 0:
        movable = [i for i in range(1, number_of) if counts[i] < largest] or [i for i in range(1, number_of) if counts[i] < bound]
        mass, left = sum([weights[i] for i in movable]), surplus
        for i in movable:
            more = min(bound - counts[i], max(1, left * weights[i] // mass), surplus)
            counts[i] = counts[i] + more
            surplus = surplus - more
    return np.array(counts)


def gaussian(own_key, shape, spread, limit, split=(), kind=jnp.bfloat16):
    array = spread * jax.random.normal(own_key, shape, jnp.float32)
    if split:
        array = array * steps_of(own_key, shape, split, -0.22, 0.18)
    return jnp.clip(array, -limit, limit).astype(kind)


def setup_inputs(seed: int = 0) -> dict:
    keys = jax.random.split(jax.random.key(seed), 7)
    tokens = gaussian(keys[0], (TOKENS, D), 1.0, 6.0, ((0, 128),))
    expert_ids_keys = jax.random.split(jax.random.fold_in(keys[1], 1), TOKENS // TOK_DEV)
    expert_ids_turns = jax.random.permutation(jax.random.fold_in(keys[1], 3), TOKENS // TOK_DEV)
    expert_ids = jax.vmap(lambda own, number: assign_block(jax.random.fold_in(keys[1], 2), own, number, TOK_DEV, EXPERTS, TOP, CAP, 2))(expert_ids_keys, expert_ids_turns).reshape((TOKENS, TOP))
    route_weights = jnp.clip(0.1 + 0.5 * jax.random.uniform(keys[2], (TOKENS, TOP), jnp.float32) ** steps_of(keys[2], (TOKENS, TOP), ((0, 128),), -0.2, 0.2), 0.1, 0.6)
    gate_weight = gaussian(keys[3], (EXPERTS, D, FF), D ** -0.5, 0.0625, ((0, 32), (2, 4)))
    up_weight = gaussian(keys[4], (EXPERTS, D, FF), D ** -0.5, 0.0625, ((0, 32), (2, 4)))
    down_weight = gaussian(keys[5], (EXPERTS, FF, D), FF ** -0.5, 0.125, ((0, 32), (1, 4)))
    return dict(tokens=tokens, expert_ids=expert_ids, route_weights=route_weights, gate_weight=gate_weight, up_weight=up_weight, down_weight=down_weight)


def reference(tokens, expert_ids, route_weights, gate_weight, up_weight, down_weight):
    sources = N_GRP * N_DEV
    quarter_width = FF // N_GRP
    flat_ids = expert_ids.reshape(-1).astype(jnp.int32)
    onehot = (flat_ids[:, None] == jnp.arange(EXPERTS, dtype=jnp.int32)[None, :]).astype(jnp.int32)
    per_source = onehot.reshape(sources, TOK_DEV * TOP, EXPERTS)
    before = jnp.cumsum(per_source, axis=1) - per_source
    slot_index = jnp.sum(before * per_source, axis=2).reshape(-1)
    source = jnp.arange(TOKENS * TOP, dtype=jnp.int32) // (TOK_DEV * TOP)
    target = flat_ids * (sources * CAP) + source * CAP + slot_index
    repeated = jnp.repeat(tokens, TOP, axis=0)
    buffer = jnp.zeros((EXPERTS * sources * CAP, D), jnp.bfloat16).at[target].set(repeated)
    buffer = buffer.reshape(EXPERTS, sources * CAP, D)

    def per_expert(inputs):
        block, w_first, w_second, w_third = inputs
        summed = jnp.zeros((sources * CAP, D), jnp.float32)
        for quarter in range(N_GRP):
            low = quarter * quarter_width
            high = low + quarter_width
            gate_out = jnp.dot(block, w_first[:, low:high], preferred_element_type=jnp.float32)
            up_out = jnp.dot(block, w_second[:, low:high], preferred_element_type=jnp.float32)
            hidden = (jax.nn.silu(gate_out) * up_out).astype(jnp.bfloat16)
            partial_value = jnp.dot(hidden, w_third[low:high, :], preferred_element_type=jnp.float32).astype(jnp.bfloat16)
            partial_value = lax.optimization_barrier(partial_value)
            summed = summed + partial_value.astype(jnp.float32)
        return summed

    expert_out = lax.map(per_expert, (buffer, gate_weight, up_weight, down_weight))
    picked = expert_out.reshape(-1, D)[target].reshape(TOKENS, TOP, D)
    mixed = jnp.sum(picked * route_weights[:, :, None].astype(jnp.float32), axis=1)
    return mixed.astype(jnp.bfloat16)
```

```python
import functools

import jax
import jax.numpy as jnp
from jax import lax
from jax.experimental import pallas as pl
from jax.experimental.pallas import tpu as pltpu
from jax.sharding import PartitionSpec as P

AXES = ("grp", "dev")
D = 7168
HALF = D // 2
EXT = 128
WIDE = HALF + EXT
ROWS = 512
SEL = 128
F32 = jnp.float32
BF16 = jnp.bfloat16
MIB = 1 << 20


def flat(z, x, y, c):
    return ((z * 4 + x) * 4 + y) * 2 + c


def cube_groups(stage):
    seen, groups = set(), []
    for z in range(4):
        for x in range(4):
            for y in range(4):
                for c in range(2):
                    if flat(z, x, y, c) in seen:
                        continue
                    m = 1 if c == stage else 3
                    members = [
                        flat(z ^ (m * i), x ^ (m * j), y ^ (m * k), c)
                        for i in (0, 1) for j in (0, 1) for k in (0, 1)
                    ]
                    seen.update(members)
                    groups.append(members)
    return groups


NEAR, FAR = cube_groups(0), cube_groups(1)


def swap_groups(values, groups):
    return lax.all_to_all(values, AXES, 0, 0, axis_index_groups=groups, tiled=True)


def to_sibling(values):
    return lax.ppermute(values, "dev", [(i, i ^ 1) for i in range(32)])


def pack_kernel(tokens_ref, ids_ref, weights_ref, out_ref):
    lane = lax.broadcasted_iota(jnp.int32, (4, EXT), 1)
    dense = jnp.zeros((4, EXT), F32)
    for k in range(8):
        dense += jnp.where(ids_ref[:, k : k + 1] == lane % 32, weights_ref[:, k : k + 1], 0.0)
    high = dense.astype(BF16).astype(F32)
    route = jnp.where(lane < 32, high, jnp.where(lane < 64, dense - high, 0.0))
    rows = tokens_ref[...].astype(F32)
    left = jnp.concatenate([rows[:, :HALF], route], axis=1)
    right = jnp.concatenate([rows[:, HALF:], route], axis=1)
    block = jnp.concatenate([left, right], axis=0).astype(BF16)
    for i in range(8):
        out_ref[i] = block


def pack(tokens, ids, weights):
    return pl.pallas_call(
        pack_kernel,
        out_shape=jax.ShapeDtypeStruct((8, 8, WIDE), BF16),
        name="pack",
    )(tokens, ids, weights)


def expert_lanes(expert, shape, dim):
    lane = lax.broadcasted_iota(jnp.int32, shape, dim)
    return (lane < 64) & (lane % 32 == expert)


def select_kernel(expert_ref, x_ref, out_ref, pick):
    own = expert_ref[0]
    turn = lax.broadcasted_iota(jnp.int32, (8, EXT), 0)
    experts = jnp.where(turn == 0, own, own ^ 1)
    wanted = jnp.where(expert_lanes(experts, (8, EXT), 1) & (turn < 2), 1.0, 0.0).astype(BF16)
    route = lax.dot_general(
        wanted, x_ref[:, HALF:], (((1,), (1,)), ((), ())), preferred_element_type=F32
    )
    chosen = route > 0
    first = lax.broadcasted_iota(jnp.int32, (ROWS, ROWS), 0)
    second = lax.broadcasted_iota(jnp.int32, (ROWS, ROWS), 1)
    earlier = jnp.where((first // 4 == second // 4) & (first < second), 1.0, 0.0).astype(BF16)
    rank = jnp.dot(jnp.where(chosen, 1.0, 0.0).astype(BF16), earlier, preferred_element_type=F32)
    column = lax.broadcasted_iota(jnp.int32, (8, ROWS), 1)
    place = jnp.where(chosen, column // 8 * 2 + rank.astype(jnp.int32), -1)
    row = lax.broadcasted_iota(jnp.int32, (SEL, ROWS), 0)
    is_left = lax.broadcasted_iota(jnp.int32, (SEL, ROWS), 1) % 8 < 4
    for e in range(2):
        hit = place[e : e + 1, :] == row
        pick[0, e * SEL : (e + 1) * SEL, :] = jnp.where(hit & is_left, 1.0, 0.0).astype(BF16)
        pick[1, e * SEL : (e + 1) * SEL, :] = jnp.where(hit & ~is_left, 1.0, 0.0).astype(BF16)

    def put(start, size, side, to):
        value = jnp.dot(pick[side], x_ref[:, start : start + size], preferred_element_type=F32).astype(BF16)
        out_ref[0, :, to : to + size] = value[:SEL]
        out_ref[1, :, to : to + size] = value[SEL:]

    for n in range(0, HALF, 512):
        put(n, 512, 0, n)
        put(n, 512, 1, HALF + n)
    put(HALF, EXT, 0, D)


def select(expert, x):
    return pl.pallas_call(
        select_kernel,
        out_shape=jax.ShapeDtypeStruct((2, SEL, D + EXT), BF16),
        in_specs=[pl.BlockSpec(memory_space=pltpu.SMEM), pl.BlockSpec(memory_space=pltpu.VMEM)],
        scratch_shapes=[pltpu.VMEM((2, 2 * SEL, ROWS), BF16)],
        compiler_params=pltpu.CompilerParams(vmem_limit_bytes=40 * MIB),
        name="select",
    )(expert, x)


STEPS = 7
BLOCK = D // STEPS


def ffn_kernel(expert_ref, mine_ref, theirs_ref, gate_ref, up_ref, down_ref, out_ref, gate_sum, up_sum, hidden):
    i = pl.program_id(0)

    @pl.when(i == 0)
    def _():
        gate_sum[...] = jnp.zeros_like(gate_sum)
        up_sum[...] = jnp.zeros_like(up_sum)

    @pl.when(i < STEPS)
    def _():
        columns = pl.ds(pl.multiple_of(i * BLOCK, BLOCK), BLOCK)
        for part, ref in enumerate((mine_ref, theirs_ref)):
            rows = slice(part * SEL, (part + 1) * SEL)
            x = ref[:, columns]
            gate_sum[rows, :] += jnp.dot(x, gate_ref[0], preferred_element_type=F32)
            up_sum[rows, :] += jnp.dot(x, up_ref[0], preferred_element_type=F32)

    @pl.when(i == STEPS - 1)
    def _():
        lanes = expert_lanes(expert_ref[0], (SEL, EXT), 1)
        for part, ref in enumerate((mine_ref, theirs_ref)):
            rows = slice(part * SEL, (part + 1) * SEL)
            route = ref[:, D:].astype(F32)
            scale = jnp.sum(jnp.where(lanes, route, 0.0), axis=1, keepdims=True)
            v = gate_sum[rows, :]
            hidden[rows, :] = (v / (1.0 + jnp.exp(-v)) * up_sum[rows, :] * scale).astype(BF16)

    @pl.when(i >= STEPS)
    def _():
        y = jnp.dot(hidden[...], down_ref[0], preferred_element_type=F32).astype(BF16)
        out_ref[0] = y[:SEL]
        out_ref[1] = y[SEL:]


def ffn(expert, mine, theirs, gate, up, down):
    first = lambda i: jnp.minimum(i, STEPS - 1)
    second = lambda i: jnp.maximum(i - STEPS, 0)
    whole = pl.BlockSpec((SEL, D + EXT), lambda i: (0, 0))
    return pl.pallas_call(
        ffn_kernel,
        grid=(2 * STEPS,),
        out_shape=jax.ShapeDtypeStruct((2, SEL, D), BF16),
        in_specs=[
            pl.BlockSpec(memory_space=pltpu.SMEM),
            whole,
            whole,
            pl.BlockSpec((1, BLOCK, 512), lambda i: (0, first(i), 0)),
            pl.BlockSpec((1, BLOCK, 512), lambda i: (0, first(i), 0)),
            pl.BlockSpec((1, 512, BLOCK), lambda i: (0, 0, second(i))),
        ],
        out_specs=pl.BlockSpec((2, SEL, BLOCK), lambda i: (0, 0, second(i))),
        scratch_shapes=[
            pltpu.VMEM((2 * SEL, 512), F32),
            pltpu.VMEM((2 * SEL, 512), F32),
            pltpu.VMEM((2 * SEL, 512), BF16),
        ],
        compiler_params=pltpu.CompilerParams(vmem_limit_bytes=40 * MIB),
        name="ffn",
    )(expert, mine, theirs, gate, up, down)


def spread_kernel(expert_ref, route_ref, mine_ref, theirs_ref, out_ref, place_scr, y):
    own = expert_ref[0]
    turn = lax.broadcasted_iota(jnp.int32, (EXT, EXT), 1)
    experts = jnp.where(turn == 0, own, own ^ 1)
    wanted = jnp.where(expert_lanes(experts, (EXT, EXT), 0) & (turn < 2), 1.0, 0.0).astype(BF16)
    chosen = jnp.dot(route_ref[...], wanted, preferred_element_type=F32) > 0
    first = lax.broadcasted_iota(jnp.int32, (ROWS, ROWS), 0)
    second = lax.broadcasted_iota(jnp.int32, (ROWS, ROWS), 1)
    earlier = jnp.where((first // 4 == second // 4) & (second < first), 1.0, 0.0).astype(BF16)
    rank = jnp.dot(earlier, jnp.where(chosen, 1.0, 0.0).astype(BF16), preferred_element_type=F32)
    token = lax.broadcasted_iota(jnp.int32, (ROWS, EXT), 0)
    place = jnp.where(chosen, token // 8 * 2 + rank.astype(jnp.int32), -1)
    column = lax.broadcasted_iota(jnp.int32, (ROWS, SEL), 1)
    is_left = lax.broadcasted_iota(jnp.int32, (ROWS, SEL), 0) % 8 < 4
    for e in range(2):
        hit = place[:, e : e + 1] == column
        place_scr[:, e * SEL : (e + 1) * SEL] = jnp.where(hit & is_left, 1.0, 0.0).astype(BF16)
        place_scr[:, (2 + e) * SEL : (3 + e) * SEL] = jnp.where(hit & ~is_left, 1.0, 0.0).astype(BF16)
    for n in range(0, HALF, 512):
        y[0 * SEL : 1 * SEL, :] = mine_ref[:, n : n + 512]
        y[1 * SEL : 2 * SEL, :] = theirs_ref[:, n : n + 512]
        y[2 * SEL : 3 * SEL, :] = mine_ref[:, HALF + n : HALF + n + 512]
        y[3 * SEL : 4 * SEL, :] = theirs_ref[:, HALF + n : HALF + n + 512]
        out_ref[:, n : n + 512] = jnp.dot(place_scr[...], y[...], preferred_element_type=F32).astype(BF16)


def spread(expert, route, mine, theirs):
    vmem = pl.BlockSpec(memory_space=pltpu.VMEM)
    return pl.pallas_call(
        spread_kernel,
        out_shape=jax.ShapeDtypeStruct((ROWS, HALF), BF16),
        in_specs=[pl.BlockSpec(memory_space=pltpu.SMEM), vmem, vmem, vmem],
        scratch_shapes=[pltpu.VMEM((ROWS, 4 * SEL), BF16), pltpu.VMEM((4 * SEL, 512), BF16)],
        compiler_params=pltpu.CompilerParams(vmem_limit_bytes=40 * MIB),
        name="spread",
    )(expert, route, mine, theirs)


def body(tokens, ids, weights, gate, up, down):
    expert = lax.axis_index("dev").astype(jnp.int32).reshape(1)
    near = swap_groups(pack(tokens, ids, weights), NEAR)
    copies = jnp.broadcast_to(near.reshape(1, 64, WIDE), (8, 64, WIDE))
    x = swap_groups(copies, FAR).reshape(ROWS, WIDE)
    picked = select(expert, x)
    mine, sent = picked[0], picked[1]
    results = ffn(expert, mine, to_sibling(sent), gate, up, down)
    returned = to_sibling(results[1])
    y = spread(expert, x[:, HALF:], results[0], returned)
    far = swap_groups(y.reshape(8, 64, HALF), FAR)
    far = jnp.sum(far.astype(F32), axis=0).astype(BF16)
    near = swap_groups(far.reshape(8, 8, HALF), NEAR)
    near = jnp.sum(near.astype(F32), axis=0)
    return jnp.concatenate([near[:4], near[4:]], axis=1).astype(BF16)


def solution(mesh):
    in_specs = (
        P(AXES, None),
        P(AXES, None),
        P(AXES, None),
        P("dev", None, "grp"),
        P("dev", None, "grp"),
        P("dev", "grp", None),
    )
    return jax.shard_map(body, mesh=mesh, in_specs=in_specs, out_specs=P(AXES, None), check_vma=False)
```

```python
import functools

import jax
import jax.numpy as jnp
from jax import lax
from jax.experimental import pallas as pl
from jax.experimental.pallas import tpu as pltpu
from jax.sharding import PartitionSpec as P

AXES = ("grp", "dev")
D = 7168
HALF = D // 2
EXT = 128
WIDE = HALF + EXT
ROWS = 512
SEL = 128
F32 = jnp.float32
BF16 = jnp.bfloat16
MIB = 1 << 20
VMEM = pl.BlockSpec(memory_space=pltpu.VMEM)
SMEM = pl.BlockSpec(memory_space=pltpu.SMEM)


def flat(z, x, y, c):
    return ((z * 4 + x) * 4 + y) * 2 + c


def cube_groups(stage):
    seen, groups = set(), []
    for z in range(4):
        for x in range(4):
            for y in range(4):
                for c in range(2):
                    if flat(z, x, y, c) in seen:
                        continue
                    m = 1 if c == stage else 3
                    members = [
                        flat(z ^ (m * i), x ^ (m * j), y ^ (m * k), c)
                        for i in (0, 1) for j in (0, 1) for k in (0, 1)
                    ]
                    seen.update(members)
                    groups.append(members)
    return groups


NEAR, FAR = cube_groups(0), cube_groups(1)


def swap_groups(values, groups):
    return lax.all_to_all(values, AXES, 0, 0, axis_index_groups=groups, tiled=True)


def to_sibling(values):
    return lax.ppermute(values, "dev", [(i, i ^ 1) for i in range(32)])


def pack_kernel(expert_ref, tokens_ref, ids_ref, weights_ref, out_ref):
    del expert_ref
    lane = lax.broadcasted_iota(jnp.int32, (4, EXT), 1)
    dense = jnp.zeros((4, EXT), F32)
    for k in range(8):
        dense += jnp.where(ids_ref[:, k : k + 1] == lane % 32, weights_ref[:, k : k + 1], 0.0)
    high = dense.astype(BF16).astype(F32)
    route = jnp.where(lane < 32, high, jnp.where(lane < 64, dense - high, 0.0))
    rows = tokens_ref[...].astype(F32)
    left = jnp.concatenate([rows[:, :HALF], route], axis=1)
    right = jnp.concatenate([rows[:, HALF:], route], axis=1)
    block = jnp.concatenate([left, right], axis=0).astype(BF16)
    for i in range(8):
        out_ref[i] = block


def pack(expert, tokens, ids, weights):
    return pl.pallas_call(
        pack_kernel,
        out_shape=jax.ShapeDtypeStruct((8, 8, WIDE), BF16),
        compiler_params=pltpu.CompilerParams(vmem_limit_bytes=4 * MIB),
        in_specs=[SMEM, VMEM, VMEM, VMEM],
        out_specs=VMEM,
        name="pack",
    )(expert, tokens, ids, weights)


def expert_lanes(expert, shape, dim):
    lane = lax.broadcasted_iota(jnp.int32, shape, dim)
    return (lane < 64) & (lane % 32 == expert)


def select_kernel(expert_ref, x_ref, mine_ref, sent_ref, pick):
    own = expert_ref[0]
    turn = lax.broadcasted_iota(jnp.int32, (8, EXT), 0)
    experts = jnp.where(turn == 0, own, own ^ 1)
    wanted = jnp.where(expert_lanes(experts, (8, EXT), 1) & (turn < 2), 1.0, 0.0).astype(BF16)
    route = lax.dot_general(
        wanted, x_ref[:, HALF:], (((1,), (1,)), ((), ())), preferred_element_type=F32
    )
    chosen = route > 0
    first = lax.broadcasted_iota(jnp.int32, (ROWS, ROWS), 0)
    second = lax.broadcasted_iota(jnp.int32, (ROWS, ROWS), 1)
    earlier = jnp.where((first // 4 == second // 4) & (first < second), 1.0, 0.0).astype(BF16)
    rank = jnp.dot(jnp.where(chosen, 1.0, 0.0).astype(BF16), earlier, preferred_element_type=F32)
    column = lax.broadcasted_iota(jnp.int32, (8, ROWS), 1)
    place = jnp.where(chosen, column // 8 * 2 + rank.astype(jnp.int32), -1)
    row = lax.broadcasted_iota(jnp.int32, (SEL, ROWS), 0)
    is_left = lax.broadcasted_iota(jnp.int32, (SEL, ROWS), 1) % 8 < 4
    for e in range(2):
        hit = place[e : e + 1, :] == row
        pick[0, e * SEL : (e + 1) * SEL, :] = jnp.where(hit & is_left, 1.0, 0.0).astype(BF16)
        pick[1, e * SEL : (e + 1) * SEL, :] = jnp.where(hit & ~is_left, 1.0, 0.0).astype(BF16)

    def put(start, size, side, to):
        value = jnp.dot(pick[side], x_ref[:, start : start + size], preferred_element_type=F32).astype(BF16)
        mine_ref[:, to : to + size] = value[:SEL]
        sent_ref[:, to : to + size] = value[SEL:]

    for n in range(0, HALF, 512):
        put(n, 512, 0, n)
        put(n, 512, 1, HALF + n)
    put(HALF, EXT, 0, D)


def select(expert, x):
    return pl.pallas_call(
        select_kernel,
        out_shape=[jax.ShapeDtypeStruct((SEL, D + EXT), BF16)] * 2,
        in_specs=[pl.BlockSpec(memory_space=pltpu.SMEM), pl.BlockSpec(memory_space=pltpu.VMEM)],
        scratch_shapes=[pltpu.VMEM((2, 2 * SEL, ROWS), BF16)],
        compiler_params=pltpu.CompilerParams(vmem_limit_bytes=12 * MIB),
        name="select",
    )(expert, x)


DEPTH = 1792


def hidden_units(expert_ref, x_ref, gate_ref, up_ref, hidden, gate_sum, up_sum):
    gate_sum[...] = jnp.zeros_like(gate_sum)
    up_sum[...] = jnp.zeros_like(up_sum)

    @pl.loop(0, D // DEPTH)
    def _(i):
        block = pl.ds(pl.multiple_of(i * DEPTH, DEPTH), DEPTH)
        x = x_ref[:, block]
        gate_sum[...] += jnp.dot(x, gate_ref[0, block, :], preferred_element_type=F32)
        up_sum[...] += jnp.dot(x, up_ref[0, block, :], preferred_element_type=F32)

    lanes = expert_lanes(expert_ref[0], (SEL, EXT), 1)
    scale = jnp.sum(jnp.where(lanes, x_ref[:, D:].astype(F32), 0.0), axis=1, keepdims=True)
    v = gate_sum[...]
    hidden[...] = (v / (1.0 + jnp.exp(-v)) * up_sum[...] * scale).astype(BF16)


def down_rows(hidden, down_ref, out_ref):
    @pl.loop(0, D // 1024)
    def _(i):
        block = pl.ds(pl.multiple_of(i * 1024, 1024), 1024)
        out_ref[:, block] = jnp.dot(hidden[...], down_ref[0, :, block], preferred_element_type=F32).astype(BF16)


def hidden_units_after(expert_ref, x_ref, gate_ref, up_ref, earlier_ref, *rest):
    del earlier_ref
    hidden_units(expert_ref, x_ref, gate_ref, up_ref, *rest)


SUMS = [pltpu.VMEM((SEL, 512), F32), pltpu.VMEM((SEL, 512), F32)]
SMALL = pltpu.CompilerParams(vmem_limit_bytes=8 * MIB)


def first_half(expert, x, gate, up, earlier=()):
    return pl.pallas_call(
        hidden_units_after if earlier else hidden_units,
        out_shape=jax.ShapeDtypeStruct((SEL, 512), BF16),
        in_specs=[SMEM, VMEM, VMEM, VMEM] + [VMEM] * len(earlier),
        out_specs=VMEM,
        scratch_shapes=SUMS,
        compiler_params=SMALL,
        cost_estimate=pl.CostEstimate(flops=4 * SEL * D * 512, bytes_accessed=17 << 20, transcendentals=0),
        name="hidden",
    )(expert, x, gate, up, *earlier)


def second_half(hidden, down):
    return pl.pallas_call(
        down_rows,
        out_shape=jax.ShapeDtypeStruct((SEL, D), BF16),
        in_specs=[VMEM, VMEM],
        out_specs=VMEM,
        compiler_params=SMALL,
        cost_estimate=pl.CostEstimate(flops=2 * SEL * D * 512, bytes_accessed=9 << 20, transcendentals=0),
        name="down",
    )(hidden, down)


def spread_kernel(expert_ref, route_ref, mine_ref, theirs_ref, out_ref, place_scr, y):
    own = expert_ref[0]
    turn = lax.broadcasted_iota(jnp.int32, (EXT, EXT), 1)
    experts = jnp.where(turn == 0, own, own ^ 1)
    wanted = jnp.where(expert_lanes(experts, (EXT, EXT), 0) & (turn < 2), 1.0, 0.0).astype(BF16)
    chosen = jnp.dot(route_ref[...], wanted, preferred_element_type=F32) > 0
    first = lax.broadcasted_iota(jnp.int32, (ROWS, ROWS), 0)
    second = lax.broadcasted_iota(jnp.int32, (ROWS, ROWS), 1)
    earlier = jnp.where((first // 4 == second // 4) & (second < first), 1.0, 0.0).astype(BF16)
    rank = jnp.dot(earlier, jnp.where(chosen, 1.0, 0.0).astype(BF16), preferred_element_type=F32)
    token = lax.broadcasted_iota(jnp.int32, (ROWS, EXT), 0)
    place = jnp.where(chosen, token // 8 * 2 + rank.astype(jnp.int32), -1)
    column = lax.broadcasted_iota(jnp.int32, (ROWS, SEL), 1)
    is_left = lax.broadcasted_iota(jnp.int32, (ROWS, SEL), 0) % 8 < 4
    for e in range(2):
        hit = place[:, e : e + 1] == column
        place_scr[:, e * SEL : (e + 1) * SEL] = jnp.where(hit & is_left, 1.0, 0.0).astype(BF16)
        place_scr[:, (2 + e) * SEL : (3 + e) * SEL] = jnp.where(hit & ~is_left, 1.0, 0.0).astype(BF16)
    for n in range(0, HALF, 512):
        y[0 * SEL : 1 * SEL, :] = mine_ref[:, n : n + 512]
        y[1 * SEL : 2 * SEL, :] = theirs_ref[:, n : n + 512]
        y[2 * SEL : 3 * SEL, :] = mine_ref[:, HALF + n : HALF + n + 512]
        y[3 * SEL : 4 * SEL, :] = theirs_ref[:, HALF + n : HALF + n + 512]
        out_ref[:, n : n + 512] = jnp.dot(place_scr[...], y[...], preferred_element_type=F32).astype(BF16)


def spread(expert, route, mine, theirs):
    vmem = pl.BlockSpec(memory_space=pltpu.VMEM)
    return pl.pallas_call(
        spread_kernel,
        out_shape=jax.ShapeDtypeStruct((ROWS, HALF), BF16),
        in_specs=[pl.BlockSpec(memory_space=pltpu.SMEM), vmem, vmem, vmem],
        scratch_shapes=[pltpu.VMEM((ROWS, 4 * SEL), BF16), pltpu.VMEM((4 * SEL, 512), BF16)],
        compiler_params=pltpu.CompilerParams(vmem_limit_bytes=12 * MIB),
        name="spread",
    )(expert, route, mine, theirs)


def total_kernel(parts_ref, out_ref):
    for n in range(0, HALF, 512):
        total = parts_ref[0, :, n : n + 512].astype(F32)
        for i in range(1, 8):
            total += parts_ref[i, :, n : n + 512].astype(F32)
        out_ref[:, n : n + 512] = total.astype(BF16)


def total(parts):
    return pl.pallas_call(
        total_kernel,
        out_shape=jax.ShapeDtypeStruct((64, HALF), BF16),
        in_specs=[VMEM],
        out_specs=VMEM,
        compiler_params=SMALL,
        name="total",
    )(parts)


def finish_kernel(parts_ref, out_ref):
    total = parts_ref[0].astype(F32)
    for i in range(1, 8):
        total += parts_ref[i].astype(F32)
    out_ref[:, :HALF] = total[:4].astype(BF16)
    out_ref[:, HALF:] = total[4:].astype(BF16)


def finish(parts):
    return pl.pallas_call(
        finish_kernel,
        out_shape=jax.ShapeDtypeStruct((4, D), BF16),
        in_specs=[VMEM],
        out_specs=VMEM,
        compiler_params=SMALL,
        name="finish",
    )(parts)


def body(tokens, ids, weights, gate, up, down):
    expert = lax.axis_index("dev").astype(jnp.int32).reshape(1)
    near = swap_groups(pack(expert, tokens, ids, weights), NEAR)
    copies = jnp.broadcast_to(near.reshape(1, 64, WIDE), (8, 64, WIDE))
    x = swap_groups(copies, FAR).reshape(ROWS, WIDE)
    mine, sent = select(expert, x)
    arrived = to_sibling(sent)
    hidden = first_half(expert, mine, gate, up)
    hidden_sent = first_half(expert, arrived, gate, up, (hidden,))
    returned = to_sibling(second_half(hidden_sent, down))
    y = spread(expert, x[:, HALF:], second_half(hidden, down), returned)
    far = total(swap_groups(y.reshape(8, 64, HALF), FAR))
    return finish(swap_groups(far.reshape(8, 8, HALF), NEAR))


def solution(mesh):
    in_specs = (
        P(AXES, None),
        P(AXES, None),
        P(AXES, None),
        P("dev", None, "grp"),
        P("dev", None, "grp"),
        P("dev", "grp", None),
    )
    return jax.shard_map(body, mesh=mesh, in_specs=in_specs, out_specs=P(AXES, None), check_vma=False)
```

```python
import functools

import jax
import jax.numpy as jnp
from jax import lax
from jax.experimental import pallas as pl
from jax.experimental.pallas import tpu as pltpu
from jax.sharding import PartitionSpec as P

AXES = ("grp", "dev")
D = 7168
HALF = D // 2
EXT = 128
WIDE = HALF + EXT
BLOCK = 64
PART = 4 * BLOCK
SEL = 64
F32 = jnp.float32
BF16 = jnp.bfloat16
MIB = 1 << 20
VMEM = pl.BlockSpec(memory_space=pltpu.VMEM)
SMEM = pl.BlockSpec(memory_space=pltpu.SMEM)


BRIEF = pl.CostEstimate(flops=1000, bytes_accessed=1000, transcendentals=0)


def flat(z, x, y, c):
    return ((z * 4 + x) * 4 + y) * 2 + c


def near_groups():
    seen, groups = set(), []
    for z in range(4):
        for x in range(4):
            for y in range(4):
                for c in range(2):
                    if flat(z, x, y, c) in seen:
                        continue
                    m = 3 if c else 1
                    members = [
                        flat(z ^ (m * i), x ^ (m * j), y ^ (m * k), c)
                        for i in (0, 1) for j in (0, 1) for k in (0, 1)
                    ]
                    seen.update(members)
                    groups.append(members)
    return groups


def far_pairs(axis):
    pairs = []
    for z in range(4):
        for x in range(4):
            for y in range(4):
                for c in range(2):
                    at = [z, x, y]
                    at[axis] ^= 1 if c else 3
                    pairs.append((flat(z, x, y, c), flat(*at, c)))
    return pairs


NEAR = near_groups()
FAR = [far_pairs(axis) for axis in range(3)]


def swap_near(values):
    return lax.all_to_all(values, AXES, 0, 0, axis_index_groups=NEAR, tiled=True)


def swap_far(values, axis):
    return lax.ppermute(values, AXES, FAR[axis])


def to_sibling(values):
    return lax.ppermute(values, "dev", [(i, i ^ 1) for i in range(32)])


def pack_kernel(expert_ref, tokens_ref, ids_ref, weights_ref, out_ref):
    del expert_ref
    lane = lax.broadcasted_iota(jnp.int32, (4, EXT), 1)
    dense = jnp.zeros((4, EXT), F32)
    for k in range(8):
        dense += jnp.where(ids_ref[:, k : k + 1] == lane % 32, weights_ref[:, k : k + 1], 0.0)
    high = dense.astype(BF16).astype(F32)
    route = jnp.where(lane < 32, high, jnp.where(lane < 64, dense - high, 0.0))
    rows = tokens_ref[...].astype(F32)
    left = jnp.concatenate([rows[:, :HALF], route], axis=1)
    right = jnp.concatenate([rows[:, HALF:], route], axis=1)
    block = jnp.concatenate([left, right], axis=0).astype(BF16)
    for i in range(8):
        out_ref[i] = block


def pack(expert, tokens, ids, weights):
    return pl.pallas_call(
        pack_kernel,
        out_shape=jax.ShapeDtypeStruct((8, 8, WIDE), BF16),
        compiler_params=pltpu.CompilerParams(vmem_limit_bytes=4 * MIB),
        in_specs=[SMEM, VMEM, VMEM, VMEM],
        out_specs=VMEM,
        name="pack",
    )(expert, tokens, ids, weights)


def expert_lanes(expert, shape, dim):
    lane = lax.broadcasted_iota(jnp.int32, shape, dim)
    return (lane < 64) & (lane % 32 == expert)


def select_kernel(expert_ref, a_ref, b_ref, c_ref, d_ref, after_ref, mine_ref, sent_ref, pick):
    del after_ref
    blocks = (a_ref, b_ref, c_ref, d_ref)
    own = expert_ref[0]
    turn = lax.broadcasted_iota(jnp.int32, (8, EXT), 0)
    experts = jnp.where(turn == 0, own, own ^ 1)
    wanted = jnp.where(expert_lanes(experts, (8, EXT), 1) & (turn < 2), 1.0, 0.0).astype(BF16)
    ext = jnp.concatenate([ref[:, HALF:] for ref in blocks], axis=0)
    route = lax.dot_general(wanted, ext, (((1,), (1,)), ((), ())), preferred_element_type=F32)
    chosen = route > 0
    first = lax.broadcasted_iota(jnp.int32, (PART, PART), 0)
    second = lax.broadcasted_iota(jnp.int32, (PART, PART), 1)
    earlier = jnp.where((first // 4 == second // 4) & (first < second), 1.0, 0.0).astype(BF16)
    rank = jnp.dot(jnp.where(chosen, 1.0, 0.0).astype(BF16), earlier, preferred_element_type=F32)
    column = lax.broadcasted_iota(jnp.int32, (8, PART), 1)
    place = jnp.where(chosen, column // 8 * 2 + rank.astype(jnp.int32), -1)
    row = lax.broadcasted_iota(jnp.int32, (SEL, PART), 0)
    is_left = lax.broadcasted_iota(jnp.int32, (SEL, PART), 1) % 8 < 4
    for e in range(2):
        hit = place[e : e + 1, :] == row
        pick[e * SEL : (e + 1) * SEL, :] = jnp.where(hit & is_left, 1.0, 0.0).astype(BF16)
        pick[(2 + e) * SEL : (3 + e) * SEL, :] = jnp.where(hit & ~is_left, 1.0, 0.0).astype(BF16)
    for n in range(0, HALF, 512):
        x = jnp.concatenate([ref[:, n : n + 512] for ref in blocks], axis=0)
        value = jnp.dot(pick[...], x, preferred_element_type=F32).astype(BF16)
        mine_ref[:, n : n + 512] = value[:SEL]
        sent_ref[:, n : n + 512] = value[SEL : 2 * SEL]
        mine_ref[:, HALF + n : HALF + n + 512] = value[2 * SEL : 3 * SEL]
        sent_ref[:, HALF + n : HALF + n + 512] = value[3 * SEL :]
    value = jnp.dot(pick[: 2 * SEL, :], ext, preferred_element_type=F32).astype(BF16)
    mine_ref[:, D:] = value[:SEL]
    sent_ref[:, D:] = value[SEL:]


def select(expert, blocks, after):
    return pl.pallas_call(
        select_kernel,
        out_shape=[jax.ShapeDtypeStruct((SEL, D + EXT), BF16)] * 2,
        in_specs=[SMEM] + [VMEM] * 4 + [pl.BlockSpec(memory_space=pl.ANY)],
        out_specs=[VMEM, VMEM],
        scratch_shapes=[pltpu.VMEM((PART, PART), BF16)],
        compiler_params=SMALL,
        cost_estimate=BRIEF,
        name="select",
    )(expert, *blocks, after)


DEPTH = 1792


def hidden_units(expert_ref, x_ref, gate_ref, up_ref, hidden, gate_sum, up_sum):
    for i in range(0, D, DEPTH):
        block = slice(i, i + DEPTH)
        x = x_ref[:, block]
        gate = jnp.dot(x, gate_ref[0, block, :], preferred_element_type=F32)
        up = jnp.dot(x, up_ref[0, block, :], preferred_element_type=F32)
        gate_sum[...] = gate if i == 0 else gate_sum[...] + gate
        up_sum[...] = up if i == 0 else up_sum[...] + up
    lanes = expert_lanes(expert_ref[0], (SEL, EXT), 1)
    scale = jnp.sum(jnp.where(lanes, x_ref[:, D:].astype(F32), 0.0), axis=1, keepdims=True)
    v = gate_sum[...]
    hidden[...] = (v / (1.0 + jnp.exp(-v)) * up_sum[...] * scale).astype(BF16)


def down_rows(hidden, down_ref, out_ref):
    for n in range(0, D, 1024):
        block = slice(n, n + 1024)
        out_ref[:, block] = jnp.dot(hidden[...], down_ref[0, :, block], preferred_element_type=F32).astype(BF16)


def hidden_units_after(expert_ref, x_ref, gate_ref, up_ref, earlier_ref, *rest):
    del earlier_ref
    hidden_units(expert_ref, x_ref, gate_ref, up_ref, *rest)


SUMS = [pltpu.VMEM((SEL, 512), F32), pltpu.VMEM((SEL, 512), F32)]
SMALL = pltpu.CompilerParams(vmem_limit_bytes=8 * MIB)


def load_kernel(source_ref, after_ref, out_ref, sem):
    del after_ref
    copy = pltpu.make_async_copy(source_ref, out_ref, sem)
    copy.start()
    copy.wait()


def load(source, after):
    return pl.pallas_call(
        load_kernel,
        out_shape=jax.ShapeDtypeStruct(source.shape, source.dtype),
        in_specs=[pl.BlockSpec(memory_space=pltpu.HBM), pl.BlockSpec(memory_space=pl.ANY)],
        out_specs=VMEM,
        scratch_shapes=[pltpu.SemaphoreType.DMA],
        compiler_params=SMALL,
        cost_estimate=BRIEF,
        name="load",
    )(pltpu.with_memory_space_constraint(source, pltpu.HBM), after)


def first_half(expert, x, gate, up, earlier=()):
    return pl.pallas_call(
        hidden_units_after if earlier else hidden_units,
        out_shape=jax.ShapeDtypeStruct((SEL, 512), BF16),
        in_specs=[SMEM, VMEM, VMEM, VMEM] + [VMEM] * len(earlier),
        out_specs=VMEM,
        scratch_shapes=SUMS,
        compiler_params=SMALL,
        cost_estimate=BRIEF,
        name="hidden",
    )(expert, x, gate, up, *earlier)


def second_half(hidden, down):
    return pl.pallas_call(
        down_rows,
        out_shape=jax.ShapeDtypeStruct((SEL, D), BF16),
        in_specs=[VMEM, VMEM],
        out_specs=VMEM,
        compiler_params=SMALL,
        cost_estimate=BRIEF,
        name="down",
    )(hidden, down)


def spread_kernel(count, expert_ref, a_ref, b_ref, c_ref, d_ref, mine_ref, theirs_ref, *refs):
    arrived, outs, place_scr = refs[:count], refs[count : count + 4], refs[count + 4]
    own = expert_ref[0]
    turn = lax.broadcasted_iota(jnp.int32, (EXT, EXT), 1)
    experts = jnp.where(turn == 0, own, own ^ 1)
    wanted = jnp.where(expert_lanes(experts, (EXT, EXT), 0) & (turn < 2), 1.0, 0.0).astype(BF16)
    ext = jnp.concatenate([ref[:, HALF:] for ref in (a_ref, b_ref, c_ref, d_ref)], axis=0)
    chosen = jnp.dot(ext, wanted, preferred_element_type=F32) > 0
    first = lax.broadcasted_iota(jnp.int32, (PART, PART), 0)
    second = lax.broadcasted_iota(jnp.int32, (PART, PART), 1)
    earlier = jnp.where((first // 4 == second // 4) & (second < first), 1.0, 0.0).astype(BF16)
    rank = jnp.dot(earlier, jnp.where(chosen, 1.0, 0.0).astype(BF16), preferred_element_type=F32)
    token = lax.broadcasted_iota(jnp.int32, (PART, EXT), 0)
    place = jnp.where(chosen, token // 8 * 2 + rank.astype(jnp.int32), -1)
    column = lax.broadcasted_iota(jnp.int32, (PART, 2 * SEL), 1)
    hit = jnp.where(column < SEL, place[:, 0:1], place[:, 1:2]) == column % SEL
    is_left = lax.broadcasted_iota(jnp.int32, (PART, 2 * SEL), 0) % 8 < 4
    place_scr[:, : 2 * SEL] = jnp.where(hit & is_left, 1.0, 0.0).astype(BF16)
    place_scr[:, 2 * SEL :] = jnp.where(hit & ~is_left, 1.0, 0.0).astype(BF16)
    for n in range(0, HALF, 512):
        left, right = slice(n, n + 512), slice(HALF + n, HALF + n + 512)
        y = jnp.concatenate([mine_ref[:, left], theirs_ref[:, left], mine_ref[:, right], theirs_ref[:, right]], axis=0)
        value = jnp.dot(place_scr[...], y, preferred_element_type=F32)
        for i in range(4):
            block = value[i * BLOCK : (i + 1) * BLOCK]
            if i < count:
                block += arrived[i][:, left].astype(F32)
            outs[i][:, left] = block.astype(BF16)


def spread(expert, blocks, mine, theirs, arrived=()):
    return pl.pallas_call(
        functools.partial(spread_kernel, len(arrived)),
        out_shape=[jax.ShapeDtypeStruct((BLOCK, HALF), BF16)] * 4,
        in_specs=[SMEM] + [VMEM] * (6 + len(arrived)),
        out_specs=[VMEM] * 4,
        scratch_shapes=[pltpu.VMEM((PART, 4 * SEL), BF16)],
        compiler_params=SMALL,
        cost_estimate=BRIEF,
        name="spread",
    )(expert, *blocks, mine, theirs, *arrived)


def add(*terms):
    total = terms[0].astype(F32)
    for term in terms[1:]:
        total += term.astype(F32)
    return total.astype(BF16)


def finish_kernel(parts_ref, out_ref):
    total = parts_ref[0].astype(F32)
    for i in range(1, 8):
        total += parts_ref[i].astype(F32)
    out_ref[:, :HALF] = total[:4].astype(BF16)
    out_ref[:, HALF:] = total[4:].astype(BF16)


def finish(parts):
    return pl.pallas_call(
        finish_kernel,
        out_shape=jax.ShapeDtypeStruct((4, D), BF16),
        in_specs=[VMEM],
        out_specs=VMEM,
        compiler_params=SMALL,
        name="finish",
    )(parts)


def body(tokens, ids, weights, gate, up, down):
    expert = lax.axis_index("dev").astype(jnp.int32).reshape(1)
    own = swap_near(pack(expert, tokens, ids, weights)).reshape(BLOCK, WIDE)
    x, y, z = swap_far(own, 0), swap_far(own, 1), swap_far(own, 2)
    up = load(up, own)
    xy, yz, zx = swap_far(y, 0), swap_far(z, 1), swap_far(x, 2)
    mine_near, sent_near = select(expert, (x, y, z, own), up)
    got_near = to_sibling(sent_near)
    hidden_mine_near = first_half(expert, mine_near, gate, up)
    xy, yz, zx, hidden_mine_near = lax.optimization_barrier((xy, yz, zx, hidden_mine_near))
    xyz = swap_far(yz, 0)
    hidden_got_near = first_half(expert, got_near, gate, up, (hidden_mine_near,))
    mine_far, sent_far = select(expert, (xy, zx, yz, xyz), hidden_got_near)
    got_far = to_sibling(sent_far)
    hidden_mine_far = first_half(expert, mine_far, gate, up, (hidden_got_near,))
    hidden_got_far = first_half(expert, got_far, gate, up, (hidden_mine_far,))
    returned = to_sibling(second_half(hidden_got_far, down))
    y_xy, y_zx, y_yz, y_xyz = spread(expert, (xy, zx, yz, xyz), second_half(hidden_mine_far, down), returned)
    at_yz = swap_far(y_xyz, 0)
    at_y, at_x = swap_far(y_xy, 0), swap_far(y_zx, 2)
    returned = to_sibling(second_half(hidden_got_near, down))
    at_z = swap_far(add(y_yz, at_yz), 1)
    y_x, y_y, y_z, y_own = spread(
        expert, (x, y, z, own), second_half(hidden_mine_near, down), returned, (at_x, at_y)
    )
    total = add(y_own, swap_far(y_x, 0), swap_far(y_y, 1), swap_far(add(y_z, at_z), 2))
    return finish(swap_near(total.reshape(8, 8, HALF)))


def solution(mesh):
    in_specs = (
        P(AXES, None),
        P(AXES, None),
        P(AXES, None),
        P("dev", None, "grp"),
        P("dev", None, "grp"),
        P("dev", "grp", None),
    )
    return jax.shard_map(body, mesh=mesh, in_specs=in_specs, out_specs=P(AXES, None), check_vma=False)
```

```python
import functools

import jax
import jax.numpy as jnp
from jax import lax
from jax.experimental import pallas as pl
from jax.experimental.pallas import tpu as pltpu
from jax.sharding import PartitionSpec as P

AXES = ("grp", "dev")
D = 7168
HALF = D // 2
EXT = 128
WIDE = HALF + EXT
BLOCK = 64
PART = 4 * BLOCK
SEL = 64
F32 = jnp.float32
BF16 = jnp.bfloat16
MIB = 1 << 20
VMEM = pl.BlockSpec(memory_space=pltpu.VMEM)
SMEM = pl.BlockSpec(memory_space=pltpu.SMEM)
HBM = pl.BlockSpec(memory_space=pltpu.HBM)
ANY = pl.BlockSpec(memory_space=pl.ANY)
SMALL = pltpu.CompilerParams(vmem_limit_bytes=8 * MIB)
CUT = 2048


BRIEF = pl.CostEstimate(flops=1000, bytes_accessed=1000, transcendentals=0)


def flat(z, x, y, c):
    return ((z * 4 + x) * 4 + y) * 2 + c


def near_groups():
    seen, groups = set(), []
    for z in range(4):
        for x in range(4):
            for y in range(4):
                for c in range(2):
                    if flat(z, x, y, c) in seen:
                        continue
                    m = 3 if c else 1
                    members = [
                        flat(z ^ (m * i), x ^ (m * j), y ^ (m * k), c)
                        for i in (0, 1) for j in (0, 1) for k in (0, 1)
                    ]
                    seen.update(members)
                    groups.append(members)
    return groups


def far_pairs(axis):
    pairs = []
    for z in range(4):
        for x in range(4):
            for y in range(4):
                for c in range(2):
                    at = [z, x, y]
                    at[axis] ^= 1 if c else 3
                    pairs.append((flat(z, x, y, c), flat(*at, c)))
    return pairs


NEAR = near_groups()
FAR = [far_pairs(axis) for axis in range(3)]


def swap_near(values):
    return lax.all_to_all(values, AXES, 0, 0, axis_index_groups=NEAR, tiled=True)


def swap_far(values, axis):
    return lax.ppermute(values, AXES, FAR[axis])


def to_sibling(values):
    return lax.ppermute(values, "dev", [(i, i ^ 1) for i in range(32)])


def pack_kernel(expert_ref, tokens_hbm, ids_hbm, weights_hbm, out_ref, tokens_ref, ids_ref, weights_ref, sems):
    del expert_ref
    pairs = ((tokens_hbm, tokens_ref), (ids_hbm, ids_ref), (weights_hbm, weights_ref))
    copies = [pltpu.make_async_copy(source, target, sems.at[i]) for i, (source, target) in enumerate(pairs)]
    for copy in copies:
        copy.start()
    for copy in copies:
        copy.wait()
    lane = lax.broadcasted_iota(jnp.int32, (4, EXT), 1)
    dense = jnp.zeros((4, EXT), F32)
    for k in range(8):
        dense += jnp.where(ids_ref[:, k : k + 1] == lane % 32, weights_ref[:, k : k + 1], 0.0)
    high = dense.astype(BF16).astype(F32)
    route = jnp.where(lane < 32, high, jnp.where(lane < 64, dense - high, 0.0))
    rows = tokens_ref[...].astype(F32)
    left = jnp.concatenate([rows[:, :HALF], route], axis=1)
    right = jnp.concatenate([rows[:, HALF:], route], axis=1)
    block = jnp.concatenate([left, right], axis=0).astype(BF16)
    for i in range(8):
        out_ref[i] = block


def in_hbm(values):
    return pltpu.with_memory_space_constraint(values, pltpu.HBM)


def pack(expert, tokens, ids, weights):
    return pl.pallas_call(
        pack_kernel,
        out_shape=jax.ShapeDtypeStruct((8, 8, WIDE), BF16),
        in_specs=[SMEM, HBM, HBM, HBM],
        out_specs=VMEM,
        scratch_shapes=[
            pltpu.VMEM((4, D), BF16),
            pltpu.VMEM((4, 8), jnp.int32),
            pltpu.VMEM((4, 8), F32),
            pltpu.SemaphoreType.DMA((3,)),
        ],
        compiler_params=pltpu.CompilerParams(vmem_limit_bytes=4 * MIB),
        name="pack",
    )(expert, in_hbm(tokens), in_hbm(ids), in_hbm(weights))


def expert_lanes(expert, shape, dim):
    lane = lax.broadcasted_iota(jnp.int32, shape, dim)
    return (lane < 64) & (lane % 32 == expert)


def block_columns(refs, start, size):
    if len(refs) == 1:
        return refs[0][:, start : start + size]
    if start < CUT:
        return refs[0][:, start : start + size]
    return refs[1][:, start - CUT : start - CUT + size]


def select_kernel(pieces, loads, expert_ref, *refs):
    refs = list(refs)
    blocks = [[refs.pop(0) for _ in range(n)] for n in pieces]
    sources = [refs.pop(0) for _ in range(loads)]
    del refs[0]
    mine_ref, sent_ref = refs[:2]
    targets = refs[2 : 2 + loads]
    pick, sems = refs[2 + loads :]
    copies = [pltpu.make_async_copy(sources[i], targets[i], sems.at[i]) for i in range(loads)]
    for copy in copies:
        copy.start()
    own = expert_ref[0]
    turn = lax.broadcasted_iota(jnp.int32, (8, EXT), 0)
    experts = jnp.where(turn == 0, own, own ^ 1)
    wanted = jnp.where(expert_lanes(experts, (8, EXT), 1) & (turn < 2), 1.0, 0.0).astype(BF16)
    ext = jnp.concatenate([block_columns(block, HALF, EXT) for block in blocks], axis=0)
    route = lax.dot_general(wanted, ext, (((1,), (1,)), ((), ())), preferred_element_type=F32)
    chosen = route > 0
    first = lax.broadcasted_iota(jnp.int32, (PART, PART), 0)
    second = lax.broadcasted_iota(jnp.int32, (PART, PART), 1)
    earlier = jnp.where((first // 4 == second // 4) & (first < second), 1.0, 0.0).astype(BF16)
    rank = jnp.dot(jnp.where(chosen, 1.0, 0.0).astype(BF16), earlier, preferred_element_type=F32)
    column = lax.broadcasted_iota(jnp.int32, (8, PART), 1)
    place = jnp.where(chosen, column // 8 * 2 + rank.astype(jnp.int32), -1)
    row = lax.broadcasted_iota(jnp.int32, (SEL, PART), 0)
    is_left = lax.broadcasted_iota(jnp.int32, (SEL, PART), 1) % 8 < 4
    for e in range(2):
        hit = place[e : e + 1, :] == row
        pick[e * SEL : (e + 1) * SEL, :] = jnp.where(hit & is_left, 1.0, 0.0).astype(BF16)
        pick[(2 + e) * SEL : (3 + e) * SEL, :] = jnp.where(hit & ~is_left, 1.0, 0.0).astype(BF16)
    for n in range(0, HALF, 512):
        x = jnp.concatenate([block_columns(block, n, 512) for block in blocks], axis=0)
        value = jnp.dot(pick[...], x, preferred_element_type=F32).astype(BF16)
        mine_ref[:, n : n + 512] = value[:SEL]
        sent_ref[:, n : n + 512] = value[SEL : 2 * SEL]
        mine_ref[:, HALF + n : HALF + n + 512] = value[2 * SEL : 3 * SEL]
        sent_ref[:, HALF + n : HALF + n + 512] = value[3 * SEL :]
    value = jnp.dot(pick[: 2 * SEL, :], ext, preferred_element_type=F32).astype(BF16)
    mine_ref[:, D:] = value[:SEL]
    sent_ref[:, D:] = value[SEL:]
    for copy in copies:
        copy.wait()


def select(expert, blocks, after, loads=()):
    arrays = [piece for block in blocks for piece in block]
    return pl.pallas_call(
        functools.partial(select_kernel, tuple(len(block) for block in blocks), len(loads)),
        out_shape=[jax.ShapeDtypeStruct((SEL, D + EXT), BF16)] * 2
        + [jax.ShapeDtypeStruct(load.shape, load.dtype) for load in loads],
        in_specs=[SMEM] + [VMEM] * len(arrays) + [HBM] * len(loads) + [ANY],
        out_specs=[VMEM] * (2 + len(loads)),
        scratch_shapes=[pltpu.VMEM((PART, PART), BF16), pltpu.SemaphoreType.DMA((2,))],
        compiler_params=SMALL,
        cost_estimate=BRIEF,
        name="select",
    )(expert, *arrays, *[in_hbm(load) for load in loads], after)


DEPTH = 1792


def load_kernel(source_ref, after_ref, out_ref, sem):
    del after_ref
    copy = pltpu.make_async_copy(source_ref, out_ref, sem)
    copy.start()
    copy.wait()


def load(source, after):
    return pl.pallas_call(
        load_kernel,
        out_shape=jax.ShapeDtypeStruct(source.shape, source.dtype),
        in_specs=[HBM, ANY],
        out_specs=VMEM,
        scratch_shapes=[pltpu.SemaphoreType.DMA],
        compiler_params=SMALL,
        cost_estimate=BRIEF,
        name="load",
    )(in_hbm(source), after)


def hidden_kernel(expert_ref, mine_ref, theirs_ref, gate_ref, up_ref, after_ref, hidden, gate_sum, up_sum):
    del after_ref
    for i in range(0, D, DEPTH):
        block = slice(i, i + DEPTH)
        x = jnp.concatenate([mine_ref[:, block], theirs_ref[:, block]], axis=0)
        gate = jnp.dot(x, gate_ref[0, block, :], preferred_element_type=F32)
        up = jnp.dot(x, up_ref[0, block, :], preferred_element_type=F32)
        gate_sum[...] = gate if i == 0 else gate_sum[...] + gate
        up_sum[...] = up if i == 0 else up_sum[...] + up
    lanes = expert_lanes(expert_ref[0], (2 * SEL, EXT), 1)
    route = jnp.concatenate([mine_ref[:, D:], theirs_ref[:, D:]], axis=0).astype(F32)
    scale = jnp.sum(jnp.where(lanes, route, 0.0), axis=1, keepdims=True)
    v = gate_sum[...]
    hidden[...] = (v / (1.0 + jnp.exp(-v)) * up_sum[...] * scale).astype(BF16)


def hidden_units(expert, mine, theirs, gate, up, after):
    return pl.pallas_call(
        hidden_kernel,
        out_shape=jax.ShapeDtypeStruct((2 * SEL, 512), BF16),
        in_specs=[SMEM, VMEM, VMEM, VMEM, VMEM, ANY],
        out_specs=VMEM,
        scratch_shapes=[pltpu.VMEM((2 * SEL, 512), F32)] * 2,
        compiler_params=SMALL,
        cost_estimate=BRIEF,
        name="hidden",
    )(expert, mine, theirs, gate, up, after)


def down_kernel(part, hidden_ref, down_ref, after_ref, out_ref):
    del after_ref
    for n in range(0, D, 1024):
        block = slice(n, n + 1024)
        rows = hidden_ref[part * SEL : (part + 1) * SEL, :]
        out_ref[:, block] = jnp.dot(rows, down_ref[0, :, block], preferred_element_type=F32).astype(BF16)


def down_rows(part, hidden, down, after):
    return pl.pallas_call(
        functools.partial(down_kernel, part),
        out_shape=jax.ShapeDtypeStruct((SEL, D), BF16),
        in_specs=[VMEM, VMEM, ANY],
        out_specs=VMEM,
        compiler_params=SMALL,
        cost_estimate=BRIEF,
        name="down",
    )(hidden, down, after)


def spread_kernel(expert_ref, *refs):
    refs = list(refs)
    exts = [refs.pop(0) for _ in range(4)]
    mine_ref, theirs_ref = refs[:2]
    outs = [refs[3 + i] for i in range(4)]
    place_scr = refs[7]
    own = expert_ref[0]
    turn = lax.broadcasted_iota(jnp.int32, (EXT, EXT), 1)
    experts = jnp.where(turn == 0, own, own ^ 1)
    wanted = jnp.where(expert_lanes(experts, (EXT, EXT), 0) & (turn < 2), 1.0, 0.0).astype(BF16)
    ext = jnp.concatenate([ref[:, ref.shape[1] - EXT :] for ref in exts], axis=0)
    chosen = jnp.dot(ext, wanted, preferred_element_type=F32) > 0
    first = lax.broadcasted_iota(jnp.int32, (PART, PART), 0)
    second = lax.broadcasted_iota(jnp.int32, (PART, PART), 1)
    earlier = jnp.where((first // 4 == second // 4) & (second < first), 1.0, 0.0).astype(BF16)
    rank = jnp.dot(earlier, jnp.where(chosen, 1.0, 0.0).astype(BF16), preferred_element_type=F32)
    token = lax.broadcasted_iota(jnp.int32, (PART, EXT), 0)
    place = jnp.where(chosen, token // 8 * 2 + rank.astype(jnp.int32), -1)
    column = lax.broadcasted_iota(jnp.int32, (PART, 2 * SEL), 1)
    hit = jnp.where(column < SEL, place[:, 0:1], place[:, 1:2]) == column % SEL
    is_left = lax.broadcasted_iota(jnp.int32, (PART, 2 * SEL), 0) % 8 < 4
    place_scr[:, : 2 * SEL] = jnp.where(hit & is_left, 1.0, 0.0).astype(BF16)
    place_scr[:, 2 * SEL :] = jnp.where(hit & ~is_left, 1.0, 0.0).astype(BF16)
    for n in range(0, HALF, 512):
        left, right = slice(n, n + 512), slice(HALF + n, HALF + n + 512)
        y = jnp.concatenate([mine_ref[:, left], theirs_ref[:, left], mine_ref[:, right], theirs_ref[:, right]], axis=0)
        value = jnp.dot(place_scr[...], y, preferred_element_type=F32).astype(BF16)
        for i in range(4):
            outs[i][:, left] = value[i * BLOCK : (i + 1) * BLOCK]


def spread(expert, blocks, mine, theirs, after):
    exts = [block[-1] for block in blocks]
    return pl.pallas_call(
        spread_kernel,
        out_shape=[jax.ShapeDtypeStruct((BLOCK, HALF), BF16)] * 4,
        in_specs=[SMEM] + [VMEM] * 6 + [ANY],
        out_specs=[VMEM] * 4,
        scratch_shapes=[pltpu.VMEM((PART, 4 * SEL), BF16)],
        compiler_params=SMALL,
        cost_estimate=BRIEF,
        name="spread",
    )(expert, *exts, mine, theirs, after)


def add(*terms):
    total = terms[0].astype(F32)
    for term in terms[1:]:
        total += term.astype(F32)
    return total.astype(BF16)


def finish_kernel(parts_ref, out_ref):
    total = parts_ref[0].astype(F32)
    for i in range(1, 8):
        total += parts_ref[i].astype(F32)
    out_ref[:, :HALF] = total[:4].astype(BF16)
    out_ref[:, HALF:] = total[4:].astype(BF16)


def finish(parts):
    return pl.pallas_call(
        finish_kernel,
        out_shape=jax.ShapeDtypeStruct((4, D), BF16),
        in_specs=[VMEM],
        out_specs=VMEM,
        compiler_params=SMALL,
        name="finish",
    )(parts)


def body(tokens, ids, weights, gate, up, down):
    expert = lax.axis_index("dev").astype(jnp.int32).reshape(1)
    own = swap_near(pack(expert, tokens, ids, weights)).reshape(BLOCK, WIDE)
    x, y, z = swap_far(own, 0), swap_far(own, 1), swap_far(own, 2)
    xy, yz, zx = swap_far(y, 0), swap_far(z, 1), swap_far(x, 2)
    near = ((x,), (y,), (z,), (own,))
    up = load(up, own)
    mine_near, sent = select(expert, near, up)
    xy, yz, zx, sent = lax.optimization_barrier((xy, yz, zx, sent))
    got_near = to_sibling(sent)
    far = ((xy,), (zx,), (yz,), (swap_far(yz[:, :CUT], 0), swap_far(xy[:, CUT:], 2)))
    hidden_near = hidden_units(expert, mine_near, got_near, gate, up, own)
    mine_far, sent = select(expert, far, hidden_near)
    got_far = to_sibling(sent)
    theirs = down_rows(1, hidden_near, down, mine_far)
    returned_near = to_sibling(theirs)
    result_near = down_rows(0, hidden_near, down, theirs)
    hidden_far = hidden_units(expert, mine_far, got_far, gate, up, result_near)
    theirs = down_rows(1, hidden_far, down, own)
    returned = to_sibling(theirs)
    result = down_rows(0, hidden_far, down, theirs)
    y_xy, y_zx, y_yz, y_xyz = spread(expert, far, result, returned, own)
    at_yz = swap_far(y_xyz, 0)
    at_y, at_x = swap_far(y_xy, 0), swap_far(y_zx, 2)
    y_x, y_y, y_z, y_own = spread(expert, near, result_near, returned_near, y_xyz)
    at_z = swap_far(add(y_yz, at_yz), 1)
    total = add(
        y_own,
        swap_far(add(y_x, at_x), 0),
        swap_far(add(y_y, at_y), 1),
        swap_far(add(y_z, at_z), 2),
    )
    return finish(swap_near(total.reshape(8, 8, HALF)))


def solution(mesh):
    in_specs = (
        P(AXES, None),
        P(AXES, None),
        P(AXES, None),
        P("dev", None, "grp"),
        P("dev", None, "grp"),
        P("dev", "grp", None),
    )
    return jax.shard_map(body, mesh=mesh, in_specs=in_specs, out_specs=P(AXES, None), check_vma=False)
```

```python
import functools

import jax
import jax.numpy as jnp
from jax import lax
from jax.experimental import pallas as pl
from jax.experimental.pallas import tpu as pltpu
from jax.sharding import PartitionSpec as P

AXES = ("grp", "dev")
D = 7168
HALF = D // 2
EXT = 128
WIDE = HALF + EXT
BLOCK = 64
PART = 4 * BLOCK
SEL = 64
F32 = jnp.float32
BF16 = jnp.bfloat16
MIB = 1 << 20
VMEM = pl.BlockSpec(memory_space=pltpu.VMEM)
SMEM = pl.BlockSpec(memory_space=pltpu.SMEM)
HBM = pl.BlockSpec(memory_space=pltpu.HBM)
ANY = pl.BlockSpec(memory_space=pl.ANY)
SMALL = pltpu.CompilerParams(vmem_limit_bytes=8 * MIB)


DEPTH = 1792
MIDDLE = D // 2
BRIEF = pl.CostEstimate(flops=1000, bytes_accessed=1000, transcendentals=0)


def flat(z, x, y, c):
    return ((z * 4 + x) * 4 + y) * 2 + c


def near_groups():
    seen, groups = set(), []
    for z in range(4):
        for x in range(4):
            for y in range(4):
                for c in range(2):
                    if flat(z, x, y, c) in seen:
                        continue
                    m = 3 if c else 1
                    members = [
                        flat(z ^ (m * i), x ^ (m * j), y ^ (m * k), c)
                        for i in (0, 1) for j in (0, 1) for k in (0, 1)
                    ]
                    seen.update(members)
                    groups.append(members)
    return groups


def far_pairs(*axes):
    pairs = []
    for z in range(4):
        for x in range(4):
            for y in range(4):
                for c in range(2):
                    at = [z, x, y]
                    for axis in axes:
                        at[axis] ^= 1 if c else 3
                    pairs.append((flat(z, x, y, c), flat(*at, c)))
    return pairs


NEAR = near_groups()
FAR = [far_pairs(0), far_pairs(1), far_pairs(2), far_pairs(0, 1, 2)]


def swap_near(values):
    return lax.all_to_all(values, AXES, 0, 0, axis_index_groups=NEAR, tiled=True)


def swap_far(values, axis):
    return lax.ppermute(values, AXES, FAR[axis])


def to_sibling(values):
    return lax.ppermute(values, "dev", [(i, i ^ 1) for i in range(32)])


def pack_kernel(expert_ref, tokens_hbm, ids_hbm, weights_hbm, out_ref, tokens_ref, ids_ref, weights_ref, sems):
    del expert_ref
    pairs = ((tokens_hbm, tokens_ref), (ids_hbm, ids_ref), (weights_hbm, weights_ref))
    copies = [pltpu.make_async_copy(source, target, sems.at[i]) for i, (source, target) in enumerate(pairs)]
    for copy in copies:
        copy.start()
    for copy in copies:
        copy.wait()
    lane = lax.broadcasted_iota(jnp.int32, (4, EXT), 1)
    dense = jnp.zeros((4, EXT), F32)
    for k in range(8):
        dense += jnp.where(ids_ref[:, k : k + 1] == lane % 32, weights_ref[:, k : k + 1], 0.0)
    high = dense.astype(BF16).astype(F32)
    route = jnp.where(lane < 32, high, jnp.where(lane < 64, dense - high, 0.0))
    rows = tokens_ref[...].astype(F32)
    left = jnp.concatenate([rows[:, :HALF], route], axis=1)
    right = jnp.concatenate([rows[:, HALF:], route], axis=1)
    block = jnp.concatenate([left, right], axis=0).astype(BF16)
    for i in range(8):
        out_ref[i] = block


def in_hbm(values):
    return pltpu.with_memory_space_constraint(values, pltpu.HBM)


def pack(expert, tokens, ids, weights):
    return pl.pallas_call(
        pack_kernel,
        out_shape=jax.ShapeDtypeStruct((8, 8, WIDE), BF16),
        in_specs=[SMEM, HBM, HBM, HBM],
        out_specs=VMEM,
        scratch_shapes=[
            pltpu.VMEM((4, D), BF16),
            pltpu.VMEM((4, 8), jnp.int32),
            pltpu.VMEM((4, 8), F32),
            pltpu.SemaphoreType.DMA((3,)),
        ],
        compiler_params=pltpu.CompilerParams(vmem_limit_bytes=4 * MIB),
        name="pack",
    )(expert, in_hbm(tokens), in_hbm(ids), in_hbm(weights))


def expert_lanes(expert, shape, dim):
    lane = lax.broadcasted_iota(jnp.int32, shape, dim)
    return (lane < 64) & (lane % 32 == expert)


def select_kernel(loads, expert_ref, *refs):
    refs = list(refs)
    blocks = [refs.pop(0) for _ in range(4)]
    sources = [refs.pop(0) for _ in range(loads)]
    del refs[0]
    mine_ref, sent_ref = refs[:2]
    targets = refs[2 : 2 + loads]
    pick, sem = refs[2 + loads :]
    copies = [pltpu.make_async_copy(a.at[:, :MIDDLE, :], b, sem) for a, b in zip(sources, targets)]
    for copy in copies:
        copy.start()
    own = expert_ref[0]
    turn = lax.broadcasted_iota(jnp.int32, (8, EXT), 0)
    experts = jnp.where(turn == 0, own, own ^ 1)
    wanted = jnp.where(expert_lanes(experts, (8, EXT), 1) & (turn < 2), 1.0, 0.0).astype(BF16)
    ext = jnp.concatenate([ref[:, HALF:] for ref in blocks], axis=0)
    route = lax.dot_general(wanted, ext, (((1,), (1,)), ((), ())), preferred_element_type=F32)
    chosen = route > 0
    first = lax.broadcasted_iota(jnp.int32, (PART, PART), 0)
    second = lax.broadcasted_iota(jnp.int32, (PART, PART), 1)
    earlier = jnp.where((first // 4 == second // 4) & (first < second), 1.0, 0.0).astype(BF16)
    rank = jnp.dot(jnp.where(chosen, 1.0, 0.0).astype(BF16), earlier, preferred_element_type=F32)
    column = lax.broadcasted_iota(jnp.int32, (8, PART), 1)
    place = jnp.where(chosen, column // 8 * 2 + rank.astype(jnp.int32), -1)
    row = lax.broadcasted_iota(jnp.int32, (SEL, PART), 0)
    is_left = lax.broadcasted_iota(jnp.int32, (SEL, PART), 1) % 8 < 4
    for e in range(2):
        hit = place[e : e + 1, :] == row
        pick[e * SEL : (e + 1) * SEL, :] = jnp.where(hit & is_left, 1.0, 0.0).astype(BF16)
        pick[(2 + e) * SEL : (3 + e) * SEL, :] = jnp.where(hit & ~is_left, 1.0, 0.0).astype(BF16)
    for n in range(0, HALF, 512):
        x = jnp.concatenate([ref[:, n : n + 512] for ref in blocks], axis=0)
        value = jnp.dot(pick[...], x, preferred_element_type=F32).astype(BF16)
        mine_ref[:, n : n + 512] = value[:SEL]
        sent_ref[:, n : n + 512] = value[SEL : 2 * SEL]
        mine_ref[:, HALF + n : HALF + n + 512] = value[2 * SEL : 3 * SEL]
        sent_ref[:, HALF + n : HALF + n + 512] = value[3 * SEL :]
    value = jnp.dot(pick[: 2 * SEL, :], ext, preferred_element_type=F32).astype(BF16)
    mine_ref[:, D:] = value[:SEL]
    sent_ref[:, D:] = value[SEL:]
    for copy in copies:
        copy.wait()


def select(expert, blocks, after, loads=()):
    return pl.pallas_call(
        functools.partial(select_kernel, len(loads)),
        out_shape=[jax.ShapeDtypeStruct((SEL, D + EXT), BF16)] * 2
        + [jax.ShapeDtypeStruct((1, MIDDLE, 512), BF16) for _ in loads],
        in_specs=[SMEM] + [VMEM] * 4 + [HBM] * len(loads) + [ANY],
        out_specs=[VMEM] * (2 + len(loads)),
        scratch_shapes=[pltpu.VMEM((PART, PART), BF16), pltpu.SemaphoreType.DMA],
        compiler_params=SMALL,
        cost_estimate=BRIEF,
        name="select",
    )(expert, *blocks, *[in_hbm(load) for load in loads], after)


def hidden_kernel(streams, expert_ref, mine_ref, theirs_ref, gate_ref, first_ref, rest_ref, after_ref, *refs):
    del after_ref
    if streams:
        hidden, second_ref, gate_sum, up_sum, sem = refs
        copy = pltpu.make_async_copy(rest_ref.at[:, MIDDLE:, :], second_ref, sem)
        copy.start()
    else:
        hidden, gate_sum, up_sum = refs
        second_ref = rest_ref

    def rows(block):
        return jnp.concatenate([mine_ref[:, block], theirs_ref[:, block]], axis=0)

    for i in range(0, D, DEPTH):
        block = slice(i, i + DEPTH)
        gate = jnp.dot(rows(block), gate_ref[0, block, :], preferred_element_type=F32)
        gate_sum[...] = gate if i == 0 else gate_sum[...] + gate
    for i in range(0, D, DEPTH):
        if streams and i == MIDDLE:
            copy.wait()
        ref, start = (first_ref, i) if i < MIDDLE else (second_ref, i - MIDDLE)
        up = jnp.dot(rows(slice(i, i + DEPTH)), ref[0, start : start + DEPTH, :], preferred_element_type=F32)
        up_sum[...] = up if i == 0 else up_sum[...] + up
    lanes = expert_lanes(expert_ref[0], (2 * SEL, EXT), 1)
    scale = jnp.sum(jnp.where(lanes, rows(slice(D, D + EXT)).astype(F32), 0.0), axis=1, keepdims=True)
    v = gate_sum[...]
    hidden[...] = (v / (1.0 + jnp.exp(-v)) * up_sum[...] * scale).astype(BF16)


def hidden_units(expert, mine, theirs, gate, first, rest, after, streams):
    half = jax.ShapeDtypeStruct((1, MIDDLE, 512), BF16)
    return pl.pallas_call(
        functools.partial(hidden_kernel, streams),
        out_shape=[jax.ShapeDtypeStruct((2 * SEL, 512), BF16)] + [half] * streams,
        in_specs=[SMEM, VMEM, VMEM, VMEM, VMEM, HBM if streams else VMEM, ANY],
        out_specs=[VMEM] * (1 + streams),
        scratch_shapes=[pltpu.VMEM((2 * SEL, 512), F32)] * 2 + [pltpu.SemaphoreType.DMA] * streams,
        compiler_params=SMALL,
        cost_estimate=BRIEF,
        name="hidden",
    )(expert, mine, theirs, gate, first, in_hbm(rest) if streams else rest, after)


def down_kernel(hidden_ref, down_ref, after_ref, mine_ref, theirs_ref):
    del after_ref
    for n in range(0, D, 1024):
        block = slice(n, n + 1024)
        value = jnp.dot(hidden_ref[...], down_ref[0, :, block], preferred_element_type=F32).astype(BF16)
        mine_ref[:, block] = value[:SEL]
        theirs_ref[:, block] = value[SEL:]


def down_rows(hidden, down, after):
    return pl.pallas_call(
        down_kernel,
        out_shape=[jax.ShapeDtypeStruct((SEL, D), BF16)] * 2,
        in_specs=[VMEM, VMEM, ANY],
        out_specs=[VMEM, VMEM],
        compiler_params=SMALL,
        cost_estimate=BRIEF,
        name="down",
    )(hidden, down, after)


def spread_kernel(expert_ref, *refs):
    refs = list(refs)
    exts = [refs.pop(0) for _ in range(4)]
    mine_ref, theirs_ref = refs[:2]
    outs = [refs[3 + i] for i in range(4)]
    place_scr = refs[7]
    own = expert_ref[0]
    turn = lax.broadcasted_iota(jnp.int32, (EXT, EXT), 1)
    experts = jnp.where(turn == 0, own, own ^ 1)
    wanted = jnp.where(expert_lanes(experts, (EXT, EXT), 0) & (turn < 2), 1.0, 0.0).astype(BF16)
    ext = jnp.concatenate([ref[:, HALF:] for ref in exts], axis=0)
    chosen = jnp.dot(ext, wanted, preferred_element_type=F32) > 0
    first = lax.broadcasted_iota(jnp.int32, (PART, PART), 0)
    second = lax.broadcasted_iota(jnp.int32, (PART, PART), 1)
    earlier = jnp.where((first // 4 == second // 4) & (second < first), 1.0, 0.0).astype(BF16)
    rank = jnp.dot(earlier, jnp.where(chosen, 1.0, 0.0).astype(BF16), preferred_element_type=F32)
    token = lax.broadcasted_iota(jnp.int32, (PART, EXT), 0)
    place = jnp.where(chosen, token // 8 * 2 + rank.astype(jnp.int32), -1)
    column = lax.broadcasted_iota(jnp.int32, (PART, 2 * SEL), 1)
    hit = jnp.where(column < SEL, place[:, 0:1], place[:, 1:2]) == column % SEL
    is_left = lax.broadcasted_iota(jnp.int32, (PART, 2 * SEL), 0) % 8 < 4
    place_scr[:, : 2 * SEL] = jnp.where(hit & is_left, 1.0, 0.0).astype(BF16)
    place_scr[:, 2 * SEL :] = jnp.where(hit & ~is_left, 1.0, 0.0).astype(BF16)
    for n in range(0, HALF, 512):
        left, right = slice(n, n + 512), slice(HALF + n, HALF + n + 512)
        y = jnp.concatenate([mine_ref[:, left], theirs_ref[:, left], mine_ref[:, right], theirs_ref[:, right]], axis=0)
        value = jnp.dot(place_scr[...], y, preferred_element_type=F32).astype(BF16)
        for i in range(4):
            outs[i][:, left] = value[i * BLOCK : (i + 1) * BLOCK]


def spread(expert, blocks, mine, theirs, after):
    return pl.pallas_call(
        spread_kernel,
        out_shape=[jax.ShapeDtypeStruct((BLOCK, HALF), BF16)] * 4,
        in_specs=[SMEM] + [VMEM] * 6 + [ANY],
        out_specs=[VMEM] * 4,
        scratch_shapes=[pltpu.VMEM((PART, 4 * SEL), BF16)],
        compiler_params=SMALL,
        cost_estimate=BRIEF,
        name="spread",
    )(expert, *blocks, mine, theirs, after)


def add(*terms):
    total = terms[0].astype(F32)
    for term in terms[1:]:
        total += term.astype(F32)
    return total.astype(BF16)


def finish_kernel(parts_ref, out_ref):
    total = parts_ref[0].astype(F32)
    for i in range(1, 8):
        total += parts_ref[i].astype(F32)
    out_ref[:, :HALF] = total[:4].astype(BF16)
    out_ref[:, HALF:] = total[4:].astype(BF16)


def finish(parts):
    return pl.pallas_call(
        finish_kernel,
        out_shape=jax.ShapeDtypeStruct((4, D), BF16),
        in_specs=[VMEM],
        out_specs=VMEM,
        compiler_params=SMALL,
        name="finish",
    )(parts)


def body(tokens, ids, weights, gate, up, down):
    expert = lax.axis_index("dev").astype(jnp.int32).reshape(1)
    own = swap_near(pack(expert, tokens, ids, weights)).reshape(BLOCK, WIDE)
    x, y, z = swap_far(own, 0), swap_far(own, 1), swap_far(own, 2)
    xyz = swap_far(own, 3)
    xy, yz, zx = swap_far(y, 0), swap_far(z, 1), swap_far(x, 2)
    near = (x, y, z, own)
    mine_near, sent, up_first = select(expert, near, own, (up,))
    xy, yz, zx, xyz, sent = lax.optimization_barrier((xy, yz, zx, xyz, sent))
    got_near = to_sibling(sent)
    far = (xy, zx, yz, xyz)
    mine_far, sent = select(expert, far, own)
    got_far = to_sibling(sent)
    hidden_near, up_second = hidden_units(expert, mine_near, got_near, gate, up_first, up, mine_far, 1)
    result_near, theirs = down_rows(hidden_near, down, own)
    returned_near = to_sibling(theirs)
    (hidden_far,) = hidden_units(expert, mine_far, got_far, gate, up_first, up_second, result_near, 0)
    result, theirs = down_rows(hidden_far, down, own)
    returned = to_sibling(theirs)
    y_x, y_y, y_z, y_own = spread(expert, near, result_near, returned_near, result)
    y_xy, y_zx, y_yz, y_xyz = spread(expert, far, result, returned, y_own)
    at_y, at_z, at_x = swap_far(y_xy, 0), swap_far(y_yz, 1), swap_far(y_zx, 2)
    at_own = swap_far(y_xyz, 3)
    total = add(
        y_own,
        swap_far(add(y_x, at_x), 0),
        swap_far(add(y_y, at_y), 1),
        swap_far(add(y_z, at_z), 2),
        at_own,
    )
    return finish(swap_near(total.reshape(8, 8, HALF)))


def solution(mesh):
    in_specs = (
        P(AXES, None),
        P(AXES, None),
        P(AXES, None),
        P("dev", None, "grp"),
        P("dev", None, "grp"),
        P("dev", "grp", None),
    )
    return jax.shard_map(body, mesh=mesh, in_specs=in_specs, out_specs=P(AXES, None), check_vma=False)
```

```python
import functools

import jax
import jax.numpy as jnp
from jax import lax
from jax.experimental import pallas as pl
from jax.experimental.pallas import tpu as pltpu
from jax.sharding import PartitionSpec as P

AXES = ("grp", "dev")
D = 7168
HALF = D // 2
EXT = 128
WIDE = HALF + EXT
BLOCK = 64
PART = 4 * BLOCK
SEL = 64
F32 = jnp.float32
BF16 = jnp.bfloat16
MIB = 1 << 20
VMEM = pl.BlockSpec(memory_space=pltpu.VMEM)
SMEM = pl.BlockSpec(memory_space=pltpu.SMEM)
HBM = pl.BlockSpec(memory_space=pltpu.HBM)
ANY = pl.BlockSpec(memory_space=pl.ANY)
SMALL = pltpu.CompilerParams(vmem_limit_bytes=8 * MIB)


MIDDLE = D // 2
CUTS = ((0, MIDDLE), (MIDDLE, D))
BRIEF = pl.CostEstimate(flops=1000, bytes_accessed=1000, transcendentals=0)


def flat(z, x, y, c):
    return ((z * 4 + x) * 4 + y) * 2 + c


def near_groups():
    seen, groups = set(), []
    for z in range(4):
        for x in range(4):
            for y in range(4):
                for c in range(2):
                    if flat(z, x, y, c) in seen:
                        continue
                    m = 3 if c else 1
                    members = [
                        flat(z ^ (m * i), x ^ (m * j), y ^ (m * k), c)
                        for i in (0, 1) for j in (0, 1) for k in (0, 1)
                    ]
                    seen.update(members)
                    groups.append(members)
    return groups


def far_pairs(*axes):
    pairs = []
    for z in range(4):
        for x in range(4):
            for y in range(4):
                for c in range(2):
                    at = [z, x, y]
                    for axis in axes:
                        at[axis] ^= 1 if c else 3
                    pairs.append((flat(z, x, y, c), flat(*at, c)))
    return pairs


NEAR = near_groups()
FAR = [far_pairs(0), far_pairs(1), far_pairs(2), far_pairs(0, 1, 2), far_pairs(0, 1)]


def swap_near(values):
    return lax.all_to_all(values, AXES, 0, 0, axis_index_groups=NEAR, tiled=True)


def swap_far(values, axis):
    return lax.ppermute(values, AXES, FAR[axis])


def both_cores(values):
    return lax.all_gather(values, "dev", axis_index_groups=[[i, i + 1] for i in range(0, 32, 2)])


def to_sibling(values):
    return lax.ppermute(values, "dev", [(i, i ^ 1) for i in range(32)])


def pack_kernel(expert_ref, tokens_hbm, ids_hbm, weights_hbm, out_ref, tokens_ref, ids_ref, weights_ref, sems):
    del expert_ref
    pairs = ((tokens_hbm, tokens_ref), (ids_hbm, ids_ref), (weights_hbm, weights_ref))
    copies = [pltpu.make_async_copy(source, target, sems.at[i]) for i, (source, target) in enumerate(pairs)]
    for copy in copies:
        copy.start()
    for copy in copies:
        copy.wait()
    lane = lax.broadcasted_iota(jnp.int32, (4, EXT), 1)
    dense = jnp.zeros((4, EXT), F32)
    for k in range(8):
        dense += jnp.where(ids_ref[:, k : k + 1] == lane % 32, weights_ref[:, k : k + 1], 0.0)
    high = dense.astype(BF16).astype(F32)
    route = jnp.where(lane < 32, high, jnp.where(lane < 64, dense - high, 0.0))
    rows = tokens_ref[...].astype(F32)
    left = jnp.concatenate([rows[:, :HALF], route], axis=1)
    right = jnp.concatenate([rows[:, HALF:], route], axis=1)
    block = jnp.concatenate([left, right], axis=0).astype(BF16)
    for i in range(8):
        out_ref[i] = block


def in_hbm(values):
    return pltpu.with_memory_space_constraint(values, pltpu.HBM)


def pack(expert, tokens, ids, weights):
    return pl.pallas_call(
        pack_kernel,
        out_shape=jax.ShapeDtypeStruct((8, 8, WIDE), BF16),
        in_specs=[SMEM, HBM, HBM, HBM],
        out_specs=VMEM,
        scratch_shapes=[
            pltpu.VMEM((4, D), BF16),
            pltpu.VMEM((4, 8), jnp.int32),
            pltpu.VMEM((4, 8), F32),
            pltpu.SemaphoreType.DMA((3,)),
        ],
        compiler_params=pltpu.CompilerParams(vmem_limit_bytes=4 * MIB),
        name="pack",
    )(expert, in_hbm(tokens), in_hbm(ids), in_hbm(weights))


def expert_lanes(expert, shape, dim):
    lane = lax.broadcasted_iota(jnp.int32, shape, dim)
    return (lane < 64) & (lane % 32 == expert)


def select_kernel(loads, expert_ref, *refs):
    refs = list(refs)
    blocks = [refs.pop(0) for _ in range(4)]
    sources = [refs.pop(0) for _ in range(loads)]
    del refs[0]
    mine_ref, sent_refs, targets = refs[0], refs[1:3], refs[3 : 3 + loads]
    pick, sem = refs[3 + loads :]
    copies = [pltpu.make_async_copy(a.at[:, :MIDDLE, :], b, sem) for a, b in zip(sources, targets)]
    for copy in copies:
        copy.start()
    own = expert_ref[0]
    turn = lax.broadcasted_iota(jnp.int32, (8, EXT), 0)
    experts = jnp.where(turn == 0, own, own ^ 1)
    wanted = jnp.where(expert_lanes(experts, (8, EXT), 1) & (turn < 2), 1.0, 0.0).astype(BF16)
    ext = jnp.concatenate([ref[:, HALF:] for ref in blocks], axis=0)
    route = lax.dot_general(wanted, ext, (((1,), (1,)), ((), ())), preferred_element_type=F32)
    chosen = route > 0
    first = lax.broadcasted_iota(jnp.int32, (PART, PART), 0)
    second = lax.broadcasted_iota(jnp.int32, (PART, PART), 1)
    earlier = jnp.where((first // 4 == second // 4) & (first < second), 1.0, 0.0).astype(BF16)
    rank = jnp.dot(jnp.where(chosen, 1.0, 0.0).astype(BF16), earlier, preferred_element_type=F32)
    column = lax.broadcasted_iota(jnp.int32, (8, PART), 1)
    place = jnp.where(chosen, column // 8 * 2 + rank.astype(jnp.int32), -1)
    row = lax.broadcasted_iota(jnp.int32, (SEL, PART), 0)
    is_left = lax.broadcasted_iota(jnp.int32, (SEL, PART), 1) % 8 < 4
    for e in range(2):
        hit = place[e : e + 1, :] == row
        pick[e * SEL : (e + 1) * SEL, :] = jnp.where(hit & is_left, 1.0, 0.0).astype(BF16)
        pick[(2 + e) * SEL : (3 + e) * SEL, :] = jnp.where(hit & ~is_left, 1.0, 0.0).astype(BF16)

    for n in range(0, HALF, 512):
        x = jnp.concatenate([ref[:, n : n + 512] for ref in blocks], axis=0)
        value = jnp.dot(pick[...], x, preferred_element_type=F32).astype(BF16)
        mine_ref[:, n : n + 512] = value[:SEL]
        sent_refs[0][:, n : n + 512] = value[SEL : 2 * SEL]
        mine_ref[:, HALF + n : HALF + n + 512] = value[2 * SEL : 3 * SEL]
        sent_refs[1][:, n : n + 512] = value[3 * SEL :]
    value = jnp.dot(pick[: 2 * SEL, :], ext, preferred_element_type=F32).astype(BF16)
    mine_ref[:, D:] = value[:SEL]
    sent_refs[1][:, HALF:] = value[SEL:]
    for copy in copies:
        copy.wait()


def select(expert, blocks, after, loads=()):
    return pl.pallas_call(
        functools.partial(select_kernel, len(loads)),
        out_shape=[jax.ShapeDtypeStruct((SEL, D + EXT), BF16)]
        + [jax.ShapeDtypeStruct((SEL, high - low + EXT * (high == D)), BF16) for low, high in CUTS]
        + [jax.ShapeDtypeStruct((1, MIDDLE, 512), BF16) for _ in loads],
        in_specs=[SMEM] + [VMEM] * 4 + [HBM] * len(loads) + [ANY],
        out_specs=[VMEM] * (3 + len(loads)),
        scratch_shapes=[pltpu.VMEM((PART, PART), BF16), pltpu.SemaphoreType.DMA],
        compiler_params=SMALL,
        cost_estimate=BRIEF,
        name="select",
    )(expert, *blocks, *[in_hbm(load) for load in loads], after)


def hidden_kernel(streams, expert_ref, mine_ref, a_ref, b_ref, gate_ref, first_ref, rest_ref, after_ref, *refs):
    del after_ref
    if streams:
        hidden, second_ref, gate_sum, up_sum, sem = refs
        copy = pltpu.make_async_copy(rest_ref.at[:, MIDDLE:, :], second_ref, sem)
        copy.start()
    else:
        hidden, gate_sum, up_sum = refs
        second_ref = rest_ref

    def rows(piece, low, high):
        start = CUTS[piece][0]
        theirs_ref, block = (a_ref, b_ref)[piece], slice(low - start, high - start)
        theirs = theirs_ref[1 - expert_ref[0] % 2, :, block] if streams else theirs_ref[:, block]
        return jnp.concatenate([mine_ref[:, low:high], theirs], axis=0)

    for piece, (low, high) in enumerate(CUTS):
        gate = jnp.dot(rows(piece, low, high), gate_ref[0, low:high, :], preferred_element_type=F32)
        gate_sum[...] = gate if low == 0 else gate_sum[...] + gate
    for piece, (low, high) in enumerate(CUTS):
        if streams and low == MIDDLE:
            copy.wait()
        ref, start = (first_ref, 0) if low < MIDDLE else (second_ref, MIDDLE)
        up = jnp.dot(rows(piece, low, high), ref[0, low - start : high - start, :], preferred_element_type=F32)
        up_sum[...] = up if low == 0 else up_sum[...] + up
    lanes = expert_lanes(expert_ref[0], (2 * SEL, EXT), 1)
    scale = jnp.sum(jnp.where(lanes, rows(1, D, D + EXT).astype(F32), 0.0), axis=1, keepdims=True)
    v = gate_sum[...]
    hidden[...] = (v / (1.0 + jnp.exp(-v)) * up_sum[...] * scale).astype(BF16)


def hidden_units(expert, mine, theirs, gate, first, rest, after, streams):
    second = jax.ShapeDtypeStruct((1, D - MIDDLE, 512), BF16)
    return pl.pallas_call(
        functools.partial(hidden_kernel, streams),
        out_shape=[jax.ShapeDtypeStruct((2 * SEL, 512), BF16)] + [second] * streams,
        in_specs=[SMEM] + [VMEM] * 5 + [HBM if streams else VMEM, ANY],
        out_specs=[VMEM] * (1 + streams),
        scratch_shapes=[pltpu.VMEM((2 * SEL, 512), F32)] * 2 + [pltpu.SemaphoreType.DMA] * streams,
        compiler_params=SMALL,
        cost_estimate=BRIEF,
        name="hidden",
    )(expert, mine, *theirs, gate, first, in_hbm(rest) if streams else rest, after)


def down_kernel(hidden_ref, down_ref, after_ref, mine_ref, theirs_ref):
    del after_ref
    for n in range(0, D, 1024):
        block = slice(n, n + 1024)
        value = jnp.dot(hidden_ref[...], down_ref[0, :, block], preferred_element_type=F32).astype(BF16)
        mine_ref[:, block] = value[:SEL]
        theirs_ref[:, block] = value[SEL:]


def down_rows(hidden, down, after):
    return pl.pallas_call(
        down_kernel,
        out_shape=[jax.ShapeDtypeStruct((SEL, D), BF16)] * 2,
        in_specs=[VMEM, VMEM, ANY],
        out_specs=[VMEM, VMEM],
        compiler_params=SMALL,
        cost_estimate=BRIEF,
        name="down",
    )(hidden, down, after)


def spread_kernel(expert_ref, *refs):
    refs = list(refs)
    exts = [refs.pop(0) for _ in range(4)]
    mine_ref, theirs_ref = refs[:2]
    outs = [refs[3 + i] for i in range(4)]
    place_scr = refs[7]
    own = expert_ref[0]
    turn = lax.broadcasted_iota(jnp.int32, (EXT, EXT), 1)
    experts = jnp.where(turn == 0, own, own ^ 1)
    wanted = jnp.where(expert_lanes(experts, (EXT, EXT), 0) & (turn < 2), 1.0, 0.0).astype(BF16)
    ext = jnp.concatenate([ref[:, HALF:] for ref in exts], axis=0)
    chosen = jnp.dot(ext, wanted, preferred_element_type=F32) > 0
    first = lax.broadcasted_iota(jnp.int32, (PART, PART), 0)
    second = lax.broadcasted_iota(jnp.int32, (PART, PART), 1)
    earlier = jnp.where((first // 4 == second // 4) & (second < first), 1.0, 0.0).astype(BF16)
    rank = jnp.dot(earlier, jnp.where(chosen, 1.0, 0.0).astype(BF16), preferred_element_type=F32)
    token = lax.broadcasted_iota(jnp.int32, (PART, EXT), 0)
    place = jnp.where(chosen, token // 8 * 2 + rank.astype(jnp.int32), -1)
    column = lax.broadcasted_iota(jnp.int32, (PART, 2 * SEL), 1)
    hit = jnp.where(column < SEL, place[:, 0:1], place[:, 1:2]) == column % SEL
    is_left = lax.broadcasted_iota(jnp.int32, (PART, 2 * SEL), 0) % 8 < 4
    place_scr[:, : 2 * SEL] = jnp.where(hit & is_left, 1.0, 0.0).astype(BF16)
    place_scr[:, 2 * SEL :] = jnp.where(hit & ~is_left, 1.0, 0.0).astype(BF16)
    for n in range(0, HALF, 512):
        left, right = slice(n, n + 512), slice(HALF + n, HALF + n + 512)
        y = jnp.concatenate([mine_ref[:, left], theirs_ref[:, left], mine_ref[:, right], theirs_ref[:, right]], axis=0)
        value = jnp.dot(place_scr[...], y, preferred_element_type=F32).astype(BF16)
        for i in range(4):
            outs[i][:, left] = value[i * BLOCK : (i + 1) * BLOCK]


def spread(expert, blocks, mine, theirs, after):
    return pl.pallas_call(
        spread_kernel,
        out_shape=[jax.ShapeDtypeStruct((BLOCK, HALF), BF16)] * 4,
        in_specs=[SMEM] + [VMEM] * 6 + [ANY],
        out_specs=[VMEM] * 4,
        scratch_shapes=[pltpu.VMEM((PART, 4 * SEL), BF16)],
        compiler_params=SMALL,
        cost_estimate=BRIEF,
        name="spread",
    )(expert, *blocks, mine, theirs, after)


def add(*terms):
    total = terms[0].astype(F32)
    for term in terms[1:]:
        total += term.astype(F32)
    return total.astype(BF16)


def finish_kernel(parts_ref, out_ref):
    total = parts_ref[0].astype(F32)
    for i in range(1, 8):
        total += parts_ref[i].astype(F32)
    out_ref[:, :HALF] = total[:4].astype(BF16)
    out_ref[:, HALF:] = total[4:].astype(BF16)


def finish(parts):
    return pl.pallas_call(
        finish_kernel,
        out_shape=jax.ShapeDtypeStruct((4, D), BF16),
        in_specs=[VMEM],
        out_specs=VMEM,
        compiler_params=SMALL,
        name="finish",
    )(parts)


def body(tokens, ids, weights, gate, up, down):
    expert = lax.axis_index("dev").astype(jnp.int32).reshape(1)
    own = swap_near(pack(expert, tokens, ids, weights)).reshape(BLOCK, WIDE)
    x, y, z = swap_far(own, 0), swap_far(own, 1), swap_far(own, 2)
    xy, yz, zx = swap_far(y, 0), swap_far(z, 1), swap_far(x, 2)
    xyz = swap_far(z, 4)
    near = (x, y, z, own)
    mine_near, *sent, up_first = select(expert, near, own, (up,))
    got_near = [both_cores(piece) for piece in sent]
    hidden_near, up_second = hidden_units(expert, mine_near, got_near, gate, up_first, up, own, 1)
    result_near, theirs = down_rows(hidden_near, down, own)
    xy, yz, zx, xyz, theirs = lax.optimization_barrier((xy, yz, zx, xyz, theirs))
    far = (xy, zx, yz, xyz)
    returned_near = to_sibling(theirs)
    mine_far, *sent = select(expert, far, result_near)
    got_far = [to_sibling(piece) for piece in sent]
    y_x, y_y, y_z, y_own = spread(expert, near, result_near, returned_near, mine_far)
    (hidden_far,) = hidden_units(expert, mine_far, got_far, gate, up_first, up_second, y_own, 0)
    result, theirs = down_rows(hidden_far, down, own)
    returned = to_sibling(theirs)
    y_xy, y_zx, y_yz, y_xyz = spread(expert, far, result, returned, own)
    at_y, at_z, at_x = swap_far(y_xy, 0), swap_far(y_yz, 1), swap_far(y_zx, 2)
    at_own = swap_far(y_xyz, 3)
    total = add(
        y_own,
        swap_far(add(y_x, at_x), 0),
        swap_far(add(y_y, at_y), 1),
        swap_far(add(y_z, at_z), 2),
        at_own,
    )
    return finish(swap_near(total.reshape(8, 8, HALF)))


def solution(mesh):
    in_specs = (
        P(AXES, None),
        P(AXES, None),
        P(AXES, None),
        P("dev", None, "grp"),
        P("dev", None, "grp"),
        P("dev", "grp", None),
    )
    return jax.shard_map(body, mesh=mesh, in_specs=in_specs, out_specs=P(AXES, None), check_vma=False)
```

```python
import functools

import jax
import jax.numpy as jnp
from jax import lax
from jax.experimental import pallas as pl
from jax.experimental.pallas import tpu as pltpu
from jax.sharding import PartitionSpec as P

AXES = ("grp", "dev")
D = 7168
HALF = D // 2
EXT = 128
WIDE = HALF + EXT
BLOCK = 64
PART = 4 * BLOCK
SEL = 64
F32 = jnp.float32
BF16 = jnp.bfloat16
MIB = 1 << 20
VMEM = pl.BlockSpec(memory_space=pltpu.VMEM)
SMEM = pl.BlockSpec(memory_space=pltpu.SMEM)
HBM = pl.BlockSpec(memory_space=pltpu.HBM)
ANY = pl.BlockSpec(memory_space=pl.ANY)
SMALL = pltpu.CompilerParams(vmem_limit_bytes=8 * MIB)


MIDDLE = D // 2
CUTS = ((0, MIDDLE), (MIDDLE, D))
BRIEF = pl.CostEstimate(flops=1000, bytes_accessed=1000, transcendentals=0)


def flat(z, x, y, c):
    return ((z * 4 + x) * 4 + y) * 2 + c


def near_groups():
    seen, groups = set(), []
    for z in range(4):
        for x in range(4):
            for y in range(4):
                for c in range(2):
                    if flat(z, x, y, c) in seen:
                        continue
                    m = 3 if c else 1
                    members = [
                        flat(z ^ (m * i), x ^ (m * j), y ^ (m * k), c)
                        for i in (0, 1) for j in (0, 1) for k in (0, 1)
                    ]
                    seen.update(members)
                    groups.append(members)
    return groups


def far_pairs(*axes):
    pairs = []
    for z in range(4):
        for x in range(4):
            for y in range(4):
                for c in range(2):
                    at = [z, x, y]
                    for axis in axes:
                        at[axis] ^= 1 if c else 3
                    pairs.append((flat(z, x, y, c), flat(*at, c)))
    return pairs


NEAR = near_groups()
FAR = [far_pairs(0), far_pairs(1), far_pairs(2), far_pairs(0, 1, 2), far_pairs(0, 1)]


def swap_near(values):
    return lax.all_to_all(values, AXES, 0, 0, axis_index_groups=NEAR, tiled=True)


def swap_far(values, axis):
    return lax.ppermute(values, AXES, FAR[axis])


def swap_cores(values):
    return lax.all_to_all(values, "dev", 0, 0, axis_index_groups=[[i, i + 1] for i in range(0, 32, 2)], tiled=True)


def to_sibling(values):
    return lax.ppermute(values, "dev", [(i, i ^ 1) for i in range(32)])


def pack_kernel(expert_ref, tokens_hbm, ids_hbm, weights_hbm, out_ref, tokens_ref, ids_ref, weights_ref, sems):
    del expert_ref
    pairs = ((tokens_hbm, tokens_ref), (ids_hbm, ids_ref), (weights_hbm, weights_ref))
    copies = [pltpu.make_async_copy(source, target, sems.at[i]) for i, (source, target) in enumerate(pairs)]
    for copy in copies:
        copy.start()
    for copy in copies:
        copy.wait()
    lane = lax.broadcasted_iota(jnp.int32, (4, EXT), 1)
    dense = jnp.zeros((4, EXT), F32)
    for k in range(8):
        dense += jnp.where(ids_ref[:, k : k + 1] == lane % 32, weights_ref[:, k : k + 1], 0.0)
    high = dense.astype(BF16).astype(F32)
    route = jnp.where(lane < 32, high, jnp.where(lane < 64, dense - high, 0.0))
    rows = tokens_ref[...].astype(F32)
    left = jnp.concatenate([rows[:, :HALF], route], axis=1)
    right = jnp.concatenate([rows[:, HALF:], route], axis=1)
    block = jnp.concatenate([left, right], axis=0).astype(BF16)
    for i in range(8):
        out_ref[i] = block


def in_hbm(values):
    return pltpu.with_memory_space_constraint(values, pltpu.HBM)


def pack(expert, tokens, ids, weights):
    return pl.pallas_call(
        pack_kernel,
        out_shape=jax.ShapeDtypeStruct((8, 8, WIDE), BF16),
        in_specs=[SMEM, HBM, HBM, HBM],
        out_specs=VMEM,
        scratch_shapes=[
            pltpu.VMEM((4, D), BF16),
            pltpu.VMEM((4, 8), jnp.int32),
            pltpu.VMEM((4, 8), F32),
            pltpu.SemaphoreType.DMA((3,)),
        ],
        compiler_params=pltpu.CompilerParams(vmem_limit_bytes=4 * MIB),
        name="pack",
    )(expert, in_hbm(tokens), in_hbm(ids), in_hbm(weights))


def expert_lanes(expert, shape, dim):
    lane = lax.broadcasted_iota(jnp.int32, shape, dim)
    return (lane < 64) & (lane % 32 == expert)


def select_kernel(loads, expert_ref, *refs):
    refs = list(refs)
    blocks = [refs.pop(0) for _ in range(4)]
    sources = [refs.pop(0) for _ in range(loads)]
    del refs[0]
    pick, sem = refs[-2:]
    if loads:
        core = expert_ref[0] % 2
        mine_ref, left_ref, right_ref = refs[0].at[core], refs[0].at[1 - core, :, :HALF], refs[0].at[1 - core, :, HALF:]
    else:
        mine_ref, left_ref, right_ref = refs[:3]
    copies = [pltpu.make_async_copy(a.at[:, :MIDDLE, :], b, sem) for a, b in zip(sources, refs[1 : 1 + loads])]
    for copy in copies:
        copy.start()
    own = expert_ref[0]
    turn = lax.broadcasted_iota(jnp.int32, (8, EXT), 0)
    experts = jnp.where(turn == 0, own, own ^ 1)
    wanted = jnp.where(expert_lanes(experts, (8, EXT), 1) & (turn < 2), 1.0, 0.0).astype(BF16)
    ext = jnp.concatenate([ref[:, HALF:] for ref in blocks], axis=0)
    route = lax.dot_general(wanted, ext, (((1,), (1,)), ((), ())), preferred_element_type=F32)
    chosen = route > 0
    first = lax.broadcasted_iota(jnp.int32, (PART, PART), 0)
    second = lax.broadcasted_iota(jnp.int32, (PART, PART), 1)
    earlier = jnp.where((first // 4 == second // 4) & (first < second), 1.0, 0.0).astype(BF16)
    rank = jnp.dot(jnp.where(chosen, 1.0, 0.0).astype(BF16), earlier, preferred_element_type=F32)
    column = lax.broadcasted_iota(jnp.int32, (8, PART), 1)
    place = jnp.where(chosen, column // 8 * 2 + rank.astype(jnp.int32), -1)
    row = lax.broadcasted_iota(jnp.int32, (SEL, PART), 0)
    is_left = lax.broadcasted_iota(jnp.int32, (SEL, PART), 1) % 8 < 4
    for e in range(2):
        hit = place[e : e + 1, :] == row
        pick[e * SEL : (e + 1) * SEL, :] = jnp.where(hit & is_left, 1.0, 0.0).astype(BF16)
        pick[(2 + e) * SEL : (3 + e) * SEL, :] = jnp.where(hit & ~is_left, 1.0, 0.0).astype(BF16)

    for n in range(0, HALF, 512):
        x = jnp.concatenate([ref[:, n : n + 512] for ref in blocks], axis=0)
        value = jnp.dot(pick[...], x, preferred_element_type=F32).astype(BF16)
        mine_ref[:, n : n + 512] = value[:SEL]
        left_ref[:, n : n + 512] = value[SEL : 2 * SEL]
        mine_ref[:, HALF + n : HALF + n + 512] = value[2 * SEL : 3 * SEL]
        right_ref[:, n : n + 512] = value[3 * SEL :]
    value = jnp.dot(pick[: 2 * SEL, :], ext, preferred_element_type=F32).astype(BF16)
    mine_ref[:, D:] = value[:SEL]
    right_ref[:, HALF:] = value[SEL:]
    for copy in copies:
        copy.wait()


def select(expert, blocks, after, loads=()):
    if loads:
        shapes = [(2, SEL, D + EXT)] + [(1, MIDDLE, 512) for _ in loads]
    else:
        shapes = [(SEL, D + EXT), (SEL, HALF), (SEL, HALF + EXT)]
    return pl.pallas_call(
        functools.partial(select_kernel, len(loads)),
        out_shape=[jax.ShapeDtypeStruct(shape, BF16) for shape in shapes],
        in_specs=[SMEM] + [VMEM] * 4 + [HBM] * len(loads) + [ANY],
        out_specs=[VMEM] * len(shapes),
        scratch_shapes=[pltpu.VMEM((PART, PART), BF16), pltpu.SemaphoreType.DMA],
        compiler_params=SMALL,
        cost_estimate=BRIEF,
        name="select",
    )(expert, *blocks, *[in_hbm(load) for load in loads], after)


def hidden_kernel(streams, expert_ref, *refs):
    refs = list(refs)
    row_refs = [refs.pop(0) for _ in range(1 if streams else 3)]
    gate_ref, first_ref, rest_ref = refs[:3]
    if streams:
        hidden, second_ref, gate_sum, up_sum, sem = refs[4:]
        copy = pltpu.make_async_copy(rest_ref.at[:, MIDDLE:, :], second_ref, sem)
        copy.start()
    else:
        hidden, gate_sum, up_sum = refs[4:]
        second_ref = rest_ref
    core = expert_ref[0] % 2

    def rows(piece, low, high):
        if streams:
            return jnp.concatenate([row_refs[0][core, :, low:high], row_refs[0][1 - core, :, low:high]], axis=0)
        start = CUTS[piece][0]
        return jnp.concatenate([row_refs[0][:, low:high], row_refs[1 + piece][:, low - start : high - start]], axis=0)

    for piece, (low, high) in enumerate(CUTS):
        gate = jnp.dot(rows(piece, low, high), gate_ref[0, low:high, :], preferred_element_type=F32)
        gate_sum[...] = gate if low == 0 else gate_sum[...] + gate
    for piece, (low, high) in enumerate(CUTS):
        if streams and low == MIDDLE:
            copy.wait()
        ref, start = (first_ref, 0) if low < MIDDLE else (second_ref, MIDDLE)
        up = jnp.dot(rows(piece, low, high), ref[0, low - start : high - start, :], preferred_element_type=F32)
        up_sum[...] = up if low == 0 else up_sum[...] + up
    lanes = expert_lanes(expert_ref[0], (2 * SEL, EXT), 1)
    scale = jnp.sum(jnp.where(lanes, rows(1, D, D + EXT).astype(F32), 0.0), axis=1, keepdims=True)
    v = gate_sum[...]
    hidden[...] = (v / (1.0 + jnp.exp(-v)) * up_sum[...] * scale).astype(BF16)


def hidden_units(expert, rows, gate, first, rest, after, streams):
    second = jax.ShapeDtypeStruct((1, D - MIDDLE, 512), BF16)
    return pl.pallas_call(
        functools.partial(hidden_kernel, streams),
        out_shape=[jax.ShapeDtypeStruct((2 * SEL, 512), BF16)] + [second] * streams,
        in_specs=[SMEM] + [VMEM] * (len(rows) + 2) + [HBM if streams else VMEM, ANY],
        out_specs=[VMEM] * (1 + streams),
        scratch_shapes=[pltpu.VMEM((2 * SEL, 512), F32)] * 2 + [pltpu.SemaphoreType.DMA] * streams,
        compiler_params=SMALL,
        cost_estimate=BRIEF,
        name="hidden",
    )(expert, *rows, gate, first, in_hbm(rest) if streams else rest, after)


def down_kernel(hidden_ref, down_ref, after_ref, mine_ref, theirs_ref):
    del after_ref
    for n in range(0, D, 1024):
        block = slice(n, n + 1024)
        value = jnp.dot(hidden_ref[...], down_ref[0, :, block], preferred_element_type=F32).astype(BF16)
        mine_ref[:, block] = value[:SEL]
        theirs_ref[:, block] = value[SEL:]


def down_rows(hidden, down, after):
    return pl.pallas_call(
        down_kernel,
        out_shape=[jax.ShapeDtypeStruct((SEL, D), BF16)] * 2,
        in_specs=[VMEM, VMEM, ANY],
        out_specs=[VMEM, VMEM],
        compiler_params=SMALL,
        cost_estimate=BRIEF,
        name="down",
    )(hidden, down, after)


def spread_kernel(first, expert_ref, *refs):
    count = (len(refs) - 4) // 2
    exts, outs = refs[:count], refs[count + 3 : -1]
    mine_ref, theirs_ref = refs[count : count + 2]
    place_scr = refs[-1]
    part, sel = count * BLOCK, count * BLOCK // 4
    own = expert_ref[0]
    turn = lax.broadcasted_iota(jnp.int32, (EXT, EXT), 1)
    experts = jnp.where(turn == 0, own, own ^ 1)
    wanted = jnp.where(expert_lanes(experts, (EXT, EXT), 0) & (turn < 2), 1.0, 0.0).astype(BF16)
    ext = jnp.concatenate([ref[:, HALF:] for ref in exts], axis=0)
    chosen = jnp.dot(ext, wanted, preferred_element_type=F32) > 0
    row = lax.broadcasted_iota(jnp.int32, (part, part), 0)
    other = lax.broadcasted_iota(jnp.int32, (part, part), 1)
    earlier = jnp.where((row // 4 == other // 4) & (other < row), 1.0, 0.0).astype(BF16)
    rank = jnp.dot(earlier, jnp.where(chosen, 1.0, 0.0).astype(BF16), preferred_element_type=F32)
    token = lax.broadcasted_iota(jnp.int32, (part, EXT), 0)
    place = jnp.where(chosen, token // 8 * 2 + rank.astype(jnp.int32), -1)
    column = lax.broadcasted_iota(jnp.int32, (part, 4 * sel), 1)
    hit = jnp.where(column // sel % 2 == 0, place[:, 0:1], place[:, 1:2]) == column % sel
    is_left = lax.broadcasted_iota(jnp.int32, (part, 4 * sel), 0) % 8 < 4
    place_scr[...] = jnp.where(hit & (is_left == (column < 2 * sel)), 1.0, 0.0).astype(BF16)
    rows = slice(first * BLOCK // 4, first * BLOCK // 4 + sel)
    for n in range(0, HALF, 512):
        left, right = slice(n, n + 512), slice(HALF + n, HALF + n + 512)
        y = jnp.concatenate(
            [mine_ref[rows, left], theirs_ref[rows, left], mine_ref[rows, right], theirs_ref[rows, right]], axis=0
        )
        value = jnp.dot(place_scr[...], y, preferred_element_type=F32).astype(BF16)
        for i in range(count):
            outs[i][:, left] = value[i * BLOCK : (i + 1) * BLOCK]


def spread(expert, blocks, mine, theirs, after, first=0):
    count = len(blocks)
    return pl.pallas_call(
        functools.partial(spread_kernel, first),
        out_shape=[jax.ShapeDtypeStruct((BLOCK, HALF), BF16)] * count,
        in_specs=[SMEM] + [VMEM] * (count + 2) + [ANY],
        out_specs=[VMEM] * count,
        scratch_shapes=[pltpu.VMEM((count * BLOCK, count * BLOCK), BF16)],
        compiler_params=SMALL,
        cost_estimate=BRIEF,
        name="spread",
    )(expert, *blocks, mine, theirs, after)


def add(*terms):
    total = terms[0].astype(F32)
    for term in terms[1:]:
        total += term.astype(F32)
    return total.astype(BF16)


def finish_kernel(parts_ref, out_ref):
    total = parts_ref[0].astype(F32)
    for i in range(1, 8):
        total += parts_ref[i].astype(F32)
    out_ref[:, :HALF] = total[:4].astype(BF16)
    out_ref[:, HALF:] = total[4:].astype(BF16)


def finish(parts):
    return pl.pallas_call(
        finish_kernel,
        out_shape=jax.ShapeDtypeStruct((4, D), BF16),
        in_specs=[VMEM],
        out_specs=VMEM,
        compiler_params=SMALL,
        name="finish",
    )(parts)


def body(tokens, ids, weights, gate, up, down):
    expert = lax.axis_index("dev").astype(jnp.int32).reshape(1)
    own = swap_near(pack(expert, tokens, ids, weights)).reshape(BLOCK, WIDE)
    x, y, z = swap_far(own, 0), swap_far(own, 1), swap_far(own, 2)
    xy, yz, zx = swap_far(y, 0), swap_far(z, 1), swap_far(x, 2)
    xyz = swap_far(z, 4)
    near = (x, y, z, own)
    pair, up_first = select(expert, near, own, (up,))
    hidden_near, up_second = hidden_units(expert, [swap_cores(pair)], gate, up_first, up, own, 1)
    result_near, theirs = down_rows(hidden_near, down, own)
    xy, yz, zx, xyz, theirs = lax.optimization_barrier((xy, yz, zx, xyz, theirs))
    far = (xy, zx, yz, xyz)
    returned_near = to_sibling(theirs)
    mine_far, *sent = select(expert, far, result_near)
    rows = [mine_far] + [to_sibling(piece) for piece in sent]
    y_x, y_y, y_z, y_own = spread(expert, near, result_near, returned_near, mine_far)
    (hidden_far,) = hidden_units(expert, rows, gate, up_first, up_second, y_own, 0)
    result, theirs = down_rows(hidden_far, down, own)
    returned = to_sibling(theirs)
    y_xy, y_zx, y_yz, y_xyz = spread(expert, far, result, returned, own)
    at_own = swap_far(y_xyz, 3)
    at_y, at_z, at_x = swap_far(y_xy, 0), swap_far(y_yz, 1), swap_far(y_zx, 2)
    total = add(
        at_own,
        y_own,
        swap_far(add(y_x, at_x), 0),
        swap_far(add(y_y, at_y), 1),
        swap_far(add(y_z, at_z), 2),
    )
    return finish(swap_near(total.reshape(8, 8, HALF)))


def solution(mesh):
    in_specs = (
        P(AXES, None),
        P(AXES, None),
        P(AXES, None),
        P("dev", None, "grp"),
        P("dev", None, "grp"),
        P("dev", "grp", None),
    )
    return jax.shard_map(body, mesh=mesh, in_specs=in_specs, out_specs=P(AXES, None), check_vma=False)
```

```python
import functools

import jax
import jax.numpy as jnp
from jax import lax
from jax.experimental import pallas as pl
from jax.experimental.pallas import tpu as pltpu
from jax.sharding import PartitionSpec as P

AXES = ("grp", "dev")
D = 7168
HALF = D // 2
EXT = 128
WIDE = HALF + EXT
BLOCK = 64
PART = 4 * BLOCK
SEL = 64
F32 = jnp.float32
BF16 = jnp.bfloat16
MIB = 1 << 20
VMEM = pl.BlockSpec(memory_space=pltpu.VMEM)
SMEM = pl.BlockSpec(memory_space=pltpu.SMEM)
HBM = pl.BlockSpec(memory_space=pltpu.HBM)
ANY = pl.BlockSpec(memory_space=pl.ANY)
SMALL = pltpu.CompilerParams(vmem_limit_bytes=8 * MIB)


MIDDLE = 2560
CUTS = ((0, 2560), (2560, 5120), (5120, D))
BRIEF = pl.CostEstimate(flops=1000, bytes_accessed=1000, transcendentals=0)


def flat(z, x, y, c):
    return ((z * 4 + x) * 4 + y) * 2 + c


def near_groups():
    seen, groups = set(), []
    for z in range(4):
        for x in range(4):
            for y in range(4):
                for c in range(2):
                    if flat(z, x, y, c) in seen:
                        continue
                    m = 3 if c else 1
                    members = [
                        flat(z ^ (m * i), x ^ (m * j), y ^ (m * k), c)
                        for i in (0, 1) for j in (0, 1) for k in (0, 1)
                    ]
                    seen.update(members)
                    groups.append(members)
    return groups


def far_pairs(*axes):
    pairs = []
    for z in range(4):
        for x in range(4):
            for y in range(4):
                for c in range(2):
                    at = [x, z, y]
                    for axis in axes:
                        at[axis] ^= 1 if c else 3
                    pairs.append((flat(z, x, y, c), flat(at[1], at[0], at[2], c)))
    return pairs


NEAR = near_groups()
FAR = [far_pairs(0), far_pairs(1), far_pairs(2), far_pairs(0, 1, 2), far_pairs(0, 1)]


def swap_near(values):
    return lax.all_to_all(values, AXES, 0, 0, axis_index_groups=NEAR, tiled=True)


def swap_far(values, axis):
    return lax.ppermute(values, AXES, FAR[axis])


def to_sibling(values):
    return lax.ppermute(values, "dev", [(i, i ^ 1) for i in range(32)])


def pack_kernel(expert_ref, tokens_hbm, ids_hbm, weights_hbm, out_ref, tokens_ref, ids_ref, weights_ref, sems):
    del expert_ref
    pairs = ((tokens_hbm, tokens_ref), (ids_hbm, ids_ref), (weights_hbm, weights_ref))
    copies = [pltpu.make_async_copy(source, target, sems.at[i]) for i, (source, target) in enumerate(pairs)]
    for copy in copies:
        copy.start()
    for copy in copies:
        copy.wait()
    lane = lax.broadcasted_iota(jnp.int32, (4, EXT), 1)
    dense = jnp.zeros((4, EXT), F32)
    for k in range(8):
        dense += jnp.where(ids_ref[:, k : k + 1] == lane % 32, weights_ref[:, k : k + 1], 0.0)
    high = dense.astype(BF16).astype(F32)
    route = jnp.where(lane < 32, high, jnp.where(lane < 64, dense - high, 0.0))
    rows = tokens_ref[...].astype(F32)
    left = jnp.concatenate([rows[:, :HALF], route], axis=1)
    right = jnp.concatenate([rows[:, HALF:], route], axis=1)
    block = jnp.concatenate([left, right], axis=0).astype(BF16)
    for i in range(8):
        out_ref[i] = block


def in_hbm(values):
    return pltpu.with_memory_space_constraint(values, pltpu.HBM)


def pack(expert, tokens, ids, weights):
    return pl.pallas_call(
        pack_kernel,
        out_shape=jax.ShapeDtypeStruct((8, 8, WIDE), BF16),
        in_specs=[SMEM, HBM, HBM, HBM],
        out_specs=VMEM,
        scratch_shapes=[
            pltpu.VMEM((4, D), BF16),
            pltpu.VMEM((4, 8), jnp.int32),
            pltpu.VMEM((4, 8), F32),
            pltpu.SemaphoreType.DMA((3,)),
        ],
        compiler_params=pltpu.CompilerParams(vmem_limit_bytes=4 * MIB),
        name="pack",
    )(expert, in_hbm(tokens), in_hbm(ids), in_hbm(weights))


def expert_lanes(expert, shape, dim):
    lane = lax.broadcasted_iota(jnp.int32, shape, dim)
    return (lane < 64) & (lane % 32 == expert)


def select_kernel(loads, expert_ref, *refs):
    refs = list(refs)
    blocks = [refs.pop(0) for _ in range(4)]
    sources = [refs.pop(0) for _ in range(loads)]
    del refs[0]
    mine_ref, sent_refs, targets = refs[0], refs[1:4], refs[4 : 4 + loads]
    pick, sem = refs[4 + loads :]
    copies = [pltpu.make_async_copy(a.at[:, :MIDDLE, :], b, sem) for a, b in zip(sources, targets)]
    for copy in copies:
        copy.start()
    own = expert_ref[0]
    turn = lax.broadcasted_iota(jnp.int32, (8, EXT), 0)
    experts = jnp.where(turn == 0, own, own ^ 1)
    wanted = jnp.where(expert_lanes(experts, (8, EXT), 1) & (turn < 2), 1.0, 0.0).astype(BF16)
    ext = jnp.concatenate([ref[:, HALF:] for ref in blocks], axis=0)
    route = lax.dot_general(wanted, ext, (((1,), (1,)), ((), ())), preferred_element_type=F32)
    chosen = route > 0
    first = lax.broadcasted_iota(jnp.int32, (PART, PART), 0)
    second = lax.broadcasted_iota(jnp.int32, (PART, PART), 1)
    earlier = jnp.where((first // 4 == second // 4) & (first < second), 1.0, 0.0).astype(BF16)
    rank = jnp.dot(jnp.where(chosen, 1.0, 0.0).astype(BF16), earlier, preferred_element_type=F32)
    column = lax.broadcasted_iota(jnp.int32, (8, PART), 1)
    place = jnp.where(chosen, column // 8 * 2 + rank.astype(jnp.int32), -1)
    row = lax.broadcasted_iota(jnp.int32, (SEL, PART), 0)
    is_left = lax.broadcasted_iota(jnp.int32, (SEL, PART), 1) % 8 < 4
    for e in range(2):
        hit = place[e : e + 1, :] == row
        pick[e * SEL : (e + 1) * SEL, :] = jnp.where(hit & is_left, 1.0, 0.0).astype(BF16)
        pick[(2 + e) * SEL : (3 + e) * SEL, :] = jnp.where(hit & ~is_left, 1.0, 0.0).astype(BF16)


    def put_sent(start, value):
        low = 0
        while low < value.shape[1]:
            piece = min((start + low) // MIDDLE, 2)
            at = start + low - CUTS[piece][0]
            size = min(value.shape[1] - low, sent_refs[piece].shape[1] - at)
            sent_refs[piece][:, at : at + size] = value[:, low : low + size]
            low += size

    for n in range(0, HALF, 512):
        x = jnp.concatenate([ref[:, n : n + 512] for ref in blocks], axis=0)
        value = jnp.dot(pick[...], x, preferred_element_type=F32).astype(BF16)
        mine_ref[:, n : n + 512] = value[:SEL]
        put_sent(n, value[SEL : 2 * SEL])
        mine_ref[:, HALF + n : HALF + n + 512] = value[2 * SEL : 3 * SEL]
        put_sent(HALF + n, value[3 * SEL :])
    value = jnp.dot(pick[: 2 * SEL, :], ext, preferred_element_type=F32).astype(BF16)
    mine_ref[:, D:] = value[:SEL]
    put_sent(D, value[SEL:])
    for copy in copies:
        copy.wait()


def select(expert, blocks, after, loads=()):
    return pl.pallas_call(
        functools.partial(select_kernel, len(loads)),
        out_shape=[jax.ShapeDtypeStruct((SEL, D + EXT), BF16)]
        + [jax.ShapeDtypeStruct((SEL, high - low + EXT * (high == D)), BF16) for low, high in CUTS]
        + [jax.ShapeDtypeStruct((1, MIDDLE, 512), BF16) for _ in loads],
        in_specs=[SMEM] + [VMEM] * 4 + [HBM] * len(loads) + [ANY],
        out_specs=[VMEM] * (4 + len(loads)),
        scratch_shapes=[pltpu.VMEM((PART, PART), BF16), pltpu.SemaphoreType.DMA],
        compiler_params=SMALL,
        cost_estimate=BRIEF,
        name="select",
    )(expert, *blocks, *[in_hbm(load) for load in loads], after)


def hidden_kernel(streams, expert_ref, mine_ref, a_ref, b_ref, c_ref, gate_ref, first_ref, rest_ref, after_ref, *refs):
    del after_ref
    if streams:
        hidden, second_ref, gate_sum, up_sum, sem = refs
        copy = pltpu.make_async_copy(rest_ref.at[:, MIDDLE:, :], second_ref, sem)
        copy.start()
    else:
        hidden, gate_sum, up_sum = refs
        second_ref = rest_ref

    def rows(piece, low, high):
        start = CUTS[piece][0]
        theirs_ref = (a_ref, b_ref, c_ref)[piece]
        return jnp.concatenate([mine_ref[:, low:high], theirs_ref[:, low - start : high - start]], axis=0)

    for piece, (low, high) in enumerate(CUTS):
        gate = jnp.dot(rows(piece, low, high), gate_ref[0, low:high, :], preferred_element_type=F32)
        gate_sum[...] = gate if low == 0 else gate_sum[...] + gate
    for piece, (low, high) in enumerate(CUTS):
        if streams and low == MIDDLE:
            copy.wait()
        ref, start = (first_ref, 0) if low < MIDDLE else (second_ref, MIDDLE)
        up = jnp.dot(rows(piece, low, high), ref[0, low - start : high - start, :], preferred_element_type=F32)
        up_sum[...] = up if low == 0 else up_sum[...] + up
    lanes = expert_lanes(expert_ref[0], (2 * SEL, EXT), 1)
    scale = jnp.sum(jnp.where(lanes, rows(2, D, D + EXT).astype(F32), 0.0), axis=1, keepdims=True)
    v = gate_sum[...]
    hidden[...] = (v / (1.0 + jnp.exp(-v)) * up_sum[...] * scale).astype(BF16)


def hidden_units(expert, mine, theirs, gate, first, rest, after, streams):
    second = jax.ShapeDtypeStruct((1, D - MIDDLE, 512), BF16)
    return pl.pallas_call(
        functools.partial(hidden_kernel, streams),
        out_shape=[jax.ShapeDtypeStruct((2 * SEL, 512), BF16)] + [second] * streams,
        in_specs=[SMEM] + [VMEM] * 6 + [HBM if streams else VMEM, ANY],
        out_specs=[VMEM] * (1 + streams),
        scratch_shapes=[pltpu.VMEM((2 * SEL, 512), F32)] * 2 + [pltpu.SemaphoreType.DMA] * streams,
        compiler_params=SMALL,
        cost_estimate=BRIEF,
        name="hidden",
    )(expert, mine, *theirs, gate, first, in_hbm(rest) if streams else rest, after)


def down_kernel(hidden_ref, down_ref, after_ref, mine_ref, theirs_ref):
    del after_ref
    for n in range(0, D, 1024):
        block = slice(n, n + 1024)
        value = jnp.dot(hidden_ref[...], down_ref[0, :, block], preferred_element_type=F32).astype(BF16)
        mine_ref[:, block] = value[:SEL]
        theirs_ref[:, block] = value[SEL:]


def down_rows(hidden, down, after):
    return pl.pallas_call(
        down_kernel,
        out_shape=[jax.ShapeDtypeStruct((SEL, D), BF16)] * 2,
        in_specs=[VMEM, VMEM, ANY],
        out_specs=[VMEM, VMEM],
        compiler_params=SMALL,
        cost_estimate=BRIEF,
        name="down",
    )(hidden, down, after)


def spread_kernel(first, expert_ref, *refs):
    count = (len(refs) - 4) // 2
    exts, outs = refs[:count], refs[count + 3 : -1]
    mine_ref, theirs_ref = refs[count : count + 2]
    place_scr = refs[-1]
    part, sel = count * BLOCK, count * BLOCK // 4
    own = expert_ref[0]
    turn = lax.broadcasted_iota(jnp.int32, (EXT, EXT), 1)
    experts = jnp.where(turn == 0, own, own ^ 1)
    wanted = jnp.where(expert_lanes(experts, (EXT, EXT), 0) & (turn < 2), 1.0, 0.0).astype(BF16)
    ext = jnp.concatenate([ref[:, HALF:] for ref in exts], axis=0)
    chosen = jnp.dot(ext, wanted, preferred_element_type=F32) > 0
    row = lax.broadcasted_iota(jnp.int32, (part, part), 0)
    other = lax.broadcasted_iota(jnp.int32, (part, part), 1)
    earlier = jnp.where((row // 4 == other // 4) & (other < row), 1.0, 0.0).astype(BF16)
    rank = jnp.dot(earlier, jnp.where(chosen, 1.0, 0.0).astype(BF16), preferred_element_type=F32)
    token = lax.broadcasted_iota(jnp.int32, (part, EXT), 0)
    place = jnp.where(chosen, token // 8 * 2 + rank.astype(jnp.int32), -1)
    column = lax.broadcasted_iota(jnp.int32, (part, 4 * sel), 1)
    hit = jnp.where(column // sel % 2 == 0, place[:, 0:1], place[:, 1:2]) == column % sel
    is_left = lax.broadcasted_iota(jnp.int32, (part, 4 * sel), 0) % 8 < 4
    place_scr[...] = jnp.where(hit & (is_left == (column < 2 * sel)), 1.0, 0.0).astype(BF16)
    rows = slice(first * BLOCK // 4, first * BLOCK // 4 + sel)
    for n in range(0, HALF, 512):
        left, right = slice(n, n + 512), slice(HALF + n, HALF + n + 512)
        y = jnp.concatenate(
            [mine_ref[rows, left], theirs_ref[rows, left], mine_ref[rows, right], theirs_ref[rows, right]], axis=0
        )
        value = jnp.dot(place_scr[...], y, preferred_element_type=F32).astype(BF16)
        for i in range(count):
            outs[i][:, left] = value[i * BLOCK : (i + 1) * BLOCK]


def spread(expert, blocks, mine, theirs, after, first=0):
    count = len(blocks)
    return pl.pallas_call(
        functools.partial(spread_kernel, first),
        out_shape=[jax.ShapeDtypeStruct((BLOCK, HALF), BF16)] * count,
        in_specs=[SMEM] + [VMEM] * (count + 2) + [ANY],
        out_specs=[VMEM] * count,
        scratch_shapes=[pltpu.VMEM((count * BLOCK, count * BLOCK), BF16)],
        compiler_params=SMALL,
        cost_estimate=BRIEF,
        name="spread",
    )(expert, *blocks, mine, theirs, after)


def add(*terms):
    total = terms[0].astype(F32)
    for term in terms[1:]:
        total += term.astype(F32)
    return total.astype(BF16)


def finish_kernel(parts_ref, out_ref):
    total = parts_ref[0].astype(F32)
    for i in range(1, 8):
        total += parts_ref[i].astype(F32)
    out_ref[:, :HALF] = total[:4].astype(BF16)
    out_ref[:, HALF:] = total[4:].astype(BF16)


def finish(parts):
    return pl.pallas_call(
        finish_kernel,
        out_shape=jax.ShapeDtypeStruct((4, D), BF16),
        in_specs=[VMEM],
        out_specs=VMEM,
        compiler_params=SMALL,
        name="finish",
    )(parts)


def body(tokens, ids, weights, gate, up, down):
    expert = lax.axis_index("dev").astype(jnp.int32).reshape(1)
    own = swap_near(pack(expert, tokens, ids, weights)).reshape(BLOCK, WIDE)
    x, y, z = swap_far(own, 0), swap_far(own, 1), swap_far(own, 2)
    xy, yz, zx = swap_far(y, 0), swap_far(z, 1), swap_far(x, 2)
    xyz = swap_far(z, 4)
    near = (x, y, z, own)
    mine_near, *sent, up_first = select(expert, near, own, (up,))
    xy, yz, *sent = lax.optimization_barrier((xy, yz, *sent))
    got_near = [to_sibling(piece) for piece in sent]
    hidden_near, up_second = hidden_units(expert, mine_near, got_near, gate, up_first, up, own, 1)
    result_near, theirs = down_rows(hidden_near, down, own)
    xy, yz, zx, xyz, theirs = lax.optimization_barrier((xy, yz, zx, xyz, theirs))
    far = (xy, zx, yz, xyz)
    returned_near = to_sibling(theirs)
    mine_far, *sent = select(expert, far, result_near)
    got_far = [to_sibling(piece) for piece in sent]
    y_x, y_y, y_z, y_own = spread(expert, near, result_near, returned_near, mine_far)
    (hidden_far,) = hidden_units(expert, mine_far, got_far, gate, up_first, up_second, y_own, 0)
    result, theirs = down_rows(hidden_far, down, own)
    returned = to_sibling(theirs)
    y_xy, y_zx, y_yz, y_xyz = spread(expert, far, result, returned, own)
    at_own = swap_far(y_xyz, 3)
    at_y, at_z, at_x = swap_far(y_xy, 0), swap_far(y_yz, 1), swap_far(y_zx, 2)
    total = add(
        at_own,
        y_own,
        swap_far(add(y_x, at_x), 0),
        swap_far(add(y_y, at_y), 1),
        swap_far(add(y_z, at_z), 2),
    )
    return finish(swap_near(total.reshape(8, 8, HALF)))


def solution(mesh):
    in_specs = (
        P(AXES, None),
        P(AXES, None),
        P(AXES, None),
        P("dev", None, "grp"),
        P("dev", None, "grp"),
        P("dev", "grp", None),
    )
    return jax.shard_map(body, mesh=mesh, in_specs=in_specs, out_specs=P(AXES, None), check_vma=False)
```

```python
import functools

import jax
import jax.numpy as jnp
from jax import lax
from jax.experimental import pallas as pl
from jax.experimental.pallas import tpu as pltpu
from jax.sharding import PartitionSpec as P

AXES = ("grp", "dev")
D = 7168
HALF = D // 2
EXT = 128
WIDE = HALF + EXT
BLOCK = 64
PART = 4 * BLOCK
SEL = 64
F32 = jnp.float32
BF16 = jnp.bfloat16
MIB = 1 << 20
VMEM = pl.BlockSpec(memory_space=pltpu.VMEM)
SMEM = pl.BlockSpec(memory_space=pltpu.SMEM)
HBM = pl.BlockSpec(memory_space=pltpu.HBM)
ANY = pl.BlockSpec(memory_space=pl.ANY)
SMALL = pltpu.CompilerParams(vmem_limit_bytes=8 * MIB)


DEPTH = 1792
MIDDLE = D // 2
BRIEF = pl.CostEstimate(flops=1000, bytes_accessed=1000, transcendentals=0)


def flat(z, x, y, c):
    return ((z * 4 + x) * 4 + y) * 2 + c


def near_groups():
    seen, groups = set(), []
    for z in range(4):
        for x in range(4):
            for y in range(4):
                for c in range(2):
                    if flat(z, x, y, c) in seen:
                        continue
                    m = 3 if c else 1
                    members = [
                        flat(z ^ (m * i), x ^ (m * j), y ^ (m * k), c)
                        for i in (0, 1) for j in (0, 1) for k in (0, 1)
                    ]
                    seen.update(members)
                    groups.append(members)
    return groups


def far_pairs(*axes):
    pairs = []
    for z in range(4):
        for x in range(4):
            for y in range(4):
                for c in range(2):
                    at = [x, y, z]
                    for axis in axes:
                        at[axis] ^= 1 if c else 3
                    pairs.append((flat(z, x, y, c), flat(at[2], at[0], at[1], c)))
    return pairs


NEAR = near_groups()
FAR = [far_pairs(0), far_pairs(1), far_pairs(2), far_pairs(0, 1, 2)]


def swap_near(values):
    return lax.all_to_all(values, AXES, 0, 0, axis_index_groups=NEAR, tiled=True)


def swap_far(values, axis):
    return lax.ppermute(values, AXES, FAR[axis])


def to_sibling(values):
    return lax.ppermute(values, "dev", [(i, i ^ 1) for i in range(32)])


def pack_kernel(expert_ref, tokens_hbm, ids_hbm, weights_hbm, out_ref, tokens_ref, ids_ref, weights_ref, sems):
    del expert_ref
    pairs = ((tokens_hbm, tokens_ref), (ids_hbm, ids_ref), (weights_hbm, weights_ref))
    copies = [pltpu.make_async_copy(source, target, sems.at[i]) for i, (source, target) in enumerate(pairs)]
    for copy in copies:
        copy.start()
    for copy in copies:
        copy.wait()
    lane = lax.broadcasted_iota(jnp.int32, (4, EXT), 1)
    dense = jnp.zeros((4, EXT), F32)
    for k in range(8):
        dense += jnp.where(ids_ref[:, k : k + 1] == lane % 32, weights_ref[:, k : k + 1], 0.0)
    high = dense.astype(BF16).astype(F32)
    route = jnp.where(lane < 32, high, jnp.where(lane < 64, dense - high, 0.0))
    rows = tokens_ref[...].astype(F32)
    left = jnp.concatenate([rows[:, :HALF], route], axis=1)
    right = jnp.concatenate([rows[:, HALF:], route], axis=1)
    block = jnp.concatenate([left, right], axis=0).astype(BF16)
    for i in range(8):
        out_ref[i] = block


def in_hbm(values):
    return pltpu.with_memory_space_constraint(values, pltpu.HBM)


def pack(expert, tokens, ids, weights):
    return pl.pallas_call(
        pack_kernel,
        out_shape=jax.ShapeDtypeStruct((8, 8, WIDE), BF16),
        in_specs=[SMEM, HBM, HBM, HBM],
        out_specs=VMEM,
        scratch_shapes=[
            pltpu.VMEM((4, D), BF16),
            pltpu.VMEM((4, 8), jnp.int32),
            pltpu.VMEM((4, 8), F32),
            pltpu.SemaphoreType.DMA((3,)),
        ],
        compiler_params=pltpu.CompilerParams(vmem_limit_bytes=4 * MIB),
        name="pack",
    )(expert, in_hbm(tokens), in_hbm(ids), in_hbm(weights))


def expert_lanes(expert, shape, dim):
    lane = lax.broadcasted_iota(jnp.int32, shape, dim)
    return (lane < 64) & (lane % 32 == expert)


def select_kernel(loads, expert_ref, *refs):
    refs = list(refs)
    blocks = [refs.pop(0) for _ in range(4)]
    sources = [refs.pop(0) for _ in range(loads)]
    del refs[0]
    mine_ref, sent_ref = refs[:2]
    targets = refs[2 : 2 + loads]
    pick, sem = refs[2 + loads :]
    copies = [pltpu.make_async_copy(a.at[:, :MIDDLE, :], b, sem) for a, b in zip(sources, targets)]
    for copy in copies:
        copy.start()
    own = expert_ref[0]
    turn = lax.broadcasted_iota(jnp.int32, (8, EXT), 0)
    experts = jnp.where(turn == 0, own, own ^ 1)
    wanted = jnp.where(expert_lanes(experts, (8, EXT), 1) & (turn < 2), 1.0, 0.0).astype(BF16)
    ext = jnp.concatenate([ref[:, HALF:] for ref in blocks], axis=0)
    route = lax.dot_general(wanted, ext, (((1,), (1,)), ((), ())), preferred_element_type=F32)
    chosen = route > 0
    first = lax.broadcasted_iota(jnp.int32, (PART, PART), 0)
    second = lax.broadcasted_iota(jnp.int32, (PART, PART), 1)
    earlier = jnp.where((first // 4 == second // 4) & (first < second), 1.0, 0.0).astype(BF16)
    rank = jnp.dot(jnp.where(chosen, 1.0, 0.0).astype(BF16), earlier, preferred_element_type=F32)
    column = lax.broadcasted_iota(jnp.int32, (8, PART), 1)
    place = jnp.where(chosen, column // 8 * 2 + rank.astype(jnp.int32), -1)
    row = lax.broadcasted_iota(jnp.int32, (SEL, PART), 0)
    is_left = lax.broadcasted_iota(jnp.int32, (SEL, PART), 1) % 8 < 4
    for e in range(2):
        hit = place[e : e + 1, :] == row
        pick[e * SEL : (e + 1) * SEL, :] = jnp.where(hit & is_left, 1.0, 0.0).astype(BF16)
        pick[(2 + e) * SEL : (3 + e) * SEL, :] = jnp.where(hit & ~is_left, 1.0, 0.0).astype(BF16)
    for n in range(0, HALF, 512):
        x = jnp.concatenate([ref[:, n : n + 512] for ref in blocks], axis=0)
        value = jnp.dot(pick[...], x, preferred_element_type=F32).astype(BF16)
        mine_ref[:, n : n + 512] = value[:SEL]
        sent_ref[:, n : n + 512] = value[SEL : 2 * SEL]
        mine_ref[:, HALF + n : HALF + n + 512] = value[2 * SEL : 3 * SEL]
        sent_ref[:, HALF + n : HALF + n + 512] = value[3 * SEL :]
    value = jnp.dot(pick[: 2 * SEL, :], ext, preferred_element_type=F32).astype(BF16)
    mine_ref[:, D:] = value[:SEL]
    sent_ref[:, D:] = value[SEL:]
    for copy in copies:
        copy.wait()


def select(expert, blocks, after, loads=()):
    return pl.pallas_call(
        functools.partial(select_kernel, len(loads)),
        out_shape=[jax.ShapeDtypeStruct((SEL, D + EXT), BF16)] * 2
        + [jax.ShapeDtypeStruct((1, MIDDLE, 512), BF16) for _ in loads],
        in_specs=[SMEM] + [VMEM] * 4 + [HBM] * len(loads) + [ANY],
        out_specs=[VMEM] * (2 + len(loads)),
        scratch_shapes=[pltpu.VMEM((PART, PART), BF16), pltpu.SemaphoreType.DMA],
        compiler_params=SMALL,
        cost_estimate=BRIEF,
        name="select",
    )(expert, *blocks, *[in_hbm(load) for load in loads], after)


def hidden_kernel(streams, expert_ref, mine_ref, theirs_ref, gate_ref, first_ref, rest_ref, after_ref, *refs):
    del after_ref
    if streams:
        hidden, second_ref, gate_sum, up_sum, sem = refs
        copy = pltpu.make_async_copy(rest_ref.at[:, MIDDLE:, :], second_ref, sem)
        copy.start()
    else:
        hidden, gate_sum, up_sum = refs
        second_ref = rest_ref

    def rows(block):
        return jnp.concatenate([mine_ref[:, block], theirs_ref[:, block]], axis=0)

    for i in range(0, D, DEPTH):
        block = slice(i, i + DEPTH)
        gate = jnp.dot(rows(block), gate_ref[0, block, :], preferred_element_type=F32)
        gate_sum[...] = gate if i == 0 else gate_sum[...] + gate
    for i in range(0, D, DEPTH):
        if streams and i == MIDDLE:
            copy.wait()
        ref, start = (first_ref, i) if i < MIDDLE else (second_ref, i - MIDDLE)
        up = jnp.dot(rows(slice(i, i + DEPTH)), ref[0, start : start + DEPTH, :], preferred_element_type=F32)
        up_sum[...] = up if i == 0 else up_sum[...] + up
    lanes = expert_lanes(expert_ref[0], (2 * SEL, EXT), 1)
    scale = jnp.sum(jnp.where(lanes, rows(slice(D, D + EXT)).astype(F32), 0.0), axis=1, keepdims=True)
    v = gate_sum[...]
    hidden[...] = (v / (1.0 + jnp.exp(-v)) * up_sum[...] * scale).astype(BF16)


def hidden_units(expert, mine, theirs, gate, first, rest, after, streams):
    half = jax.ShapeDtypeStruct((1, MIDDLE, 512), BF16)
    return pl.pallas_call(
        functools.partial(hidden_kernel, streams),
        out_shape=[jax.ShapeDtypeStruct((2 * SEL, 512), BF16)] + [half] * streams,
        in_specs=[SMEM, VMEM, VMEM, VMEM, VMEM, HBM if streams else VMEM, ANY],
        out_specs=[VMEM] * (1 + streams),
        scratch_shapes=[pltpu.VMEM((2 * SEL, 512), F32)] * 2 + [pltpu.SemaphoreType.DMA] * streams,
        compiler_params=SMALL,
        cost_estimate=BRIEF,
        name="hidden",
    )(expert, mine, theirs, gate, first, in_hbm(rest) if streams else rest, after)


def down_kernel(hidden_ref, down_ref, after_ref, mine_ref, theirs_ref):
    del after_ref
    for n in range(0, D, 1024):
        block = slice(n, n + 1024)
        value = jnp.dot(hidden_ref[...], down_ref[0, :, block], preferred_element_type=F32).astype(BF16)
        mine_ref[:, block] = value[:SEL]
        theirs_ref[:, block] = value[SEL:]


def down_rows(hidden, down, after):
    return pl.pallas_call(
        down_kernel,
        out_shape=[jax.ShapeDtypeStruct((SEL, D), BF16)] * 2,
        in_specs=[VMEM, VMEM, ANY],
        out_specs=[VMEM, VMEM],
        compiler_params=SMALL,
        cost_estimate=BRIEF,
        name="down",
    )(hidden, down, after)


def spread_kernel(expert_ref, *refs):
    refs = list(refs)
    exts = [refs.pop(0) for _ in range(4)]
    mine_ref, theirs_ref = refs[:2]
    outs = [refs[3 + i] for i in range(4)]
    place_scr = refs[7]
    own = expert_ref[0]
    turn = lax.broadcasted_iota(jnp.int32, (EXT, EXT), 1)
    experts = jnp.where(turn == 0, own, own ^ 1)
    wanted = jnp.where(expert_lanes(experts, (EXT, EXT), 0) & (turn < 2), 1.0, 0.0).astype(BF16)
    ext = jnp.concatenate([ref[:, HALF:] for ref in exts], axis=0)
    chosen = jnp.dot(ext, wanted, preferred_element_type=F32) > 0
    first = lax.broadcasted_iota(jnp.int32, (PART, PART), 0)
    second = lax.broadcasted_iota(jnp.int32, (PART, PART), 1)
    earlier = jnp.where((first // 4 == second // 4) & (second < first), 1.0, 0.0).astype(BF16)
    rank = jnp.dot(earlier, jnp.where(chosen, 1.0, 0.0).astype(BF16), preferred_element_type=F32)
    token = lax.broadcasted_iota(jnp.int32, (PART, EXT), 0)
    place = jnp.where(chosen, token // 8 * 2 + rank.astype(jnp.int32), -1)
    column = lax.broadcasted_iota(jnp.int32, (PART, 2 * SEL), 1)
    hit = jnp.where(column < SEL, place[:, 0:1], place[:, 1:2]) == column % SEL
    is_left = lax.broadcasted_iota(jnp.int32, (PART, 2 * SEL), 0) % 8 < 4
    place_scr[:, : 2 * SEL] = jnp.where(hit & is_left, 1.0, 0.0).astype(BF16)
    place_scr[:, 2 * SEL :] = jnp.where(hit & ~is_left, 1.0, 0.0).astype(BF16)
    for n in range(0, HALF, 512):
        left, right = slice(n, n + 512), slice(HALF + n, HALF + n + 512)
        y = jnp.concatenate([mine_ref[:, left], theirs_ref[:, left], mine_ref[:, right], theirs_ref[:, right]], axis=0)
        value = jnp.dot(place_scr[...], y, preferred_element_type=F32).astype(BF16)
        for i in range(4):
            outs[i][:, left] = value[i * BLOCK : (i + 1) * BLOCK]


def spread(expert, blocks, mine, theirs, after):
    return pl.pallas_call(
        spread_kernel,
        out_shape=[jax.ShapeDtypeStruct((BLOCK, HALF), BF16)] * 4,
        in_specs=[SMEM] + [VMEM] * 6 + [ANY],
        out_specs=[VMEM] * 4,
        scratch_shapes=[pltpu.VMEM((PART, 4 * SEL), BF16)],
        compiler_params=SMALL,
        cost_estimate=BRIEF,
        name="spread",
    )(expert, *blocks, mine, theirs, after)


def add(*terms):
    total = terms[0].astype(F32)
    for term in terms[1:]:
        total += term.astype(F32)
    return total.astype(BF16)


def finish_kernel(parts_ref, out_ref):
    total = parts_ref[0].astype(F32)
    for i in range(1, 8):
        total += parts_ref[i].astype(F32)
    out_ref[:, :HALF] = total[:4].astype(BF16)
    out_ref[:, HALF:] = total[4:].astype(BF16)


def finish(parts):
    return pl.pallas_call(
        finish_kernel,
        out_shape=jax.ShapeDtypeStruct((4, D), BF16),
        in_specs=[VMEM],
        out_specs=VMEM,
        compiler_params=SMALL,
        name="finish",
    )(parts)


def body(tokens, ids, weights, gate, up, down):
    expert = lax.axis_index("dev").astype(jnp.int32).reshape(1)
    own = swap_near(pack(expert, tokens, ids, weights)).reshape(BLOCK, WIDE)
    x, y, z = swap_far(own, 0), swap_far(own, 1), swap_far(own, 2)
    xyz = swap_far(own, 3)
    xy, yz, zx = swap_far(y, 0), swap_far(z, 1), swap_far(x, 2)
    near = (x, y, z, own)
    mine_near, sent, up_first = select(expert, near, own, (up,))
    xy, yz, zx, xyz, sent = lax.optimization_barrier((xy, yz, zx, xyz, sent))
    got_near = to_sibling(sent)
    far = (xy, zx, yz, xyz)
    mine_far, sent = select(expert, far, own)
    got_far = to_sibling(sent)
    hidden_near, up_second = hidden_units(expert, mine_near, got_near, gate, up_first, up, mine_far, 1)
    result_near, theirs = down_rows(hidden_near, down, own)
    returned_near = to_sibling(theirs)
    (hidden_far,) = hidden_units(expert, mine_far, got_far, gate, up_first, up_second, result_near, 0)
    result, theirs = down_rows(hidden_far, down, own)
    returned = to_sibling(theirs)
    y_x, y_y, y_z, y_own = spread(expert, near, result_near, returned_near, result)
    y_xy, y_zx, y_yz, y_xyz = spread(expert, far, result, returned, y_own)
    at_y, at_x, at_z = swap_far(y_yz, 2), swap_far(y_xy, 1), swap_far(y_zx, 0)
    at_own = swap_far(y_xyz, 3)
    total = add(
        y_own,
        swap_far(add(y_x, at_x), 0),
        swap_far(add(y_y, at_y), 1),
        swap_far(add(y_z, at_z), 2),
        at_own,
    )
    return finish(swap_near(total.reshape(8, 8, HALF)))


def solution(mesh):
    in_specs = (
        P(AXES, None),
        P(AXES, None),
        P(AXES, None),
        P("dev", None, "grp"),
        P("dev", None, "grp"),
        P("dev", "grp", None),
    )
    return jax.shard_map(body, mesh=mesh, in_specs=in_specs, out_specs=P(AXES, None), check_vma=False)
```

```python
import functools

import jax
import jax.numpy as jnp
from jax import lax
from jax.experimental import pallas as pl
from jax.experimental.pallas import tpu as pltpu
from jax.sharding import PartitionSpec as P

AXES = ("grp", "dev")
D = 7168
HALF = D // 2
EXT = 128
WIDE = HALF + EXT
BLOCK = 64
PART = 4 * BLOCK
SEL = 64
F32 = jnp.float32
BF16 = jnp.bfloat16
MIB = 1 << 20
VMEM = pl.BlockSpec(memory_space=pltpu.VMEM)
SMEM = pl.BlockSpec(memory_space=pltpu.SMEM)
HBM = pl.BlockSpec(memory_space=pltpu.HBM)
ANY = pl.BlockSpec(memory_space=pl.ANY)
SMALL = pltpu.CompilerParams(vmem_limit_bytes=8 * MIB)


STEPS = ((0, 2560), (2560, 5120), (5120, D))
THREE = (0, 2560, 5120)
ONE = (0,)
BRIEF = pl.CostEstimate(flops=1000, bytes_accessed=1000, transcendentals=0)


def flat(z, x, y, c):
    return ((z * 4 + x) * 4 + y) * 2 + c


def near_groups():
    seen, groups = set(), []
    for z in range(4):
        for x in range(4):
            for y in range(4):
                for c in range(2):
                    if flat(z, x, y, c) in seen:
                        continue
                    m = 3 if c else 1
                    members = [
                        flat(z ^ (m * i), x ^ (m * j), y ^ (m * k), c)
                        for i in (0, 1) for j in (0, 1) for k in (0, 1)
                    ]
                    seen.update(members)
                    groups.append(members)
    return groups


def far_pairs(*axes):
    pairs = []
    for z in range(4):
        for x in range(4):
            for y in range(4):
                for c in range(2):
                    at = [x, z, y]
                    for axis in axes:
                        at[axis] ^= 1 if c else 3
                    pairs.append((flat(z, x, y, c), flat(at[1], at[0], at[2], c)))
    return pairs


NEAR = near_groups()
FAR = [far_pairs(0), far_pairs(1), far_pairs(2), far_pairs(0, 1, 2)]


def swap_near(values):
    return lax.all_to_all(values, AXES, 0, 0, axis_index_groups=NEAR, tiled=True)


def swap_far(values, axis):
    return lax.ppermute(values, AXES, FAR[axis])


def to_sibling(values):
    return lax.ppermute(values, "dev", [(i, i ^ 1) for i in range(32)])


def pack_kernel(expert_ref, tokens_hbm, ids_hbm, weights_hbm, out_ref, tokens_ref, ids_ref, weights_ref, sems):
    del expert_ref
    pairs = ((tokens_hbm, tokens_ref), (ids_hbm, ids_ref), (weights_hbm, weights_ref))
    copies = [pltpu.make_async_copy(source, target, sems.at[i]) for i, (source, target) in enumerate(pairs)]
    for copy in copies:
        copy.start()
    for copy in copies:
        copy.wait()
    lane = lax.broadcasted_iota(jnp.int32, (4, EXT), 1)
    dense = jnp.zeros((4, EXT), F32)
    for k in range(8):
        dense += jnp.where(ids_ref[:, k : k + 1] == lane % 32, weights_ref[:, k : k + 1], 0.0)
    high = dense.astype(BF16).astype(F32)
    route = jnp.where(lane < 32, high, jnp.where(lane < 64, dense - high, 0.0))
    rows = tokens_ref[...].astype(F32)
    left = jnp.concatenate([rows[:, :HALF], route], axis=1)
    right = jnp.concatenate([rows[:, HALF:], route], axis=1)
    block = jnp.concatenate([left, right], axis=0).astype(BF16)
    for i in range(8):
        out_ref[i] = block


def in_hbm(values):
    return pltpu.with_memory_space_constraint(values, pltpu.HBM)


def pack(expert, tokens, ids, weights):
    return pl.pallas_call(
        pack_kernel,
        out_shape=jax.ShapeDtypeStruct((8, 8, WIDE), BF16),
        in_specs=[SMEM, HBM, HBM, HBM],
        out_specs=VMEM,
        scratch_shapes=[
            pltpu.VMEM((4, D), BF16),
            pltpu.VMEM((4, 8), jnp.int32),
            pltpu.VMEM((4, 8), F32),
            pltpu.SemaphoreType.DMA((3,)),
        ],
        compiler_params=pltpu.CompilerParams(vmem_limit_bytes=4 * MIB),
        name="pack",
    )(expert, in_hbm(tokens), in_hbm(ids), in_hbm(weights))


def expert_lanes(expert, shape, dim):
    lane = lax.broadcasted_iota(jnp.int32, shape, dim)
    return (lane < 64) & (lane % 32 == expert)


def select_kernel(starts, loads, expert_ref, *refs):
    refs = list(refs)
    blocks = [refs.pop(0) for _ in range(4)]
    sources = [refs.pop(0) for _ in range(loads)]
    del refs[0]
    mine_ref, sent_refs, targets = refs[0], refs[1 : 1 + len(starts)], refs[1 + len(starts) : -2]
    pick, sem = refs[-2:]
    copies = [pltpu.make_async_copy(a, b, sem) for a, b in zip(sources, targets)]
    for copy in copies:
        copy.start()
    own = expert_ref[0]
    turn = lax.broadcasted_iota(jnp.int32, (8, EXT), 0)
    experts = jnp.where(turn == 0, own, own ^ 1)
    wanted = jnp.where(expert_lanes(experts, (8, EXT), 1) & (turn < 2), 1.0, 0.0).astype(BF16)
    ext = jnp.concatenate([ref[:, HALF:] for ref in blocks], axis=0)
    route = lax.dot_general(wanted, ext, (((1,), (1,)), ((), ())), preferred_element_type=F32)
    chosen = route > 0
    first = lax.broadcasted_iota(jnp.int32, (PART, PART), 0)
    second = lax.broadcasted_iota(jnp.int32, (PART, PART), 1)
    earlier = jnp.where((first // 4 == second // 4) & (first < second), 1.0, 0.0).astype(BF16)
    rank = jnp.dot(jnp.where(chosen, 1.0, 0.0).astype(BF16), earlier, preferred_element_type=F32)
    column = lax.broadcasted_iota(jnp.int32, (8, PART), 1)
    place = jnp.where(chosen, column // 8 * 2 + rank.astype(jnp.int32), -1)
    row = lax.broadcasted_iota(jnp.int32, (SEL, PART), 0)
    is_left = lax.broadcasted_iota(jnp.int32, (SEL, PART), 1) % 8 < 4
    for e in range(2):
        hit = place[e : e + 1, :] == row
        pick[e * SEL : (e + 1) * SEL, :] = jnp.where(hit & is_left, 1.0, 0.0).astype(BF16)
        pick[(2 + e) * SEL : (3 + e) * SEL, :] = jnp.where(hit & ~is_left, 1.0, 0.0).astype(BF16)

    def put_sent(column, value):
        done = 0
        while done < value.shape[1]:
            piece = max(i for i, start in enumerate(starts) if start <= column + done)
            at = column + done - starts[piece]
            size = min(value.shape[1] - done, sent_refs[piece].shape[1] - at)
            sent_refs[piece][:, at : at + size] = value[:, done : done + size]
            done += size

    for n in range(0, HALF, 512):
        x = jnp.concatenate([ref[:, n : n + 512] for ref in blocks], axis=0)
        value = jnp.dot(pick[...], x, preferred_element_type=F32).astype(BF16)
        mine_ref[:, n : n + 512] = value[:SEL]
        put_sent(n, value[SEL : 2 * SEL])
        mine_ref[:, HALF + n : HALF + n + 512] = value[2 * SEL : 3 * SEL]
        put_sent(HALF + n, value[3 * SEL :])
    value = jnp.dot(pick[: 2 * SEL, :], ext, preferred_element_type=F32).astype(BF16)
    mine_ref[:, D:] = value[:SEL]
    put_sent(D, value[SEL:])
    for copy in copies:
        copy.wait()


def select(expert, blocks, after, starts, loads=()):
    widths = [end - start for start, end in zip(starts, starts[1:] + (D + EXT,))]
    return pl.pallas_call(
        functools.partial(select_kernel, starts, len(loads)),
        out_shape=[jax.ShapeDtypeStruct((SEL, width), BF16) for width in [D + EXT] + widths]
        + [jax.ShapeDtypeStruct(load.shape, load.dtype) for load in loads],
        in_specs=[SMEM] + [VMEM] * 4 + [HBM] * len(loads) + [ANY],
        out_specs=[VMEM] * (1 + len(starts) + len(loads)),
        scratch_shapes=[pltpu.VMEM((PART, PART), BF16), pltpu.SemaphoreType.DMA],
        compiler_params=SMALL,
        cost_estimate=BRIEF,
        name="select",
    )(expert, *blocks, *[in_hbm(load) for load in loads], after)


def hidden_kernel(starts, expert_ref, mine_ref, *refs):
    theirs_refs = refs[: len(starts)]
    gate_ref, up_ref = refs[len(starts) : len(starts) + 2]
    hidden, gate_sum, up_sum = refs[len(starts) + 3 :]

    def rows(low, high):
        piece = max(i for i, start in enumerate(starts) if start <= low)
        theirs = theirs_refs[piece][:, low - starts[piece] : high - starts[piece]]
        return jnp.concatenate([mine_ref[:, low:high], theirs], axis=0)

    for low, high in STEPS:
        x = rows(low, high)
        gate = jnp.dot(x, gate_ref[0, low:high, :], preferred_element_type=F32)
        up = jnp.dot(x, up_ref[0, low:high, :], preferred_element_type=F32)
        gate_sum[...] = gate if low == 0 else gate_sum[...] + gate
        up_sum[...] = up if low == 0 else up_sum[...] + up
    lanes = expert_lanes(expert_ref[0], (2 * SEL, EXT), 1)
    scale = jnp.sum(jnp.where(lanes, rows(D, D + EXT).astype(F32), 0.0), axis=1, keepdims=True)
    v = gate_sum[...]
    hidden[...] = (v / (1.0 + jnp.exp(-v)) * up_sum[...] * scale).astype(BF16)


def hidden_units(expert, mine, theirs, gate, up, after, starts):
    return pl.pallas_call(
        functools.partial(hidden_kernel, starts),
        out_shape=jax.ShapeDtypeStruct((2 * SEL, 512), BF16),
        in_specs=[SMEM] + [VMEM] * (3 + len(starts)) + [ANY],
        out_specs=VMEM,
        scratch_shapes=[pltpu.VMEM((2 * SEL, 512), F32)] * 2,
        compiler_params=SMALL,
        cost_estimate=BRIEF,
        name="hidden",
    )(expert, mine, *theirs, gate, up, after)


def down_kernel(hidden_ref, down_ref, after_ref, mine_ref, theirs_ref):
    del after_ref
    for n in range(0, D, 1024):
        block = slice(n, n + 1024)
        value = jnp.dot(hidden_ref[...], down_ref[0, :, block], preferred_element_type=F32).astype(BF16)
        mine_ref[:, block] = value[:SEL]
        theirs_ref[:, block] = value[SEL:]


def down_rows(hidden, down, after):
    return pl.pallas_call(
        down_kernel,
        out_shape=[jax.ShapeDtypeStruct((SEL, D), BF16)] * 2,
        in_specs=[VMEM, VMEM, ANY],
        out_specs=[VMEM, VMEM],
        compiler_params=SMALL,
        cost_estimate=BRIEF,
        name="down",
    )(hidden, down, after)


def spread_kernel(expert_ref, *refs):
    refs = list(refs)
    exts = [refs.pop(0) for _ in range(4)]
    mine_ref, theirs_ref = refs[:2]
    outs = [refs[3 + i] for i in range(4)]
    place_scr = refs[7]
    own = expert_ref[0]
    turn = lax.broadcasted_iota(jnp.int32, (EXT, EXT), 1)
    experts = jnp.where(turn == 0, own, own ^ 1)
    wanted = jnp.where(expert_lanes(experts, (EXT, EXT), 0) & (turn < 2), 1.0, 0.0).astype(BF16)
    ext = jnp.concatenate([ref[:, HALF:] for ref in exts], axis=0)
    chosen = jnp.dot(ext, wanted, preferred_element_type=F32) > 0
    first = lax.broadcasted_iota(jnp.int32, (PART, PART), 0)
    second = lax.broadcasted_iota(jnp.int32, (PART, PART), 1)
    earlier = jnp.where((first // 4 == second // 4) & (second < first), 1.0, 0.0).astype(BF16)
    rank = jnp.dot(earlier, jnp.where(chosen, 1.0, 0.0).astype(BF16), preferred_element_type=F32)
    token = lax.broadcasted_iota(jnp.int32, (PART, EXT), 0)
    place = jnp.where(chosen, token // 8 * 2 + rank.astype(jnp.int32), -1)
    column = lax.broadcasted_iota(jnp.int32, (PART, 2 * SEL), 1)
    hit = jnp.where(column < SEL, place[:, 0:1], place[:, 1:2]) == column % SEL
    is_left = lax.broadcasted_iota(jnp.int32, (PART, 2 * SEL), 0) % 8 < 4
    place_scr[:, : 2 * SEL] = jnp.where(hit & is_left, 1.0, 0.0).astype(BF16)
    place_scr[:, 2 * SEL :] = jnp.where(hit & ~is_left, 1.0, 0.0).astype(BF16)
    for n in range(0, HALF, 512):
        left, right = slice(n, n + 512), slice(HALF + n, HALF + n + 512)
        y = jnp.concatenate([mine_ref[:, left], theirs_ref[:, left], mine_ref[:, right], theirs_ref[:, right]], axis=0)
        value = jnp.dot(place_scr[...], y, preferred_element_type=F32).astype(BF16)
        for i in range(4):
            outs[i][:, left] = value[i * BLOCK : (i + 1) * BLOCK]


def spread(expert, blocks, mine, theirs, after):
    return pl.pallas_call(
        spread_kernel,
        out_shape=[jax.ShapeDtypeStruct((BLOCK, HALF), BF16)] * 4,
        in_specs=[SMEM] + [VMEM] * 6 + [ANY],
        out_specs=[VMEM] * 4,
        scratch_shapes=[pltpu.VMEM((PART, 4 * SEL), BF16)],
        compiler_params=SMALL,
        cost_estimate=BRIEF,
        name="spread",
    )(expert, *blocks, mine, theirs, after)


def add(*terms):
    total = terms[0].astype(F32)
    for term in terms[1:]:
        total += term.astype(F32)
    return total.astype(BF16)


def finish_kernel(parts_ref, out_ref):
    total = parts_ref[0].astype(F32)
    for i in range(1, 8):
        total += parts_ref[i].astype(F32)
    out_ref[:, :HALF] = total[:4].astype(BF16)
    out_ref[:, HALF:] = total[4:].astype(BF16)


def finish(parts):
    return pl.pallas_call(
        finish_kernel,
        out_shape=jax.ShapeDtypeStruct((4, D), BF16),
        in_specs=[VMEM],
        out_specs=VMEM,
        compiler_params=SMALL,
        name="finish",
    )(parts)


def body(tokens, ids, weights, gate, up, down):
    expert = lax.axis_index("dev").astype(jnp.int32).reshape(1)
    own = swap_near(pack(expert, tokens, ids, weights)).reshape(BLOCK, WIDE)
    x, y, z = swap_far(own, 0), swap_far(own, 1), swap_far(own, 2)
    xyz = swap_far(own, 3)
    xy, yz, zx = swap_far(y, 0), swap_far(z, 1), swap_far(x, 2)
    near = (x, y, z, own)
    mine_near, *sent, up = select(expert, near, own, THREE, (up,))
    xyz, yz, *sent = lax.optimization_barrier((xyz, yz, *sent))
    got_near = [to_sibling(piece) for piece in sent]
    xy, zx, *got_near = lax.optimization_barrier((xy, zx, *got_near))
    far = (xy, zx, yz, xyz)
    mine_far, sent = select(expert, far, own, ONE)
    got_far = [to_sibling(sent)]
    hidden_near = hidden_units(expert, mine_near, got_near, gate, up, mine_far, THREE)
    result_near, theirs = down_rows(hidden_near, down, own)
    returned_near = to_sibling(theirs)
    hidden_far = hidden_units(expert, mine_far, got_far, gate, up, result_near, ONE)
    result, theirs = down_rows(hidden_far, down, own)
    returned = to_sibling(theirs)
    y_x, y_y, y_z, y_own = spread(expert, near, result_near, returned_near, result)
    y_xy, y_zx, y_yz, y_xyz = spread(expert, far, result, returned, y_own)
    at_x, at_y, at_z = swap_far(y_xy, 1), swap_far(y_yz, 2), swap_far(y_zx, 0)
    at_own = swap_far(y_xyz, 3)
    total = add(
        y_own,
        swap_far(add(y_x, at_x), 0),
        swap_far(add(y_y, at_y), 1),
        swap_far(add(y_z, at_z), 2),
        at_own,
    )
    return finish(swap_near(total.reshape(8, 8, HALF)))


def solution(mesh):
    in_specs = (
        P(AXES, None),
        P(AXES, None),
        P(AXES, None),
        P("dev", None, "grp"),
        P("dev", None, "grp"),
        P("dev", "grp", None),
    )
    return jax.shard_map(body, mesh=mesh, in_specs=in_specs, out_specs=P(AXES, None), check_vma=False)
```

```python
import functools

import jax
import jax.numpy as jnp
from jax import lax
from jax.experimental import pallas as pl
from jax.experimental.pallas import tpu as pltpu
from jax.sharding import PartitionSpec as P

AXES = ("grp", "dev")
D = 7168
HALF = D // 2
EXT = 128
WIDE = HALF + EXT
BLOCK = 64
PART = 4 * BLOCK
SEL = 64
F32 = jnp.float32
BF16 = jnp.bfloat16
MIB = 1 << 20
VMEM = pl.BlockSpec(memory_space=pltpu.VMEM)
SMEM = pl.BlockSpec(memory_space=pltpu.SMEM)
HBM = pl.BlockSpec(memory_space=pltpu.HBM)
ANY = pl.BlockSpec(memory_space=pl.ANY)
SMALL = pltpu.CompilerParams(vmem_limit_bytes=8 * MIB)


STEPS = ((0, HALF), (HALF, D))
TWO = (0, HALF)
ONE = (0,)
BRIEF = pl.CostEstimate(flops=1000, bytes_accessed=1000, transcendentals=0)


def flat(z, x, y, c):
    return ((z * 4 + x) * 4 + y) * 2 + c


def near_groups():
    seen, groups = set(), []
    for z in range(4):
        for x in range(4):
            for y in range(4):
                for c in range(2):
                    if flat(z, x, y, c) in seen:
                        continue
                    m = 3 if c else 1
                    members = [
                        flat(z ^ (m * i), x ^ (m * j), y ^ (m * k), c)
                        for i in (0, 1) for j in (0, 1) for k in (0, 1)
                    ]
                    seen.update(members)
                    groups.append(members)
    return groups


def far_pairs(*axes):
    pairs = []
    for z in range(4):
        for x in range(4):
            for y in range(4):
                for c in range(2):
                    at = [x, z, y]
                    for axis in axes:
                        at[axis] ^= 1 if c else 3
                    pairs.append((flat(z, x, y, c), flat(at[1], at[0], at[2], c)))
    return pairs


NEAR = near_groups()
FAR = [far_pairs(0), far_pairs(1), far_pairs(2), far_pairs(0, 1, 2)]


def swap_near(values):
    return lax.all_to_all(values, AXES, 0, 0, axis_index_groups=NEAR, tiled=True)


def swap_far(values, axis):
    return lax.ppermute(values, AXES, FAR[axis])


def both_cores(values):
    return lax.all_gather(values, "dev", axis_index_groups=[[i, i + 1] for i in range(0, 32, 2)])


def to_sibling(values):
    return lax.ppermute(values, "dev", [(i, i ^ 1) for i in range(32)])


def pack_kernel(expert_ref, tokens_hbm, ids_hbm, weights_hbm, out_ref, tokens_ref, ids_ref, weights_ref, sems):
    del expert_ref
    pairs = ((tokens_hbm, tokens_ref), (ids_hbm, ids_ref), (weights_hbm, weights_ref))
    copies = [pltpu.make_async_copy(source, target, sems.at[i]) for i, (source, target) in enumerate(pairs)]
    for copy in copies:
        copy.start()
    for copy in copies:
        copy.wait()
    lane = lax.broadcasted_iota(jnp.int32, (4, EXT), 1)
    dense = jnp.zeros((4, EXT), F32)
    for k in range(8):
        dense += jnp.where(ids_ref[:, k : k + 1] == lane % 32, weights_ref[:, k : k + 1], 0.0)
    high = dense.astype(BF16).astype(F32)
    route = jnp.where(lane < 32, high, jnp.where(lane < 64, dense - high, 0.0))
    rows = tokens_ref[...].astype(F32)
    left = jnp.concatenate([rows[:, :HALF], route], axis=1)
    right = jnp.concatenate([rows[:, HALF:], route], axis=1)
    block = jnp.concatenate([left, right], axis=0).astype(BF16)
    for i in range(8):
        out_ref[i] = block


def in_hbm(values):
    return pltpu.with_memory_space_constraint(values, pltpu.HBM)


def pack(expert, tokens, ids, weights):
    return pl.pallas_call(
        pack_kernel,
        out_shape=jax.ShapeDtypeStruct((8, 8, WIDE), BF16),
        in_specs=[SMEM, HBM, HBM, HBM],
        out_specs=VMEM,
        scratch_shapes=[
            pltpu.VMEM((4, D), BF16),
            pltpu.VMEM((4, 8), jnp.int32),
            pltpu.VMEM((4, 8), F32),
            pltpu.SemaphoreType.DMA((3,)),
        ],
        compiler_params=pltpu.CompilerParams(vmem_limit_bytes=4 * MIB),
        name="pack",
    )(expert, in_hbm(tokens), in_hbm(ids), in_hbm(weights))


def expert_lanes(expert, shape, dim):
    lane = lax.broadcasted_iota(jnp.int32, shape, dim)
    return (lane < 64) & (lane % 32 == expert)


def select_kernel(starts, loads, expert_ref, *refs):
    refs = list(refs)
    blocks = [refs.pop(0) for _ in range(4)]
    sources = [refs.pop(0) for _ in range(loads)]
    del refs[0]
    mine_ref, sent_refs, targets = refs[0], refs[1 : 1 + len(starts)], refs[1 + len(starts) : -2]
    pick, sem = refs[-2:]
    copies = [pltpu.make_async_copy(a, b, sem) for a, b in zip(sources, targets)]
    for copy in copies:
        copy.start()
    own = expert_ref[0]
    turn = lax.broadcasted_iota(jnp.int32, (8, EXT), 0)
    experts = jnp.where(turn == 0, own, own ^ 1)
    wanted = jnp.where(expert_lanes(experts, (8, EXT), 1) & (turn < 2), 1.0, 0.0).astype(BF16)
    ext = jnp.concatenate([ref[:, HALF:] for ref in blocks], axis=0)
    route = lax.dot_general(wanted, ext, (((1,), (1,)), ((), ())), preferred_element_type=F32)
    chosen = route > 0
    first = lax.broadcasted_iota(jnp.int32, (PART, PART), 0)
    second = lax.broadcasted_iota(jnp.int32, (PART, PART), 1)
    earlier = jnp.where((first // 4 == second // 4) & (first < second), 1.0, 0.0).astype(BF16)
    rank = jnp.dot(jnp.where(chosen, 1.0, 0.0).astype(BF16), earlier, preferred_element_type=F32)
    column = lax.broadcasted_iota(jnp.int32, (8, PART), 1)
    place = jnp.where(chosen, column // 8 * 2 + rank.astype(jnp.int32), -1)
    row = lax.broadcasted_iota(jnp.int32, (SEL, PART), 0)
    is_left = lax.broadcasted_iota(jnp.int32, (SEL, PART), 1) % 8 < 4
    for e in range(2):
        hit = place[e : e + 1, :] == row
        pick[e * SEL : (e + 1) * SEL, :] = jnp.where(hit & is_left, 1.0, 0.0).astype(BF16)
        pick[(2 + e) * SEL : (3 + e) * SEL, :] = jnp.where(hit & ~is_left, 1.0, 0.0).astype(BF16)

    def put_sent(column, value):
        done = 0
        while done < value.shape[1]:
            piece = max(i for i, start in enumerate(starts) if start <= column + done)
            at = column + done - starts[piece]
            size = min(value.shape[1] - done, sent_refs[piece].shape[1] - at)
            sent_refs[piece][:, at : at + size] = value[:, done : done + size]
            done += size

    for n in range(0, HALF, 512):
        x = jnp.concatenate([ref[:, n : n + 512] for ref in blocks], axis=0)
        value = jnp.dot(pick[...], x, preferred_element_type=F32).astype(BF16)
        mine_ref[:, n : n + 512] = value[:SEL]
        put_sent(n, value[SEL : 2 * SEL])
        mine_ref[:, HALF + n : HALF + n + 512] = value[2 * SEL : 3 * SEL]
        put_sent(HALF + n, value[3 * SEL :])
    value = jnp.dot(pick[: 2 * SEL, :], ext, preferred_element_type=F32).astype(BF16)
    mine_ref[:, D:] = value[:SEL]
    put_sent(D, value[SEL:])
    for copy in copies:
        copy.wait()


def select(expert, blocks, after, starts, loads=()):
    widths = [end - start for start, end in zip(starts, starts[1:] + (D + EXT,))]
    return pl.pallas_call(
        functools.partial(select_kernel, starts, len(loads)),
        out_shape=[jax.ShapeDtypeStruct((SEL, width), BF16) for width in [D + EXT] + widths]
        + [jax.ShapeDtypeStruct(load.shape, load.dtype) for load in loads],
        in_specs=[SMEM] + [VMEM] * 4 + [HBM] * len(loads) + [ANY],
        out_specs=[VMEM] * (1 + len(starts) + len(loads)),
        scratch_shapes=[pltpu.VMEM((PART, PART), BF16), pltpu.SemaphoreType.DMA],
        compiler_params=SMALL,
        cost_estimate=BRIEF,
        name="select",
    )(expert, *blocks, *[in_hbm(load) for load in loads], after)


def hidden_kernel(starts, expert_ref, mine_ref, *refs):
    theirs_refs = refs[: len(starts)]
    gate_ref, up_ref = refs[len(starts) : len(starts) + 2]
    hidden, gate_sum, up_sum = refs[len(starts) + 3 :]

    def rows(low, high):
        piece = max(i for i, start in enumerate(starts) if start <= low)
        columns = slice(low - starts[piece], high - starts[piece])
        if len(starts) > 1:
            theirs = theirs_refs[piece][1 - expert_ref[0] % 2, :, columns]
        else:
            theirs = theirs_refs[piece][:, columns]
        return jnp.concatenate([mine_ref[:, low:high], theirs], axis=0)

    for low, high in STEPS:
        x = rows(low, high)
        gate = jnp.dot(x, gate_ref[0, low:high, :], preferred_element_type=F32)
        up = jnp.dot(x, up_ref[0, low:high, :], preferred_element_type=F32)
        gate_sum[...] = gate if low == 0 else gate_sum[...] + gate
        up_sum[...] = up if low == 0 else up_sum[...] + up
    lanes = expert_lanes(expert_ref[0], (2 * SEL, EXT), 1)
    scale = jnp.sum(jnp.where(lanes, rows(D, D + EXT).astype(F32), 0.0), axis=1, keepdims=True)
    v = gate_sum[...]
    hidden[...] = (v / (1.0 + jnp.exp(-v)) * up_sum[...] * scale).astype(BF16)


def hidden_units(expert, mine, theirs, gate, up, after, starts):
    return pl.pallas_call(
        functools.partial(hidden_kernel, starts),
        out_shape=jax.ShapeDtypeStruct((2 * SEL, 512), BF16),
        in_specs=[SMEM] + [VMEM] * (3 + len(starts)) + [ANY],
        out_specs=VMEM,
        scratch_shapes=[pltpu.VMEM((2 * SEL, 512), F32)] * 2,
        compiler_params=SMALL,
        cost_estimate=BRIEF,
        name="hidden",
    )(expert, mine, *theirs, gate, up, after)


def down_kernel(hidden_ref, down_ref, after_ref, mine_ref, theirs_ref):
    del after_ref
    for n in range(0, D, 1024):
        block = slice(n, n + 1024)
        value = jnp.dot(hidden_ref[...], down_ref[0, :, block], preferred_element_type=F32).astype(BF16)
        mine_ref[:, block] = value[:SEL]
        theirs_ref[:, block] = value[SEL:]


def down_rows(hidden, down, after):
    return pl.pallas_call(
        down_kernel,
        out_shape=[jax.ShapeDtypeStruct((SEL, D), BF16)] * 2,
        in_specs=[VMEM, VMEM, ANY],
        out_specs=[VMEM, VMEM],
        compiler_params=SMALL,
        cost_estimate=BRIEF,
        name="down",
    )(hidden, down, after)


def spread_kernel(expert_ref, *refs):
    refs = list(refs)
    exts = [refs.pop(0) for _ in range(4)]
    mine_ref, theirs_ref = refs[:2]
    outs = [refs[3 + i] for i in range(4)]
    place_scr = refs[7]
    own = expert_ref[0]
    turn = lax.broadcasted_iota(jnp.int32, (EXT, EXT), 1)
    experts = jnp.where(turn == 0, own, own ^ 1)
    wanted = jnp.where(expert_lanes(experts, (EXT, EXT), 0) & (turn < 2), 1.0, 0.0).astype(BF16)
    ext = jnp.concatenate([ref[:, HALF:] for ref in exts], axis=0)
    chosen = jnp.dot(ext, wanted, preferred_element_type=F32) > 0
    first = lax.broadcasted_iota(jnp.int32, (PART, PART), 0)
    second = lax.broadcasted_iota(jnp.int32, (PART, PART), 1)
    earlier = jnp.where((first // 4 == second // 4) & (second < first), 1.0, 0.0).astype(BF16)
    rank = jnp.dot(earlier, jnp.where(chosen, 1.0, 0.0).astype(BF16), preferred_element_type=F32)
    token = lax.broadcasted_iota(jnp.int32, (PART, EXT), 0)
    place = jnp.where(chosen, token // 8 * 2 + rank.astype(jnp.int32), -1)
    column = lax.broadcasted_iota(jnp.int32, (PART, 2 * SEL), 1)
    hit = jnp.where(column < SEL, place[:, 0:1], place[:, 1:2]) == column % SEL
    is_left = lax.broadcasted_iota(jnp.int32, (PART, 2 * SEL), 0) % 8 < 4
    place_scr[:, : 2 * SEL] = jnp.where(hit & is_left, 1.0, 0.0).astype(BF16)
    place_scr[:, 2 * SEL :] = jnp.where(hit & ~is_left, 1.0, 0.0).astype(BF16)
    for n in range(0, HALF, 512):
        left, right = slice(n, n + 512), slice(HALF + n, HALF + n + 512)
        y = jnp.concatenate([mine_ref[:, left], theirs_ref[:, left], mine_ref[:, right], theirs_ref[:, right]], axis=0)
        value = jnp.dot(place_scr[...], y, preferred_element_type=F32).astype(BF16)
        for i in range(4):
            outs[i][:, left] = value[i * BLOCK : (i + 1) * BLOCK]


def spread(expert, blocks, mine, theirs, after):
    return pl.pallas_call(
        spread_kernel,
        out_shape=[jax.ShapeDtypeStruct((BLOCK, HALF), BF16)] * 4,
        in_specs=[SMEM] + [VMEM] * 6 + [ANY],
        out_specs=[VMEM] * 4,
        scratch_shapes=[pltpu.VMEM((PART, 4 * SEL), BF16)],
        compiler_params=SMALL,
        cost_estimate=BRIEF,
        name="spread",
    )(expert, *blocks, mine, theirs, after)


def add(*terms):
    total = terms[0].astype(F32)
    for term in terms[1:]:
        total += term.astype(F32)
    return total.astype(BF16)


def finish_kernel(parts_ref, out_ref):
    total = parts_ref[0].astype(F32)
    for i in range(1, 8):
        total += parts_ref[i].astype(F32)
    out_ref[:, :HALF] = total[:4].astype(BF16)
    out_ref[:, HALF:] = total[4:].astype(BF16)


def finish(parts):
    return pl.pallas_call(
        finish_kernel,
        out_shape=jax.ShapeDtypeStruct((4, D), BF16),
        in_specs=[VMEM],
        out_specs=VMEM,
        compiler_params=SMALL,
        name="finish",
    )(parts)


def body(tokens, ids, weights, gate, up, down):
    expert = lax.axis_index("dev").astype(jnp.int32).reshape(1)
    own = swap_near(pack(expert, tokens, ids, weights)).reshape(BLOCK, WIDE)
    x, y, z = swap_far(own, 0), swap_far(own, 1), swap_far(own, 2)
    xyz = swap_far(own, 3)
    xy, yz, zx = swap_far(y, 0), swap_far(z, 1), swap_far(x, 2)
    near = (x, y, z, own)
    mine_near, *sent, up = select(expert, near, own, TWO, (up,))
    got_near = [both_cores(piece) for piece in sent]
    xy, yz, zx, xyz, *got_near = lax.optimization_barrier((xy, yz, zx, xyz, *got_near))
    far = (xy, zx, yz, xyz)
    mine_far, sent = select(expert, far, own, ONE)
    got_far = [to_sibling(sent)]
    hidden_near = hidden_units(expert, mine_near, got_near, gate, up, mine_far, TWO)
    hidden_far = hidden_units(expert, mine_far, got_far, gate, up, hidden_near, ONE)
    result, theirs = down_rows(hidden_far, down, own)
    returned = to_sibling(theirs)
    result_near, theirs = down_rows(hidden_near, down, result)
    returned_near = to_sibling(theirs)
    y_xy, y_zx, y_yz, y_xyz = spread(expert, far, result, returned, result_near)
    at_x, at_y, at_z = swap_far(y_xy, 1), swap_far(y_yz, 2), swap_far(y_zx, 0)
    at_own = swap_far(y_xyz, 3)
    y_x, y_y, y_z, y_own = spread(expert, near, result_near, returned_near, y_xyz)
    total = add(
        y_own,
        swap_far(add(y_x, at_x), 0),
        swap_far(add(y_y, at_y), 1),
        swap_far(add(y_z, at_z), 2),
        at_own,
    )
    return finish(swap_near(total.reshape(8, 8, HALF)))


def solution(mesh):
    in_specs = (
        P(AXES, None),
        P(AXES, None),
        P(AXES, None),
        P("dev", None, "grp"),
        P("dev", None, "grp"),
        P("dev", "grp", None),
    )
    return jax.shard_map(body, mesh=mesh, in_specs=in_specs, out_specs=P(AXES, None), check_vma=False)
```

```python
import functools

import jax
import jax.numpy as jnp
from jax import lax
from jax.experimental import pallas as pl
from jax.experimental.pallas import tpu as pltpu
from jax.sharding import PartitionSpec as P

AXES = ("grp", "dev")
D = 7168
HALF = D // 2
EXT = 128
WIDE = HALF + EXT
BLOCK = 64
PART = 4 * BLOCK
SEL = 64
F32 = jnp.float32
BF16 = jnp.bfloat16
MIB = 1 << 20
VMEM = pl.BlockSpec(memory_space=pltpu.VMEM)
SMEM = pl.BlockSpec(memory_space=pltpu.SMEM)
HBM = pl.BlockSpec(memory_space=pltpu.HBM)
ANY = pl.BlockSpec(memory_space=pl.ANY)
SMALL = pltpu.CompilerParams(vmem_limit_bytes=8 * MIB)


STEPS = ((0, HALF), (HALF, D))
TWO = (0, HALF)
ONE = (0,)
BRIEF = pl.CostEstimate(flops=1000, bytes_accessed=1000, transcendentals=0)


def flat(z, x, y, c):
    return ((z * 4 + x) * 4 + y) * 2 + c


def partner(z, x, y, c, axes, near):
    at = [z, x, y]
    for axis in axes:
        at[axis] ^= 1 if near == ((axis == 1) == (c == 1)) else 3
    return flat(*at, c)


def near_groups():
    seen, groups = set(), []
    for z in range(4):
        for x in range(4):
            for y in range(4):
                for c in range(2):
                    if flat(z, x, y, c) in seen:
                        continue
                    members = [
                        partner(z, x, y, c, [axis for axis, cross in enumerate((i, j, k)) if cross], True)
                        for i in (0, 1) for j in (0, 1) for k in (0, 1)
                    ]
                    seen.update(members)
                    groups.append(members)
    return groups


def far_pairs(*axes):
    pairs = []
    for z in range(4):
        for x in range(4):
            for y in range(4):
                for c in range(2):
                    pairs.append((flat(z, x, y, c), partner(z, x, y, c, [(1, 0, 2)[axis] for axis in axes], False)))
    return pairs


NEAR = near_groups()
FAR = [far_pairs(0), far_pairs(1), far_pairs(2), far_pairs(0, 1, 2)]


def swap_near(values):
    return lax.all_to_all(values, AXES, 0, 0, axis_index_groups=NEAR, tiled=True)


def swap_far(values, axis):
    return lax.ppermute(values, AXES, FAR[axis])


def both_cores(values):
    return lax.all_gather(values, "dev", axis_index_groups=[[i, i + 1] for i in range(0, 32, 2)])


def to_sibling(values):
    return lax.ppermute(values, "dev", [(i, i ^ 1) for i in range(32)])


def pack_kernel(expert_ref, tokens_hbm, ids_hbm, weights_hbm, out_ref, tokens_ref, ids_ref, weights_ref, sems):
    del expert_ref
    pairs = ((tokens_hbm, tokens_ref), (ids_hbm, ids_ref), (weights_hbm, weights_ref))
    copies = [pltpu.make_async_copy(source, target, sems.at[i]) for i, (source, target) in enumerate(pairs)]
    for copy in copies:
        copy.start()
    for copy in copies:
        copy.wait()
    lane = lax.broadcasted_iota(jnp.int32, (4, EXT), 1)
    dense = jnp.zeros((4, EXT), F32)
    for k in range(8):
        dense += jnp.where(ids_ref[:, k : k + 1] == lane % 32, weights_ref[:, k : k + 1], 0.0)
    high = dense.astype(BF16).astype(F32)
    route = jnp.where(lane < 32, high, jnp.where(lane < 64, dense - high, 0.0))
    rows = tokens_ref[...].astype(F32)
    left = jnp.concatenate([rows[:, :HALF], route], axis=1)
    right = jnp.concatenate([rows[:, HALF:], route], axis=1)
    block = jnp.concatenate([left, right], axis=0).astype(BF16)
    for i in range(8):
        out_ref[i] = block


def in_hbm(values):
    return pltpu.with_memory_space_constraint(values, pltpu.HBM)


def pack(expert, tokens, ids, weights):
    return pl.pallas_call(
        pack_kernel,
        out_shape=jax.ShapeDtypeStruct((8, 8, WIDE), BF16),
        in_specs=[SMEM, HBM, HBM, HBM],
        out_specs=VMEM,
        scratch_shapes=[
            pltpu.VMEM((4, D), BF16),
            pltpu.VMEM((4, 8), jnp.int32),
            pltpu.VMEM((4, 8), F32),
            pltpu.SemaphoreType.DMA((3,)),
        ],
        compiler_params=pltpu.CompilerParams(vmem_limit_bytes=4 * MIB),
        name="pack",
    )(expert, in_hbm(tokens), in_hbm(ids), in_hbm(weights))


def expert_lanes(expert, shape, dim):
    lane = lax.broadcasted_iota(jnp.int32, shape, dim)
    return (lane < 64) & (lane % 32 == expert)


def select_kernel(starts, loads, expert_ref, *refs):
    refs = list(refs)
    blocks = [refs.pop(0) for _ in range(4)]
    sources = [refs.pop(0) for _ in range(loads)]
    del refs[0]
    mine_ref, sent_refs, targets = refs[0], refs[1 : 1 + len(starts)], refs[1 + len(starts) : -2]
    pick, sem = refs[-2:]
    copies = [pltpu.make_async_copy(a, b, sem) for a, b in zip(sources, targets)]
    for copy in copies:
        copy.start()
    own = expert_ref[0]
    turn = lax.broadcasted_iota(jnp.int32, (8, EXT), 0)
    experts = jnp.where(turn == 0, own, own ^ 1)
    wanted = jnp.where(expert_lanes(experts, (8, EXT), 1) & (turn < 2), 1.0, 0.0).astype(BF16)
    ext = jnp.concatenate([ref[:, HALF:] for ref in blocks], axis=0)
    route = lax.dot_general(wanted, ext, (((1,), (1,)), ((), ())), preferred_element_type=F32)
    chosen = route > 0
    first = lax.broadcasted_iota(jnp.int32, (PART, PART), 0)
    second = lax.broadcasted_iota(jnp.int32, (PART, PART), 1)
    earlier = jnp.where((first // 4 == second // 4) & (first < second), 1.0, 0.0).astype(BF16)
    rank = jnp.dot(jnp.where(chosen, 1.0, 0.0).astype(BF16), earlier, preferred_element_type=F32)
    column = lax.broadcasted_iota(jnp.int32, (8, PART), 1)
    place = jnp.where(chosen, column // 8 * 2 + rank.astype(jnp.int32), -1)
    row = lax.broadcasted_iota(jnp.int32, (SEL, PART), 0)
    is_left = lax.broadcasted_iota(jnp.int32, (SEL, PART), 1) % 8 < 4
    for e in range(2):
        hit = place[e : e + 1, :] == row
        pick[e * SEL : (e + 1) * SEL, :] = jnp.where(hit & is_left, 1.0, 0.0).astype(BF16)
        pick[(2 + e) * SEL : (3 + e) * SEL, :] = jnp.where(hit & ~is_left, 1.0, 0.0).astype(BF16)

    def put_sent(column, value):
        done = 0
        while done < value.shape[1]:
            piece = max(i for i, start in enumerate(starts) if start <= column + done)
            at = column + done - starts[piece]
            size = min(value.shape[1] - done, sent_refs[piece].shape[1] - at)
            sent_refs[piece][:, at : at + size] = value[:, done : done + size]
            done += size

    for n in range(0, HALF, 512):
        x = jnp.concatenate([ref[:, n : n + 512] for ref in blocks], axis=0)
        value = jnp.dot(pick[...], x, preferred_element_type=F32).astype(BF16)
        mine_ref[:, n : n + 512] = value[:SEL]
        put_sent(n, value[SEL : 2 * SEL])
        mine_ref[:, HALF + n : HALF + n + 512] = value[2 * SEL : 3 * SEL]
        put_sent(HALF + n, value[3 * SEL :])
    value = jnp.dot(pick[: 2 * SEL, :], ext, preferred_element_type=F32).astype(BF16)
    mine_ref[:, D:] = value[:SEL]
    put_sent(D, value[SEL:])
    for copy in copies:
        copy.wait()


def select(expert, blocks, after, starts, loads=()):
    widths = [end - start for start, end in zip(starts, starts[1:] + (D + EXT,))]
    return pl.pallas_call(
        functools.partial(select_kernel, starts, len(loads)),
        out_shape=[jax.ShapeDtypeStruct((SEL, width), BF16) for width in [D + EXT] + widths]
        + [jax.ShapeDtypeStruct(load.shape, load.dtype) for load in loads],
        in_specs=[SMEM] + [VMEM] * 4 + [HBM] * len(loads) + [ANY],
        out_specs=[VMEM] * (1 + len(starts) + len(loads)),
        scratch_shapes=[pltpu.VMEM((PART, PART), BF16), pltpu.SemaphoreType.DMA],
        compiler_params=SMALL,
        cost_estimate=BRIEF,
        name="select",
    )(expert, *blocks, *[in_hbm(load) for load in loads], after)


def hidden_kernel(starts, expert_ref, mine_ref, *refs):
    theirs_refs = refs[: len(starts)]
    gate_ref, up_ref = refs[len(starts) : len(starts) + 2]
    hidden, gate_sum, up_sum = refs[len(starts) + 3 :]

    def rows(low, high):
        piece = max(i for i, start in enumerate(starts) if start <= low)
        columns = slice(low - starts[piece], high - starts[piece])
        if len(starts) > 1:
            theirs = theirs_refs[piece][1 - expert_ref[0] % 2, :, columns]
        else:
            theirs = theirs_refs[piece][:, columns]
        return jnp.concatenate([mine_ref[:, low:high], theirs], axis=0)

    for low, high in STEPS:
        x = rows(low, high)
        gate = jnp.dot(x, gate_ref[0, low:high, :], preferred_element_type=F32)
        up = jnp.dot(x, up_ref[0, low:high, :], preferred_element_type=F32)
        gate_sum[...] = gate if low == 0 else gate_sum[...] + gate
        up_sum[...] = up if low == 0 else up_sum[...] + up
    lanes = expert_lanes(expert_ref[0], (2 * SEL, EXT), 1)
    scale = jnp.sum(jnp.where(lanes, rows(D, D + EXT).astype(F32), 0.0), axis=1, keepdims=True)
    v = gate_sum[...]
    hidden[...] = (v / (1.0 + jnp.exp(-v)) * up_sum[...] * scale).astype(BF16)


def hidden_units(expert, mine, theirs, gate, up, after, starts):
    return pl.pallas_call(
        functools.partial(hidden_kernel, starts),
        out_shape=jax.ShapeDtypeStruct((2 * SEL, 512), BF16),
        in_specs=[SMEM] + [VMEM] * (3 + len(starts)) + [ANY],
        out_specs=VMEM,
        scratch_shapes=[pltpu.VMEM((2 * SEL, 512), F32)] * 2,
        compiler_params=SMALL,
        cost_estimate=BRIEF,
        name="hidden",
    )(expert, mine, *theirs, gate, up, after)


def down_kernel(hidden_ref, down_ref, after_ref, mine_ref, theirs_ref):
    del after_ref
    for n in range(0, D, 1024):
        block = slice(n, n + 1024)
        value = jnp.dot(hidden_ref[...], down_ref[0, :, block], preferred_element_type=F32).astype(BF16)
        mine_ref[:, block] = value[:SEL]
        theirs_ref[:, block] = value[SEL:]


def down_rows(hidden, down, after):
    return pl.pallas_call(
        down_kernel,
        out_shape=[jax.ShapeDtypeStruct((SEL, D), BF16)] * 2,
        in_specs=[VMEM, VMEM, ANY],
        out_specs=[VMEM, VMEM],
        compiler_params=SMALL,
        cost_estimate=BRIEF,
        name="down",
    )(hidden, down, after)


def spread_kernel(expert_ref, *refs):
    refs = list(refs)
    exts = [refs.pop(0) for _ in range(4)]
    mine_ref, theirs_ref = refs[:2]
    outs = [refs[3 + i] for i in range(4)]
    place_scr = refs[7]
    own = expert_ref[0]
    turn = lax.broadcasted_iota(jnp.int32, (EXT, EXT), 1)
    experts = jnp.where(turn == 0, own, own ^ 1)
    wanted = jnp.where(expert_lanes(experts, (EXT, EXT), 0) & (turn < 2), 1.0, 0.0).astype(BF16)
    ext = jnp.concatenate([ref[:, HALF:] for ref in exts], axis=0)
    chosen = jnp.dot(ext, wanted, preferred_element_type=F32) > 0
    first = lax.broadcasted_iota(jnp.int32, (PART, PART), 0)
    second = lax.broadcasted_iota(jnp.int32, (PART, PART), 1)
    earlier = jnp.where((first // 4 == second // 4) & (second < first), 1.0, 0.0).astype(BF16)
    rank = jnp.dot(earlier, jnp.where(chosen, 1.0, 0.0).astype(BF16), preferred_element_type=F32)
    token = lax.broadcasted_iota(jnp.int32, (PART, EXT), 0)
    place = jnp.where(chosen, token // 8 * 2 + rank.astype(jnp.int32), -1)
    column = lax.broadcasted_iota(jnp.int32, (PART, 2 * SEL), 1)
    hit = jnp.where(column < SEL, place[:, 0:1], place[:, 1:2]) == column % SEL
    is_left = lax.broadcasted_iota(jnp.int32, (PART, 2 * SEL), 0) % 8 < 4
    place_scr[:, : 2 * SEL] = jnp.where(hit & is_left, 1.0, 0.0).astype(BF16)
    place_scr[:, 2 * SEL :] = jnp.where(hit & ~is_left, 1.0, 0.0).astype(BF16)
    for n in range(0, HALF, 512):
        left, right = slice(n, n + 512), slice(HALF + n, HALF + n + 512)
        y = jnp.concatenate([mine_ref[:, left], theirs_ref[:, left], mine_ref[:, right], theirs_ref[:, right]], axis=0)
        value = jnp.dot(place_scr[...], y, preferred_element_type=F32).astype(BF16)
        for i in range(4):
            outs[i][:, left] = value[i * BLOCK : (i + 1) * BLOCK]


def spread(expert, blocks, mine, theirs, after):
    return pl.pallas_call(
        spread_kernel,
        out_shape=[jax.ShapeDtypeStruct((BLOCK, HALF), BF16)] * 4,
        in_specs=[SMEM] + [VMEM] * 6 + [ANY],
        out_specs=[VMEM] * 4,
        scratch_shapes=[pltpu.VMEM((PART, 4 * SEL), BF16)],
        compiler_params=SMALL,
        cost_estimate=BRIEF,
        name="spread",
    )(expert, *blocks, mine, theirs, after)


def add(*terms):
    total = terms[0].astype(F32)
    for term in terms[1:]:
        total += term.astype(F32)
    return total.astype(BF16)


def finish_kernel(parts_ref, out_ref):
    total = parts_ref[0].astype(F32)
    for i in range(1, 8):
        total += parts_ref[i].astype(F32)
    out_ref[:, :HALF] = total[:4].astype(BF16)
    out_ref[:, HALF:] = total[4:].astype(BF16)


def finish(parts):
    return pl.pallas_call(
        finish_kernel,
        out_shape=jax.ShapeDtypeStruct((4, D), BF16),
        in_specs=[VMEM],
        out_specs=VMEM,
        compiler_params=SMALL,
        name="finish",
    )(parts)


def body(tokens, ids, weights, gate, up, down):
    expert = lax.axis_index("dev").astype(jnp.int32).reshape(1)
    own = swap_near(pack(expert, tokens, ids, weights)).reshape(BLOCK, WIDE)
    x, y, z = swap_far(own, 0), swap_far(own, 1), swap_far(own, 2)
    xyz = swap_far(own, 3)
    xy, yz, zx = swap_far(y, 0), swap_far(z, 1), swap_far(x, 2)
    near = (x, y, z, own)
    mine_near, *sent, up = select(expert, near, own, TWO, (up,))
    got_near = [both_cores(piece) for piece in sent]
    xy, yz, zx, xyz, *got_near = lax.optimization_barrier((xy, yz, zx, xyz, *got_near))
    far = (xy, zx, yz, xyz)
    mine_far, sent = select(expert, far, own, ONE)
    got_far = [to_sibling(sent)]
    hidden_near = hidden_units(expert, mine_near, got_near, gate, up, mine_far, TWO)
    hidden_far = hidden_units(expert, mine_far, got_far, gate, up, hidden_near, ONE)
    result, theirs = down_rows(hidden_far, down, own)
    returned = to_sibling(theirs)
    result_near, theirs = down_rows(hidden_near, down, result)
    returned_near = to_sibling(theirs)
    y_xy, y_zx, y_yz, y_xyz = spread(expert, far, result, returned, result_near)
    at_x, at_y, at_z = swap_far(y_xy, 1), swap_far(y_yz, 2), swap_far(y_zx, 0)
    at_own = swap_far(y_xyz, 3)
    y_x, y_y, y_z, y_own = spread(expert, near, result_near, returned_near, y_xyz)
    total = add(
        y_own,
        swap_far(add(y_x, at_x), 0),
        swap_far(add(y_y, at_y), 1),
        swap_far(add(y_z, at_z), 2),
        at_own,
    )
    return finish(swap_near(total.reshape(8, 8, HALF)))


def solution(mesh):
    in_specs = (
        P(AXES, None),
        P(AXES, None),
        P(AXES, None),
        P("dev", None, "grp"),
        P("dev", None, "grp"),
        P("dev", "grp", None),
    )
    return jax.shard_map(body, mesh=mesh, in_specs=in_specs, out_specs=P(AXES, None), check_vma=False)
```

```python
import functools

import jax
import jax.numpy as jnp
from jax import lax
from jax.experimental import pallas as pl
from jax.experimental.pallas import tpu as pltpu
from jax.sharding import PartitionSpec as P

AXES = ("grp", "dev")
D = 7168
HALF = D // 2
EXT = 128
WIDE = HALF + EXT
BLOCK = 64
PART = 4 * BLOCK
SEL = 64
F32 = jnp.float32
BF16 = jnp.bfloat16
MIB = 1 << 20
VMEM = pl.BlockSpec(memory_space=pltpu.VMEM)
SMEM = pl.BlockSpec(memory_space=pltpu.SMEM)
HBM = pl.BlockSpec(memory_space=pltpu.HBM)
ANY = pl.BlockSpec(memory_space=pl.ANY)
SMALL = pltpu.CompilerParams(vmem_limit_bytes=8 * MIB)


STEPS = ((0, HALF), (HALF, D))
TWO = (0, HALF)
ONE = (0,)
BRIEF = pl.CostEstimate(flops=1000, bytes_accessed=1000, transcendentals=0)


def flat(z, x, y, c):
    return ((z * 4 + x) * 4 + y) * 2 + c


def near_groups():
    seen, groups = set(), []
    for z in range(4):
        for x in range(4):
            for y in range(4):
                for c in range(2):
                    if flat(z, x, y, c) in seen:
                        continue
                    m = 3 if c else 1
                    members = [
                        flat(z ^ (m * i), x ^ (m * j), y ^ (m * k), c)
                        for i in (0, 1) for j in (0, 1) for k in (0, 1)
                    ]
                    seen.update(members)
                    groups.append(members)
    return groups


def far_pairs(*axes):
    pairs = []
    for z in range(4):
        for x in range(4):
            for y in range(4):
                for c in range(2):
                    at = [x, z, y]
                    for axis in axes:
                        at[axis] ^= 1 if c else 3
                    pairs.append((flat(z, x, y, c), flat(at[1], at[0], at[2], c)))
    return pairs


NEAR = near_groups()
FAR = [far_pairs(0), far_pairs(1), far_pairs(2), far_pairs(0, 1, 2)]


def swap_near(values):
    return lax.all_to_all(values, AXES, 0, 0, axis_index_groups=NEAR, tiled=True)


def swap_far(values, axis):
    return lax.ppermute(values, AXES, FAR[axis])


def both_cores(values):
    return lax.all_gather(values, "dev", axis_index_groups=[[i, i + 1] for i in range(0, 32, 2)])


def to_sibling(values):
    return lax.ppermute(values, "dev", [(i, i ^ 1) for i in range(32)])


def pack_kernel(expert_ref, tokens_hbm, ids_hbm, weights_hbm, out_ref, tokens_ref, ids_ref, weights_ref, sems):
    del expert_ref
    pairs = ((tokens_hbm, tokens_ref), (ids_hbm, ids_ref), (weights_hbm, weights_ref))
    copies = [pltpu.make_async_copy(source, target, sems.at[i]) for i, (source, target) in enumerate(pairs)]
    for copy in copies:
        copy.start()
    for copy in copies:
        copy.wait()
    lane = lax.broadcasted_iota(jnp.int32, (4, EXT), 1)
    dense = jnp.zeros((4, EXT), F32)
    for k in range(8):
        dense += jnp.where(ids_ref[:, k : k + 1] == lane % 32, weights_ref[:, k : k + 1], 0.0)
    high = dense.astype(BF16).astype(F32)
    route = jnp.where(lane < 32, high, jnp.where(lane < 64, dense - high, 0.0))
    rows = tokens_ref[...].astype(F32)
    left = jnp.concatenate([rows[:, :HALF], route], axis=1)
    right = jnp.concatenate([rows[:, HALF:], route], axis=1)
    block = jnp.concatenate([left, right], axis=0).astype(BF16)
    for i in range(8):
        out_ref[i] = block


def in_hbm(values):
    return pltpu.with_memory_space_constraint(values, pltpu.HBM)


def pack(expert, tokens, ids, weights):
    return pl.pallas_call(
        pack_kernel,
        out_shape=jax.ShapeDtypeStruct((8, 8, WIDE), BF16),
        in_specs=[SMEM, HBM, HBM, HBM],
        out_specs=VMEM,
        scratch_shapes=[
            pltpu.VMEM((4, D), BF16),
            pltpu.VMEM((4, 8), jnp.int32),
            pltpu.VMEM((4, 8), F32),
            pltpu.SemaphoreType.DMA((3,)),
        ],
        compiler_params=pltpu.CompilerParams(vmem_limit_bytes=4 * MIB),
        name="pack",
    )(expert, in_hbm(tokens), in_hbm(ids), in_hbm(weights))


def expert_lanes(expert, shape, dim):
    lane = lax.broadcasted_iota(jnp.int32, shape, dim)
    return (lane < 64) & (lane % 32 == expert)


def select_kernel(starts, loads, expert_ref, *refs):
    refs = list(refs)
    blocks = [refs.pop(0) for _ in range(4)]
    sources = [refs.pop(0) for _ in range(loads)]
    del refs[0]
    mine_ref, sent_refs, targets = refs[0], refs[1 : 1 + len(starts)], refs[1 + len(starts) : -2]
    pick, sem = refs[-2:]
    copies = [pltpu.make_async_copy(a, b, sem) for a, b in zip(sources, targets)]
    for copy in copies:
        copy.start()
    own = expert_ref[0]
    turn = lax.broadcasted_iota(jnp.int32, (8, EXT), 0)
    experts = jnp.where(turn == 0, own, own ^ 1)
    wanted = jnp.where(expert_lanes(experts, (8, EXT), 1) & (turn < 2), 1.0, 0.0).astype(BF16)
    ext = jnp.concatenate([ref[:, HALF:] for ref in blocks], axis=0)
    route = lax.dot_general(wanted, ext, (((1,), (1,)), ((), ())), preferred_element_type=F32)
    chosen = route > 0
    first = lax.broadcasted_iota(jnp.int32, (PART, PART), 0)
    second = lax.broadcasted_iota(jnp.int32, (PART, PART), 1)
    earlier = jnp.where((first // 4 == second // 4) & (first < second), 1.0, 0.0).astype(BF16)
    rank = jnp.dot(jnp.where(chosen, 1.0, 0.0).astype(BF16), earlier, preferred_element_type=F32)
    column = lax.broadcasted_iota(jnp.int32, (8, PART), 1)
    place = jnp.where(chosen, column // 8 * 2 + rank.astype(jnp.int32), -1)
    row = lax.broadcasted_iota(jnp.int32, (SEL, PART), 0)
    is_left = lax.broadcasted_iota(jnp.int32, (SEL, PART), 1) % 8 < 4
    for e in range(2):
        hit = place[e : e + 1, :] == row
        pick[e * SEL : (e + 1) * SEL, :] = jnp.where(hit & is_left, 1.0, 0.0).astype(BF16)
        pick[(2 + e) * SEL : (3 + e) * SEL, :] = jnp.where(hit & ~is_left, 1.0, 0.0).astype(BF16)

    def put_sent(column, value):
        done = 0
        while done < value.shape[1]:
            piece = max(i for i, start in enumerate(starts) if start <= column + done)
            at = column + done - starts[piece]
            size = min(value.shape[1] - done, sent_refs[piece].shape[1] - at)
            sent_refs[piece][:, at : at + size] = value[:, done : done + size]
            done += size

    for n in range(0, HALF, 512):
        x = jnp.concatenate([ref[:, n : n + 512] for ref in blocks], axis=0)
        value = jnp.dot(pick[...], x, preferred_element_type=F32).astype(BF16)
        mine_ref[:, n : n + 512] = value[:SEL]
        put_sent(n, value[SEL : 2 * SEL])
        mine_ref[:, HALF + n : HALF + n + 512] = value[2 * SEL : 3 * SEL]
        put_sent(HALF + n, value[3 * SEL :])
    value = jnp.dot(pick[: 2 * SEL, :], ext, preferred_element_type=F32).astype(BF16)
    mine_ref[:, D:] = value[:SEL]
    put_sent(D, value[SEL:])
    for copy in copies:
        copy.wait()


def select(expert, blocks, after, starts, loads=()):
    widths = [end - start for start, end in zip(starts, starts[1:] + (D + EXT,))]
    return pl.pallas_call(
        functools.partial(select_kernel, starts, len(loads)),
        out_shape=[jax.ShapeDtypeStruct((SEL, width), BF16) for width in [D + EXT] + widths]
        + [jax.ShapeDtypeStruct(load.shape, load.dtype) for load in loads],
        in_specs=[SMEM] + [VMEM] * 4 + [HBM] * len(loads) + [ANY],
        out_specs=[VMEM] * (1 + len(starts) + len(loads)),
        scratch_shapes=[pltpu.VMEM((PART, PART), BF16), pltpu.SemaphoreType.DMA],
        compiler_params=SMALL,
        cost_estimate=BRIEF,
        name="select",
    )(expert, *blocks, *[in_hbm(load) for load in loads], after)


def hidden_kernel(starts, expert_ref, mine_ref, *refs):
    theirs_refs = refs[: len(starts)]
    gate_ref, up_ref = refs[len(starts) : len(starts) + 2]
    hidden, gate_sum, up_sum = refs[len(starts) + 3 :]

    def rows(low, high):
        piece = max(i for i, start in enumerate(starts) if start <= low)
        columns = slice(low - starts[piece], high - starts[piece])
        if len(starts) > 1:
            theirs = theirs_refs[piece][1 - expert_ref[0] % 2, :, columns]
        else:
            theirs = theirs_refs[piece][:, columns]
        return jnp.concatenate([mine_ref[:, low:high], theirs], axis=0)

    for low, high in STEPS:
        x = rows(low, high)
        gate = jnp.dot(x, gate_ref[0, low:high, :], preferred_element_type=F32)
        up = jnp.dot(x, up_ref[0, low:high, :], preferred_element_type=F32)
        gate_sum[...] = gate if low == 0 else gate_sum[...] + gate
        up_sum[...] = up if low == 0 else up_sum[...] + up
    lanes = expert_lanes(expert_ref[0], (2 * SEL, EXT), 1)
    scale = jnp.sum(jnp.where(lanes, rows(D, D + EXT).astype(F32), 0.0), axis=1, keepdims=True)
    v = gate_sum[...]
    hidden[...] = (v / (1.0 + jnp.exp(-v)) * up_sum[...] * scale).astype(BF16)


def hidden_units(expert, mine, theirs, gate, up, after, starts):
    return pl.pallas_call(
        functools.partial(hidden_kernel, starts),
        out_shape=jax.ShapeDtypeStruct((2 * SEL, 512), BF16),
        in_specs=[SMEM] + [VMEM] * (3 + len(starts)) + [ANY],
        out_specs=VMEM,
        scratch_shapes=[pltpu.VMEM((2 * SEL, 512), F32)] * 2,
        compiler_params=SMALL,
        cost_estimate=BRIEF,
        name="hidden",
    )(expert, mine, *theirs, gate, up, after)


def down_kernel(hidden_ref, down_ref, after_ref, mine_ref, theirs_ref):
    del after_ref
    for n in range(0, D, 1024):
        block = slice(n, n + 1024)
        value = jnp.dot(hidden_ref[...], down_ref[0, :, block], preferred_element_type=F32).astype(BF16)
        mine_ref[:, block] = value[:SEL]
        theirs_ref[:, block] = value[SEL:]


def down_rows(hidden, down, after):
    return pl.pallas_call(
        down_kernel,
        out_shape=[jax.ShapeDtypeStruct((SEL, D), BF16)] * 2,
        in_specs=[VMEM, VMEM, ANY],
        out_specs=[VMEM, VMEM],
        compiler_params=SMALL,
        cost_estimate=BRIEF,
        name="down",
    )(hidden, down, after)


def places_kernel(expert_ref, a_ref, b_ref, c_ref, d_ref, after_ref, out_ref):
    del after_ref
    own = expert_ref[0]
    turn = lax.broadcasted_iota(jnp.int32, (EXT, EXT), 1)
    experts = jnp.where(turn == 0, own, own ^ 1)
    wanted = jnp.where(expert_lanes(experts, (EXT, EXT), 0) & (turn < 2), 1.0, 0.0).astype(BF16)
    ext = jnp.concatenate([ref[:, HALF:] for ref in (a_ref, b_ref, c_ref, d_ref)], axis=0)
    chosen = jnp.dot(ext, wanted, preferred_element_type=F32) > 0
    row = lax.broadcasted_iota(jnp.int32, (PART, PART), 0)
    other = lax.broadcasted_iota(jnp.int32, (PART, PART), 1)
    earlier = jnp.where((row // 4 == other // 4) & (other < row), 1.0, 0.0).astype(BF16)
    rank = jnp.dot(earlier, jnp.where(chosen, 1.0, 0.0).astype(BF16), preferred_element_type=F32)
    token = lax.broadcasted_iota(jnp.int32, (PART, EXT), 0)
    place = jnp.where(chosen, token // 8 * 2 + rank.astype(jnp.int32), -1)
    column = lax.broadcasted_iota(jnp.int32, (PART, 4 * SEL), 1)
    hit = jnp.where(column // SEL % 2 == 0, place[:, 0:1], place[:, 1:2]) == column % SEL
    is_left = row % 8 < 4
    out_ref[...] = jnp.where(hit & (is_left == (column < 2 * SEL)), 1.0, 0.0).astype(BF16)


def places(expert, blocks, after):
    return pl.pallas_call(
        places_kernel,
        out_shape=jax.ShapeDtypeStruct((PART, 4 * SEL), BF16),
        in_specs=[SMEM] + [VMEM] * 4 + [ANY],
        out_specs=VMEM,
        compiler_params=SMALL,
        cost_estimate=BRIEF,
        name="places",
    )(expert, *blocks, after)


def spread_kernel(place_ref, mine_ref, theirs_ref, after_ref, *outs):
    del after_ref
    for n in range(0, HALF, 512):
        left, right = slice(n, n + 512), slice(HALF + n, HALF + n + 512)
        y = jnp.concatenate([mine_ref[:, left], theirs_ref[:, left], mine_ref[:, right], theirs_ref[:, right]], axis=0)
        value = jnp.dot(place_ref[...], y, preferred_element_type=F32).astype(BF16)
        for i in range(4):
            outs[i][:, left] = value[i * BLOCK : (i + 1) * BLOCK]


def spread(place, mine, theirs, after):
    return pl.pallas_call(
        spread_kernel,
        out_shape=[jax.ShapeDtypeStruct((BLOCK, HALF), BF16)] * 4,
        in_specs=[VMEM] * 3 + [ANY],
        out_specs=[VMEM] * 4,
        compiler_params=SMALL,
        cost_estimate=BRIEF,
        name="spread",
    )(place, mine, theirs, after)


def add(*terms):
    total = terms[0].astype(F32)
    for term in terms[1:]:
        total += term.astype(F32)
    return total.astype(BF16)


def finish_kernel(parts_ref, out_ref):
    total = parts_ref[0].astype(F32)
    for i in range(1, 8):
        total += parts_ref[i].astype(F32)
    out_ref[:, :HALF] = total[:4].astype(BF16)
    out_ref[:, HALF:] = total[4:].astype(BF16)


def finish(parts):
    return pl.pallas_call(
        finish_kernel,
        out_shape=jax.ShapeDtypeStruct((4, D), BF16),
        in_specs=[VMEM],
        out_specs=VMEM,
        compiler_params=SMALL,
        name="finish",
    )(parts)


def body(tokens, ids, weights, gate, up, down):
    expert = lax.axis_index("dev").astype(jnp.int32).reshape(1)
    own = swap_near(pack(expert, tokens, ids, weights)).reshape(BLOCK, WIDE)
    x, y, z = swap_far(own, 0), swap_far(own, 1), swap_far(own, 2)
    xyz = swap_far(own, 3)
    xy, yz, zx = swap_far(y, 0), swap_far(z, 1), swap_far(x, 2)
    near = (x, y, z, own)
    mine_near, *sent, up = select(expert, near, own, TWO, (up,))
    got_near = [both_cores(piece) for piece in sent]
    xy, yz, zx, xyz, *got_near = lax.optimization_barrier((xy, yz, zx, xyz, *got_near))
    far = (xy, zx, yz, xyz)
    mine_far, sent = select(expert, far, own, ONE)
    got_far = [to_sibling(sent)]
    hidden_near = hidden_units(expert, mine_near, got_near, gate, up, mine_far, TWO)
    hidden_far = hidden_units(expert, mine_far, got_far, gate, up, hidden_near, ONE)
    result, theirs = down_rows(hidden_far, down, own)
    returned = to_sibling(theirs)
    result_near, theirs = down_rows(hidden_near, down, result)
    returned_near = to_sibling(theirs)
    place_far = places(expert, far, result_near)
    y_xy, y_zx, y_yz, y_xyz = spread(place_far, result, returned, result_near)
    at_x, at_y, at_z = swap_far(y_xy, 1), swap_far(y_yz, 2), swap_far(y_zx, 0)
    at_own = swap_far(y_xyz, 3)
    y_x, y_y, y_z, y_own = spread(places(expert, near, y_xyz), result_near, returned_near, y_xyz)
    total = add(
        y_own,
        swap_far(add(y_x, at_x), 0),
        swap_far(add(y_y, at_y), 1),
        swap_far(add(y_z, at_z), 2),
        at_own,
    )
    return finish(swap_near(total.reshape(8, 8, HALF)))


def solution(mesh):
    in_specs = (
        P(AXES, None),
        P(AXES, None),
        P(AXES, None),
        P("dev", None, "grp"),
        P("dev", None, "grp"),
        P("dev", "grp", None),
    )
    return jax.shard_map(body, mesh=mesh, in_specs=in_specs, out_specs=P(AXES, None), check_vma=False)
```

```python
import functools

import jax
import jax.numpy as jnp
from jax import lax
from jax.experimental import pallas as pl
from jax.experimental.pallas import tpu as pltpu
from jax.sharding import PartitionSpec as P

AXES = ("grp", "dev")
D = 7168
HALF = D // 2
EXT = 128
WIDE = HALF + EXT
BLOCK = 64
PART = 4 * BLOCK
SEL = 64
F32 = jnp.float32
BF16 = jnp.bfloat16
MIB = 1 << 20
VMEM = pl.BlockSpec(memory_space=pltpu.VMEM)
SMEM = pl.BlockSpec(memory_space=pltpu.SMEM)
HBM = pl.BlockSpec(memory_space=pltpu.HBM)
ANY = pl.BlockSpec(memory_space=pl.ANY)
SMALL = pltpu.CompilerParams(vmem_limit_bytes=8 * MIB)


STEPS = ((0, HALF), (HALF, D))
TWO = (0, HALF)
ONE = (0,)
BRIEF = pl.CostEstimate(flops=1000, bytes_accessed=1000, transcendentals=0)


def flat(z, x, y, c):
    return ((z * 4 + x) * 4 + y) * 2 + c


def near_groups():
    seen, groups = set(), []
    for z in range(4):
        for x in range(4):
            for y in range(4):
                for c in range(2):
                    if flat(z, x, y, c) in seen:
                        continue
                    m = 3 if c else 1
                    members = [
                        flat(z ^ (m * i), x ^ (m * j), y ^ (m * k), c)
                        for i in (0, 1) for j in (0, 1) for k in (0, 1)
                    ]
                    seen.update(members)
                    groups.append(members)
    return groups


def far_pairs(*axes):
    pairs = []
    for z in range(4):
        for x in range(4):
            for y in range(4):
                for c in range(2):
                    at = [x, z, y]
                    for axis in axes:
                        at[axis] ^= 1 if c else 3
                    pairs.append((flat(z, x, y, c), flat(at[1], at[0], at[2], c)))
    return pairs


NEAR = near_groups()
FAR = [far_pairs(0), far_pairs(1), far_pairs(2), far_pairs(0, 1, 2)]


def swap_near(values):
    return lax.all_to_all(values, AXES, 0, 0, axis_index_groups=NEAR, tiled=True)


def swap_far(values, axis):
    return lax.ppermute(values, AXES, FAR[axis])


def both_cores(values):
    return lax.all_gather(values, "dev", axis_index_groups=[[i, i + 1] for i in range(0, 32, 2)])


def to_sibling(values):
    return lax.ppermute(values, "dev", [(i, i ^ 1) for i in range(32)])


def pack_kernel(expert_ref, tokens_hbm, ids_hbm, weights_hbm, out_ref, tokens_ref, ids_ref, weights_ref, sems):
    del expert_ref
    pairs = ((tokens_hbm, tokens_ref), (ids_hbm, ids_ref), (weights_hbm, weights_ref))
    copies = [pltpu.make_async_copy(source, target, sems.at[i]) for i, (source, target) in enumerate(pairs)]
    for copy in copies:
        copy.start()
    for copy in copies:
        copy.wait()
    lane = lax.broadcasted_iota(jnp.int32, (4, EXT), 1)
    dense = jnp.zeros((4, EXT), F32)
    for k in range(8):
        dense += jnp.where(ids_ref[:, k : k + 1] == lane % 32, weights_ref[:, k : k + 1], 0.0)
    high = dense.astype(BF16).astype(F32)
    route = jnp.where(lane < 32, high, jnp.where(lane < 64, dense - high, 0.0))
    rows = tokens_ref[...].astype(F32)
    left = jnp.concatenate([rows[:, :HALF], route], axis=1)
    right = jnp.concatenate([rows[:, HALF:], route], axis=1)
    block = jnp.concatenate([left, right], axis=0).astype(BF16)
    for i in range(8):
        out_ref[i] = block


def in_hbm(values):
    return pltpu.with_memory_space_constraint(values, pltpu.HBM)


def pack(expert, tokens, ids, weights):
    return pl.pallas_call(
        pack_kernel,
        out_shape=jax.ShapeDtypeStruct((8, 8, WIDE), BF16),
        in_specs=[SMEM, HBM, HBM, HBM],
        out_specs=VMEM,
        scratch_shapes=[
            pltpu.VMEM((4, D), BF16),
            pltpu.VMEM((4, 8), jnp.int32),
            pltpu.VMEM((4, 8), F32),
            pltpu.SemaphoreType.DMA((3,)),
        ],
        compiler_params=pltpu.CompilerParams(vmem_limit_bytes=4 * MIB),
        name="pack",
    )(expert, in_hbm(tokens), in_hbm(ids), in_hbm(weights))


def expert_lanes(expert, shape, dim):
    lane = lax.broadcasted_iota(jnp.int32, shape, dim)
    return (lane < 64) & (lane % 32 == expert)


def select_kernel(starts, loads, expert_ref, *refs):
    refs = list(refs)
    blocks = [refs.pop(0) for _ in range(4)]
    sources = [refs.pop(0) for _ in range(loads)]
    del refs[0]
    mine_ref, sent_refs, targets = refs[0], refs[1 : 1 + len(starts)], refs[1 + len(starts) : -2]
    pick, sem = refs[-2:]
    copies = [pltpu.make_async_copy(a, b, sem) for a, b in zip(sources, targets)]
    for copy in copies:
        copy.start()
    own = expert_ref[0]
    turn = lax.broadcasted_iota(jnp.int32, (8, EXT), 0)
    experts = jnp.where(turn == 0, own, own ^ 1)
    wanted = jnp.where(expert_lanes(experts, (8, EXT), 1) & (turn < 2), 1.0, 0.0).astype(BF16)
    ext = jnp.concatenate([ref[:, HALF:] for ref in blocks], axis=0)
    route = lax.dot_general(wanted, ext, (((1,), (1,)), ((), ())), preferred_element_type=F32)
    chosen = route > 0
    first = lax.broadcasted_iota(jnp.int32, (PART, PART), 0)
    second = lax.broadcasted_iota(jnp.int32, (PART, PART), 1)
    earlier = jnp.where((first // 4 == second // 4) & (first < second), 1.0, 0.0).astype(BF16)
    rank = jnp.dot(jnp.where(chosen, 1.0, 0.0).astype(BF16), earlier, preferred_element_type=F32)
    column = lax.broadcasted_iota(jnp.int32, (8, PART), 1)
    place = jnp.where(chosen, column // 8 * 2 + rank.astype(jnp.int32), -1)
    row = lax.broadcasted_iota(jnp.int32, (SEL, PART), 0)
    is_left = lax.broadcasted_iota(jnp.int32, (SEL, PART), 1) % 8 < 4
    for e in range(2):
        hit = place[e : e + 1, :] == row
        pick[e * SEL : (e + 1) * SEL, :] = jnp.where(hit & is_left, 1.0, 0.0).astype(BF16)
        pick[(2 + e) * SEL : (3 + e) * SEL, :] = jnp.where(hit & ~is_left, 1.0, 0.0).astype(BF16)

    def put_sent(column, value):
        done = 0
        while done < value.shape[1]:
            piece = max(i for i, start in enumerate(starts) if start <= column + done)
            at = column + done - starts[piece]
            size = min(value.shape[1] - done, sent_refs[piece].shape[1] - at)
            sent_refs[piece][:, at : at + size] = value[:, done : done + size]
            done += size

    for n in range(0, HALF, 512):
        x = jnp.concatenate([ref[:, n : n + 512] for ref in blocks], axis=0)
        value = jnp.dot(pick[...], x, preferred_element_type=F32).astype(BF16)
        mine_ref[:, n : n + 512] = value[:SEL]
        put_sent(n, value[SEL : 2 * SEL])
        mine_ref[:, HALF + n : HALF + n + 512] = value[2 * SEL : 3 * SEL]
        put_sent(HALF + n, value[3 * SEL :])
    value = jnp.dot(pick[: 2 * SEL, :], ext, preferred_element_type=F32).astype(BF16)
    mine_ref[:, D:] = value[:SEL]
    put_sent(D, value[SEL:])
    for copy in copies:
        copy.wait()


def select(expert, blocks, after, starts, loads=()):
    widths = [end - start for start, end in zip(starts, starts[1:] + (D + EXT,))]
    return pl.pallas_call(
        functools.partial(select_kernel, starts, len(loads)),
        out_shape=[jax.ShapeDtypeStruct((SEL, width), BF16) for width in [D + EXT] + widths]
        + [jax.ShapeDtypeStruct(load.shape, load.dtype) for load in loads],
        in_specs=[SMEM] + [VMEM] * 4 + [HBM] * len(loads) + [ANY],
        out_specs=[VMEM] * (1 + len(starts) + len(loads)),
        scratch_shapes=[pltpu.VMEM((PART, PART), BF16), pltpu.SemaphoreType.DMA],
        compiler_params=SMALL,
        cost_estimate=BRIEF,
        name="select",
    )(expert, *blocks, *[in_hbm(load) for load in loads], after)


def hidden_kernel(starts, expert_ref, mine_ref, *refs):
    theirs_refs = refs[: len(starts)]
    gate_ref, up_ref = refs[len(starts) : len(starts) + 2]
    hidden, gate_sum, up_sum = refs[len(starts) + 3 :]

    def rows(low, high):
        piece = max(i for i, start in enumerate(starts) if start <= low)
        columns = slice(low - starts[piece], high - starts[piece])
        if len(starts) > 1:
            theirs = theirs_refs[piece][1 - expert_ref[0] % 2, :, columns]
        else:
            theirs = theirs_refs[piece][:, columns]
        return jnp.concatenate([mine_ref[:, low:high], theirs], axis=0)

    for low, high in STEPS:
        x = rows(low, high)
        gate = jnp.dot(x, gate_ref[0, low:high, :], preferred_element_type=F32)
        up = jnp.dot(x, up_ref[0, low:high, :], preferred_element_type=F32)
        gate_sum[...] = gate if low == 0 else gate_sum[...] + gate
        up_sum[...] = up if low == 0 else up_sum[...] + up
    lanes = expert_lanes(expert_ref[0], (2 * SEL, EXT), 1)
    scale = jnp.sum(jnp.where(lanes, rows(D, D + EXT).astype(F32), 0.0), axis=1, keepdims=True)
    v = gate_sum[...]
    hidden[...] = (v / (1.0 + jnp.exp(-v)) * up_sum[...] * scale).astype(BF16)


def hidden_units(expert, mine, theirs, gate, up, after, starts):
    return pl.pallas_call(
        functools.partial(hidden_kernel, starts),
        out_shape=jax.ShapeDtypeStruct((2 * SEL, 512), BF16),
        in_specs=[SMEM] + [VMEM] * (3 + len(starts)) + [ANY],
        out_specs=VMEM,
        scratch_shapes=[pltpu.VMEM((2 * SEL, 512), F32)] * 2,
        compiler_params=SMALL,
        cost_estimate=BRIEF,
        name="hidden",
    )(expert, mine, *theirs, gate, up, after)


def down_kernel(hidden_ref, down_ref, after_ref, mine_ref, theirs_ref):
    del after_ref
    for n in range(0, D, 1024):
        block = slice(n, n + 1024)
        value = jnp.dot(hidden_ref[...], down_ref[0, :, block], preferred_element_type=F32).astype(BF16)
        mine_ref[:, block] = value[:SEL]
        theirs_ref[:, block] = value[SEL:]


def down_rows(hidden, down, after):
    return pl.pallas_call(
        down_kernel,
        out_shape=[jax.ShapeDtypeStruct((SEL, D), BF16)] * 2,
        in_specs=[VMEM, VMEM, ANY],
        out_specs=[VMEM, VMEM],
        compiler_params=SMALL,
        cost_estimate=BRIEF,
        name="down",
    )(hidden, down, after)


def places_kernel(expert_ref, a_ref, b_ref, c_ref, d_ref, after_ref, out_ref):
    del after_ref
    own = expert_ref[0]
    turn = lax.broadcasted_iota(jnp.int32, (EXT, EXT), 1)
    experts = jnp.where(turn == 0, own, own ^ 1)
    wanted = jnp.where(expert_lanes(experts, (EXT, EXT), 0) & (turn < 2), 1.0, 0.0).astype(BF16)
    ext = jnp.concatenate([ref[:, HALF:] for ref in (a_ref, b_ref, c_ref, d_ref)], axis=0)
    chosen = jnp.dot(ext, wanted, preferred_element_type=F32) > 0
    row = lax.broadcasted_iota(jnp.int32, (PART, PART), 0)
    other = lax.broadcasted_iota(jnp.int32, (PART, PART), 1)
    earlier = jnp.where((row // 4 == other // 4) & (other < row), 1.0, 0.0).astype(BF16)
    rank = jnp.dot(earlier, jnp.where(chosen, 1.0, 0.0).astype(BF16), preferred_element_type=F32)
    token = lax.broadcasted_iota(jnp.int32, (PART, EXT), 0)
    place = jnp.where(chosen, token // 8 * 2 + rank.astype(jnp.int32), -1)
    column = lax.broadcasted_iota(jnp.int32, (PART, 4 * SEL), 1)
    hit = jnp.where(column // SEL % 2 == 0, place[:, 0:1], place[:, 1:2]) == column % SEL
    is_left = row % 8 < 4
    out_ref[...] = jnp.where(hit & (is_left == (column < 2 * SEL)), 1.0, 0.0).astype(BF16)


def places(expert, blocks, after):
    return pl.pallas_call(
        places_kernel,
        out_shape=jax.ShapeDtypeStruct((PART, 4 * SEL), BF16),
        in_specs=[SMEM] + [VMEM] * 4 + [ANY],
        out_specs=VMEM,
        compiler_params=SMALL,
        cost_estimate=BRIEF,
        name="places",
    )(expert, *blocks, after)


def spread_kernel(place_ref, mine_ref, theirs_ref, after_ref, *outs):
    del after_ref
    for n in range(0, HALF, 512):
        left, right = slice(n, n + 512), slice(HALF + n, HALF + n + 512)
        y = jnp.concatenate([mine_ref[:, left], theirs_ref[:, left], mine_ref[:, right], theirs_ref[:, right]], axis=0)
        value = jnp.dot(place_ref[...], y, preferred_element_type=F32).astype(BF16)
        for i in range(4):
            outs[i][:, left] = value[i * BLOCK : (i + 1) * BLOCK]


def spread(place, mine, theirs, after):
    return pl.pallas_call(
        spread_kernel,
        out_shape=[jax.ShapeDtypeStruct((BLOCK, HALF), BF16)] * 4,
        in_specs=[VMEM] * 3 + [ANY],
        out_specs=[VMEM] * 4,
        compiler_params=SMALL,
        cost_estimate=BRIEF,
        name="spread",
    )(place, mine, theirs, after)


def add(*terms):
    total = terms[0].astype(F32)
    for term in terms[1:]:
        total += term.astype(F32)
    return total.astype(BF16)


def finish_kernel(parts_ref, out_ref):
    total = parts_ref[0].astype(F32)
    for i in range(1, 8):
        total += parts_ref[i].astype(F32)
    out_ref[:, :HALF] = total[:4].astype(BF16)
    out_ref[:, HALF:] = total[4:].astype(BF16)


def finish(parts):
    return pl.pallas_call(
        finish_kernel,
        out_shape=jax.ShapeDtypeStruct((4, D), BF16),
        in_specs=[VMEM],
        out_specs=VMEM,
        compiler_params=SMALL,
        name="finish",
    )(parts)


def body(tokens, ids, weights, gate, up, down):
    expert = lax.axis_index("dev").astype(jnp.int32).reshape(1)
    own = swap_near(pack(expert, tokens, ids, weights)).reshape(BLOCK, WIDE)
    x, y, z = swap_far(own, 0), swap_far(own, 1), swap_far(own, 2)
    xyz = swap_far(own, 3)
    xy, yz, zx = swap_far(x, 1), swap_far(y, 2), swap_far(z, 0)
    near = (x, y, z, own)
    mine_near, *sent, up = select(expert, near, own, TWO, (up,))
    got_near = [both_cores(piece) for piece in sent]
    place_near = places(expert, near, got_near[0])
    xy, yz, zx, xyz, place_near, *got_near = lax.optimization_barrier((xy, yz, zx, xyz, place_near, *got_near))
    far = (xy, zx, yz, xyz)
    mine_far, sent = select(expert, far, own, ONE)
    got_far = [to_sibling(sent)]
    hidden_near = hidden_units(expert, mine_near, got_near, gate, up, mine_far, TWO)
    hidden_far = hidden_units(expert, mine_far, got_far, gate, up, hidden_near, ONE)
    result, theirs = down_rows(hidden_far, down, own)
    returned = to_sibling(theirs)
    result_near, theirs = down_rows(hidden_near, down, result)
    returned_near = to_sibling(theirs)
    place_far = places(expert, far, result_near)
    y_xy, y_zx, y_yz, y_xyz = spread(place_far, result, returned, result_near)
    at_x, at_y, at_z = swap_far(y_xy, 1), swap_far(y_yz, 2), swap_far(y_zx, 0)
    at_own = swap_far(y_xyz, 3)
    y_x, y_y, y_z, y_own = spread(place_near, result_near, returned_near, y_xyz)
    total = add(
        y_own,
        swap_far(add(y_x, at_x), 0),
        swap_far(add(y_y, at_y), 1),
        swap_far(add(y_z, at_z), 2),
        at_own,
    )
    return finish(swap_near(total.reshape(8, 8, HALF)))


def solution(mesh):
    in_specs = (
        P(AXES, None),
        P(AXES, None),
        P(AXES, None),
        P("dev", None, "grp"),
        P("dev", None, "grp"),
        P("dev", "grp", None),
    )
    return jax.shard_map(body, mesh=mesh, in_specs=in_specs, out_specs=P(AXES, None), check_vma=False)
```

```python
import functools

import jax
import jax.numpy as jnp
from jax import lax
from jax.experimental import pallas as pl
from jax.experimental.pallas import tpu as pltpu
from jax.sharding import PartitionSpec as P

AXES = ("grp", "dev")
D = 7168
HALF = D // 2
EXT = 128
WIDE = HALF + EXT
BLOCK = 64
PART = 4 * BLOCK
SEL = 64
F32 = jnp.float32
BF16 = jnp.bfloat16
MIB = 1 << 20
VMEM = pl.BlockSpec(memory_space=pltpu.VMEM)
SMEM = pl.BlockSpec(memory_space=pltpu.SMEM)
HBM = pl.BlockSpec(memory_space=pltpu.HBM)
ANY = pl.BlockSpec(memory_space=pl.ANY)
SMALL = pltpu.CompilerParams(vmem_limit_bytes=8 * MIB)


STEPS = ((0, HALF), (HALF, D))
TWO = (0, HALF)
ONE = (0,)
BRIEF = pl.CostEstimate(flops=1000, bytes_accessed=1000, transcendentals=0)


def flat(z, x, y, c):
    return ((z * 4 + x) * 4 + y) * 2 + c


def near_groups():
    seen, groups = set(), []
    for z in range(4):
        for x in range(4):
            for y in range(4):
                for c in range(2):
                    if flat(z, x, y, c) in seen:
                        continue
                    m = 3 if c else 1
                    members = [
                        flat(z ^ (m * i), x ^ (m * j), y ^ (m * k), c)
                        for i in (0, 1) for j in (0, 1) for k in (0, 1)
                    ]
                    seen.update(members)
                    groups.append(members)
    return groups


def far_pairs(*axes):
    pairs = []
    for z in range(4):
        for x in range(4):
            for y in range(4):
                for c in range(2):
                    at = [x, z, y]
                    for axis in axes:
                        at[axis] ^= 1 if c else 3
                    pairs.append((flat(z, x, y, c), flat(at[1], at[0], at[2], c)))
    return pairs


NEAR = near_groups()
FAR = [far_pairs(0), far_pairs(1), far_pairs(2), far_pairs(0, 1, 2)]


def swap_near(values):
    return lax.all_to_all(values, AXES, 0, 0, axis_index_groups=NEAR, tiled=True)


def swap_far(values, axis):
    return lax.ppermute(values, AXES, FAR[axis])


def both_cores(values):
    return lax.all_gather(values, "dev", axis_index_groups=[[i, i + 1] for i in range(0, 32, 2)])


def to_sibling(values):
    return lax.ppermute(values, "dev", [(i, i ^ 1) for i in range(32)])


def pack_kernel(expert_ref, tokens_hbm, ids_hbm, weights_hbm, out_ref, tokens_ref, ids_ref, weights_ref, sems):
    del expert_ref
    pairs = ((tokens_hbm, tokens_ref), (ids_hbm, ids_ref), (weights_hbm, weights_ref))
    copies = [pltpu.make_async_copy(source, target, sems.at[i]) for i, (source, target) in enumerate(pairs)]
    for copy in copies:
        copy.start()
    for copy in copies:
        copy.wait()
    lane = lax.broadcasted_iota(jnp.int32, (4, EXT), 1)
    dense = jnp.zeros((4, EXT), F32)
    for k in range(8):
        dense += jnp.where(ids_ref[:, k : k + 1] == lane % 32, weights_ref[:, k : k + 1], 0.0)
    high = dense.astype(BF16).astype(F32)
    route = jnp.where(lane < 32, high, jnp.where(lane < 64, dense - high, 0.0))
    rows = tokens_ref[...].astype(F32)
    left = jnp.concatenate([rows[:, :HALF], route], axis=1)
    right = jnp.concatenate([rows[:, HALF:], route], axis=1)
    block = jnp.concatenate([left, right], axis=0).astype(BF16)
    for i in range(8):
        out_ref[i] = block


def in_hbm(values):
    return pltpu.with_memory_space_constraint(values, pltpu.HBM)


def pack(expert, tokens, ids, weights):
    return pl.pallas_call(
        pack_kernel,
        out_shape=jax.ShapeDtypeStruct((8, 8, WIDE), BF16),
        in_specs=[SMEM, HBM, HBM, HBM],
        out_specs=VMEM,
        scratch_shapes=[
            pltpu.VMEM((4, D), BF16),
            pltpu.VMEM((4, 8), jnp.int32),
            pltpu.VMEM((4, 8), F32),
            pltpu.SemaphoreType.DMA((3,)),
        ],
        compiler_params=pltpu.CompilerParams(vmem_limit_bytes=4 * MIB),
        name="pack",
    )(expert, in_hbm(tokens), in_hbm(ids), in_hbm(weights))


def expert_lanes(expert, shape, dim):
    lane = lax.broadcasted_iota(jnp.int32, shape, dim)
    return (lane < 64) & (lane % 32 == expert)


def select_kernel(starts, loads, expert_ref, *refs):
    refs = list(refs)
    blocks = [refs.pop(0) for _ in range(4)]
    sources = [refs.pop(0) for _ in range(loads)]
    del refs[0]
    mine_ref, sent_refs, targets = refs[0], refs[1 : 1 + len(starts)], refs[1 + len(starts) : -2]
    pick, sem = refs[-2:]
    copies = [pltpu.make_async_copy(a, b, sem) for a, b in zip(sources, targets)]
    for copy in copies:
        copy.start()
    own = expert_ref[0]
    turn = lax.broadcasted_iota(jnp.int32, (8, EXT), 0)
    experts = jnp.where(turn == 0, own, own ^ 1)
    wanted = jnp.where(expert_lanes(experts, (8, EXT), 1) & (turn < 2), 1.0, 0.0).astype(BF16)
    ext = jnp.concatenate([ref[:, HALF:] for ref in blocks], axis=0)
    route = lax.dot_general(wanted, ext, (((1,), (1,)), ((), ())), preferred_element_type=F32)
    chosen = route > 0
    first = lax.broadcasted_iota(jnp.int32, (PART, PART), 0)
    second = lax.broadcasted_iota(jnp.int32, (PART, PART), 1)
    earlier = jnp.where((first // 4 == second // 4) & (first < second), 1.0, 0.0).astype(BF16)
    rank = jnp.dot(jnp.where(chosen, 1.0, 0.0).astype(BF16), earlier, preferred_element_type=F32)
    column = lax.broadcasted_iota(jnp.int32, (8, PART), 1)
    place = jnp.where(chosen, column // 8 * 2 + rank.astype(jnp.int32), -1)
    row = lax.broadcasted_iota(jnp.int32, (SEL, PART), 0)
    is_left = lax.broadcasted_iota(jnp.int32, (SEL, PART), 1) % 8 < 4
    for e in range(2):
        hit = place[e : e + 1, :] == row
        pick[e * SEL : (e + 1) * SEL, :] = jnp.where(hit & is_left, 1.0, 0.0).astype(BF16)
        pick[(2 + e) * SEL : (3 + e) * SEL, :] = jnp.where(hit & ~is_left, 1.0, 0.0).astype(BF16)

    def put_sent(column, value):
        done = 0
        while done < value.shape[1]:
            piece = max(i for i, start in enumerate(starts) if start <= column + done)
            at = column + done - starts[piece]
            size = min(value.shape[1] - done, sent_refs[piece].shape[1] - at)
            sent_refs[piece][:, at : at + size] = value[:, done : done + size]
            done += size

    for n in range(0, HALF, 512):
        x = jnp.concatenate([ref[:, n : n + 512] for ref in blocks], axis=0)
        value = jnp.dot(pick[...], x, preferred_element_type=F32).astype(BF16)
        mine_ref[:, n : n + 512] = value[:SEL]
        put_sent(n, value[SEL : 2 * SEL])
        mine_ref[:, HALF + n : HALF + n + 512] = value[2 * SEL : 3 * SEL]
        put_sent(HALF + n, value[3 * SEL :])
    value = jnp.dot(pick[: 2 * SEL, :], ext, preferred_element_type=F32).astype(BF16)
    mine_ref[:, D:] = value[:SEL]
    put_sent(D, value[SEL:])
    for copy in copies:
        copy.wait()


def select(expert, blocks, after, starts, loads=()):
    widths = [end - start for start, end in zip(starts, starts[1:] + (D + EXT,))]
    return pl.pallas_call(
        functools.partial(select_kernel, starts, len(loads)),
        out_shape=[jax.ShapeDtypeStruct((SEL, width), BF16) for width in [D + EXT] + widths]
        + [jax.ShapeDtypeStruct(load.shape, load.dtype) for load in loads],
        in_specs=[SMEM] + [VMEM] * 4 + [HBM] * len(loads) + [ANY],
        out_specs=[VMEM] * (1 + len(starts) + len(loads)),
        scratch_shapes=[pltpu.VMEM((PART, PART), BF16), pltpu.SemaphoreType.DMA],
        compiler_params=SMALL,
        cost_estimate=BRIEF,
        name="select",
    )(expert, *blocks, *[in_hbm(load) for load in loads], after)


def hidden_kernel(starts, expert_ref, mine_ref, *refs):
    theirs_refs = refs[: len(starts)]
    gate_ref, up_ref = refs[len(starts) : len(starts) + 2]
    hidden, gate_sum, up_sum = refs[len(starts) + 3 :]

    def rows(low, high):
        piece = max(i for i, start in enumerate(starts) if start <= low)
        columns = slice(low - starts[piece], high - starts[piece])
        if len(starts) > 1:
            theirs = theirs_refs[piece][1 - expert_ref[0] % 2, :, columns]
        else:
            theirs = theirs_refs[piece][:, columns]
        return jnp.concatenate([mine_ref[:, low:high], theirs], axis=0)

    for low, high in STEPS:
        x = rows(low, high)
        gate = jnp.dot(x, gate_ref[0, low:high, :], preferred_element_type=F32)
        up = jnp.dot(x, up_ref[0, low:high, :], preferred_element_type=F32)
        gate_sum[...] = gate if low == 0 else gate_sum[...] + gate
        up_sum[...] = up if low == 0 else up_sum[...] + up
    lanes = expert_lanes(expert_ref[0], (2 * SEL, EXT), 1)
    scale = jnp.sum(jnp.where(lanes, rows(D, D + EXT).astype(F32), 0.0), axis=1, keepdims=True)
    v = gate_sum[...]
    hidden[...] = (v / (1.0 + jnp.exp(-v)) * up_sum[...] * scale).astype(BF16)


def hidden_units(expert, mine, theirs, gate, up, after, starts):
    return pl.pallas_call(
        functools.partial(hidden_kernel, starts),
        out_shape=jax.ShapeDtypeStruct((2 * SEL, 512), BF16),
        in_specs=[SMEM] + [VMEM] * (3 + len(starts)) + [ANY],
        out_specs=VMEM,
        scratch_shapes=[pltpu.VMEM((2 * SEL, 512), F32)] * 2,
        compiler_params=SMALL,
        cost_estimate=BRIEF,
        name="hidden",
    )(expert, mine, *theirs, gate, up, after)


def down_kernel(hidden_ref, down_ref, after_ref, mine_ref, theirs_ref):
    del after_ref
    for n in range(0, D, 1024):
        block = slice(n, n + 1024)
        value = jnp.dot(hidden_ref[...], down_ref[0, :, block], preferred_element_type=F32).astype(BF16)
        mine_ref[:, block] = value[:SEL]
        theirs_ref[:, block] = value[SEL:]


def down_rows(hidden, down, after):
    return pl.pallas_call(
        down_kernel,
        out_shape=[jax.ShapeDtypeStruct((SEL, D), BF16)] * 2,
        in_specs=[VMEM, VMEM, ANY],
        out_specs=[VMEM, VMEM],
        compiler_params=SMALL,
        cost_estimate=BRIEF,
        name="down",
    )(hidden, down, after)


def places_kernel(expert_ref, a_ref, b_ref, c_ref, d_ref, after_ref, out_ref):
    del after_ref
    own = expert_ref[0]
    turn = lax.broadcasted_iota(jnp.int32, (EXT, EXT), 1)
    experts = jnp.where(turn == 0, own, own ^ 1)
    wanted = jnp.where(expert_lanes(experts, (EXT, EXT), 0) & (turn < 2), 1.0, 0.0).astype(BF16)
    ext = jnp.concatenate([ref[:, HALF:] for ref in (a_ref, b_ref, c_ref, d_ref)], axis=0)
    chosen = jnp.dot(ext, wanted, preferred_element_type=F32) > 0
    row = lax.broadcasted_iota(jnp.int32, (PART, PART), 0)
    other = lax.broadcasted_iota(jnp.int32, (PART, PART), 1)
    earlier = jnp.where((row // 4 == other // 4) & (other < row), 1.0, 0.0).astype(BF16)
    rank = jnp.dot(earlier, jnp.where(chosen, 1.0, 0.0).astype(BF16), preferred_element_type=F32)
    token = lax.broadcasted_iota(jnp.int32, (PART, EXT), 0)
    place = jnp.where(chosen, token // 8 * 2 + rank.astype(jnp.int32), -1)
    column = lax.broadcasted_iota(jnp.int32, (PART, 4 * SEL), 1)
    hit = jnp.where(column // SEL % 2 == 0, place[:, 0:1], place[:, 1:2]) == column % SEL
    is_left = row % 8 < 4
    out_ref[...] = jnp.where(hit & (is_left == (column < 2 * SEL)), 1.0, 0.0).astype(BF16)


def places(expert, blocks, after):
    return pl.pallas_call(
        places_kernel,
        out_shape=jax.ShapeDtypeStruct((PART, 4 * SEL), BF16),
        in_specs=[SMEM] + [VMEM] * 4 + [ANY],
        out_specs=VMEM,
        compiler_params=SMALL,
        cost_estimate=BRIEF,
        name="places",
    )(expert, *blocks, after)


def spread_kernel(place_ref, mine_ref, theirs_ref, after_ref, *outs):
    del after_ref
    for n in range(0, HALF, 512):
        left, right = slice(n, n + 512), slice(HALF + n, HALF + n + 512)
        y = jnp.concatenate([mine_ref[:, left], theirs_ref[:, left], mine_ref[:, right], theirs_ref[:, right]], axis=0)
        value = jnp.dot(place_ref[...], y, preferred_element_type=F32).astype(BF16)
        for i in range(4):
            outs[i][:, left] = value[i * BLOCK : (i + 1) * BLOCK]


def spread(place, mine, theirs, after):
    return pl.pallas_call(
        spread_kernel,
        out_shape=[jax.ShapeDtypeStruct((BLOCK, HALF), BF16)] * 4,
        in_specs=[VMEM] * 3 + [ANY],
        out_specs=[VMEM] * 4,
        compiler_params=SMALL,
        cost_estimate=BRIEF,
        name="spread",
    )(place, mine, theirs, after)


def add(*terms):
    total = terms[0].astype(F32)
    for term in terms[1:]:
        total += term.astype(F32)
    return total.astype(BF16)


def finish_kernel(parts_ref, out_ref):
    total = parts_ref[0].astype(F32)
    for i in range(1, 8):
        total += parts_ref[i].astype(F32)
    out_ref[:, :HALF] = total[:4].astype(BF16)
    out_ref[:, HALF:] = total[4:].astype(BF16)


def finish(parts):
    return pl.pallas_call(
        finish_kernel,
        out_shape=jax.ShapeDtypeStruct((4, D), BF16),
        in_specs=[VMEM],
        out_specs=VMEM,
        compiler_params=SMALL,
        name="finish",
    )(parts)


def body(tokens, ids, weights, gate, up, down):
    expert = lax.axis_index("dev").astype(jnp.int32).reshape(1)
    own = swap_near(pack(expert, tokens, ids, weights)).reshape(BLOCK, WIDE)
    x, y, z = swap_far(own, 0), swap_far(own, 1), swap_far(own, 2)
    xyz = swap_far(own, 3)
    xy, yz, zx = swap_far(y, 0), swap_far(z, 1), swap_far(x, 2)
    near = (x, y, z, own)
    mine_near, *sent, up = select(expert, near, own, TWO, (up,))
    got_near = [both_cores(piece) for piece in sent]
    xy, yz, zx, xyz, *got_near = lax.optimization_barrier((xy, yz, zx, xyz, *got_near))
    far = (xy, zx, yz, xyz)
    mine_far, sent = select(expert, far, own, ONE)
    got_far = [to_sibling(sent)]
    hidden_near = hidden_units(expert, mine_near, got_near, gate, up, mine_far, TWO)
    hidden_far = hidden_units(expert, mine_far, got_far, gate, up, hidden_near, ONE)
    result, theirs = down_rows(hidden_far, down, own)
    returned = to_sibling(theirs)
    result_near, theirs = down_rows(hidden_near, down, result)
    returned_near = to_sibling(theirs)
    place_far = places(expert, far, result_near)
    place_near = places(expert, near, place_far)
    y_xy, y_zx, y_yz, y_xyz = spread(place_far, result, returned, place_near)
    at_x, at_y, at_z = swap_far(y_xy, 1), swap_far(y_yz, 2), swap_far(y_zx, 0)
    at_own = swap_far(y_xyz, 3)
    y_x, y_y, y_z, y_own = spread(place_near, result_near, returned_near, y_xyz)
    total = add(
        y_own,
        swap_far(add(y_x, at_x), 0),
        swap_far(add(y_y, at_y), 1),
        swap_far(add(y_z, at_z), 2),
        at_own,
    )
    return finish(swap_near(total.reshape(8, 8, HALF)))


def solution(mesh):
    in_specs = (
        P(AXES, None),
        P(AXES, None),
        P(AXES, None),
        P("dev", None, "grp"),
        P("dev", None, "grp"),
        P("dev", "grp", None),
    )
    return jax.shard_map(body, mesh=mesh, in_specs=in_specs, out_specs=P(AXES, None), check_vma=False)
```
